128 devices in a mesh: ctx: 16 (over x, z_lo, core), dp: 8 (over y, z_hi).
Axes of the slice: x: 4, y: 4, z: 4 (z_hi: 2, z_lo: 2; z = z_hi * 2 + z_lo), core: 2. Of those that a mesh axis runs over, the one named last changes fastest.
Arguments:
- query: bfloat16 [8, 8192, 1024], P('dp', 'ctx'), may hold values from -30 to 30
- key: bfloat16 [8, 8192, 1024], P('dp', 'ctx'), may hold values from -30 to 30
- value: bfloat16 [8, 8192, 1024], P('dp', 'ctx'), may hold values from -6 to 6
- segment_ids: int32 [8, 8192], P('dp', 'ctx'), may hold values from 0 to 1, never falling along the last dimension, each value on 1 to 7680 neighbouring positions
- out_weight: bfloat16 [1024, 2048], replicated, may hold values from -0.1875 to 0.1875
- cotangent: bfloat16 [8, 8192, 2048], P('dp', 'ctx'), may hold values from -6 to 6
Outputs:
- output: bfloat16 [8, 8192, 2048], P('dp', 'ctx')
- grad_query: bfloat16 [8, 8192, 1024], P('dp', 'ctx')
- grad_key: bfloat16 [8, 8192, 1024], P('dp', 'ctx')
- grad_value: bfloat16 [8, 8192, 1024], P('dp', 'ctx')
- grad_weight: float32 [1024, 2048], P(('ctx', 'dp'))
The draws below stay inside these ranges and needn't reach their ends.
All inputs are finite; a program needn't handle non-finite values.
Results may differ from the reference program's by a relative error of at most 0.023.
Values may be sent and summed in bfloat16 or wider, within the bound.
No kernel may reach another device: no remote copies, remote signals or barrier semaphores. Data moves between devices by JAX's collectives and lax.ppermute only.
A program may use at most 192 MiB of HBM per device.

```python
import math
from functools import partial
import jax
import jax.numpy as jnp
import numpy as np
from jax import lax

D = 2048
HEADS = 8
HEAD_DIM = 128
LEVELS = 3
TOK_DEV = 512
HD = 1024
TOKENS = 8192
SEQS = 8
N_CTX = 16


def draw_query(key, part):
    key = jax.random.fold_in(key, 11)
    shape = (SEQS, TOKENS, HD)
    result = jnp.clip(jax.random.normal(key, shape, jnp.float32), -6.0, 6.0)
    return result.astype(jnp.bfloat16)


def draw_key(key, part):
    key = jax.random.fold_in(key, 23)
    shape = (SEQS, TOKENS, HD)
    result = jnp.clip(jax.random.normal(key, shape, jnp.float32), -6.0, 6.0)
    return result.astype(jnp.bfloat16)


def steps_of(key, extent, split, smallest, largest):
    loudness = 1.0
    for position, blocks in split:
        draws = jax.random.uniform(jax.random.fold_in(jax.random.fold_in(key, 6), position), (blocks,), jnp.float32, smallest / len(split), largest / len(split))
        loudness = loudness * jnp.repeat(jnp.exp(draws), extent[position] // blocks).reshape((-1,) + (1,) * (len(extent) - 1 - position))
    return loudness


def split_up(number_of, total, reach, slope):
    weights = [(1 << 20) // math.isqrt(grade ** slope) + 1 for grade in range(2, number_of + 1)]
    rest, given = total - reach - (number_of - 1), [1] * (number_of - 1)
    while rest > 0:
        free = [i for i in range(number_of - 1) if given[i] < reach]
        mass, left = sum([weights[i] for i in free]), rest
        for i in free:
            addition = min(reach - given[i], max(1, left * weights[i] // mass), rest)
            given[i] = given[i] + addition
            rest = rest - addition
    return np.array([reach] + given)


def ragged_sizes(stream_key, count, total, bound, skew):
    if count == 2:
        one = jax.random.randint(stream_key, (), max(1, total - bound), min(bound, total - 1) + 1)
        return jnp.stack([one, total - one])
    sizes = jnp.asarray(split_up(count, total, bound, skew), jnp.int32)
    twos = (count - 1) // 2
    giver, taker = sizes[1:1 + 2 * twos:2], sizes[2:2 + 2 * twos:2]
    margin = jnp.minimum(giver - 1, bound - taker)
    moved = jax.random.randint(jax.random.fold_in(stream_key, 1), (twos,), 0, 1 << 20) % (margin + 1)
    sizes = sizes.at[1:1 + 2 * twos:2].set(giver - moved).at[2:2 + 2 * twos:2].set(taker + moved)
    return sizes[jax.random.permutation(jax.random.fold_in(stream_key, 2), count)]


def noise(rng, dims, scale, limit, shards=(), held_as=jnp.bfloat16):
    entries = scale * jax.random.normal(rng, dims, jnp.float32)
    if shards:
        entries = entries * steps_of(rng, dims, shards, -0.22, 0.18)
    return jnp.clip(entries, -limit, limit).astype(held_as)


def setup_inputs(seed: int = 0) -> dict:
    splits = jax.random.split(jax.random.key(seed), 7)
    return {
        "query": draw_query(jax.random.fold_in(splits[6], 71), 0),
        "key": draw_key(jax.random.fold_in(splits[6], 71), 0),
        "value": noise(splits[2], (SEQS, TOKENS, HD), 1.0, 6.0, ((0, 8), (1, 16))),
        "segment_ids": jax.vmap(lambda own: jnp.searchsorted(jnp.cumsum(ragged_sizes(own, 2, TOKENS, TOKENS - TOK_DEV, 0)), jnp.arange(TOKENS), side="right"))(jax.random.split(splits[3], SEQS)).reshape((SEQS, TOKENS)).astype(jnp.int32),
        "out_weight": noise(splits[4], (HD, D), HD ** -0.5, 0.1875),
        "cotangent": noise(splits[5], (SEQS, TOKENS, D), 1.0, 6.0, ((0, 8), (1, 16))),
    }


def level_heights(blocks):
    summit = int(blocks).bit_length() - 1
    return list(range(summit - LEVELS, summit))

def pool_rows(values32, factor):
    shape = values32.shape
    grouped = values32.reshape(shape[:-2] + (shape[-2] // factor, factor, shape[-1]))
    return lax.optimization_barrier(jnp.mean(grouped, axis=-2)).astype(jnp.bfloat16)

def attend(queries, keys32, values32, segments, coarse, heights=()):
    count = queries.shape[0]
    scale = 1.0 / math.sqrt(HEAD_DIM)
    query_f = queries.astype(jnp.float32).reshape(count, HEADS, HEAD_DIM)
    key_sets = [(keys32, values32, segments, 0.0)]
    for height, triple in zip(heights, coarse):
        key_sets.append((triple[0].astype(jnp.float32), triple[1].astype(jnp.float32), triple[2], math.log(2.0 ** (height + 1))))
    blocks = []
    values_all = []
    for key_f, value_f, key_seg, offset in key_sets:
        width = key_f.shape[0]
        logits = jnp.einsum('qhe,khe->hqk', query_f, key_f.reshape(width, HEADS, HEAD_DIM)) * scale + offset
        allowed = segments[:, None] == key_seg[None, :]
        blocks.append(jnp.where(allowed[None], logits, -1e+30))
        values_all.append(value_f.reshape(width, HEADS, HEAD_DIM))
    scores = jnp.concatenate(blocks, -1)
    top = lax.stop_gradient(lax.optimization_barrier(jnp.max(scores, -1, keepdims=True)))
    expo = jnp.exp(scores - top)
    weights = (expo / lax.optimization_barrier(jnp.sum(expo, -1, keepdims=True))).astype(jnp.bfloat16)
    mixed = jnp.einsum('hqk,khe->qhe', weights.astype(jnp.float32), jnp.concatenate(values_all, 0))
    return mixed.reshape(count, HEADS * HEAD_DIM).astype(jnp.bfloat16)

def group_table(height):
    blocks = np.arange(N_CTX)
    first = (blocks >> height ^ 1) << height
    return jnp.asarray(first[:, None] + np.arange(2 ** height)[None, :], jnp.int32)

def sequence_grads(queries, keys, values, segments, grad_attention):
    nblocks = N_CTX
    rows = TOK_DEV
    heights = level_heights(N_CTX)
    query_b = queries.reshape(nblocks, rows, HD)
    key_b = keys.astype(jnp.float32).reshape(nblocks, rows, HD)
    value_b = values.astype(jnp.float32).reshape(nblocks, rows, HD)
    seg_b = segments.reshape(nblocks, rows)
    coarse_k = []
    coarse_v = []
    coarse_s = []
    for height in heights:
        factor = 2 ** (height + 1)
        table = group_table(height)
        coarse_k.append(pool_rows(key_b, factor)[table].reshape(nblocks, rows // 2, HD))
        coarse_v.append(pool_rows(value_b, factor)[table].reshape(nblocks, rows // 2, HD))
        coarse_s.append(seg_b[:, ::factor][table].reshape(nblocks, rows // 2))

    def local(query_s, key_s, value_s, ckeys, cvals):
        return jax.vmap(partial(attend, heights=heights))(query_s, key_s, value_s, seg_b, tuple(zip(ckeys, cvals, coarse_s)))
    attention, pull = jax.vjp(local, query_b, key_b, value_b, tuple(coarse_k), tuple(coarse_v))
    grad_q, grad_k, grad_v, grad_ck, grad_cv = pull(grad_attention.reshape(nblocks, rows, HD))
    for place, height in enumerate(heights):
        factor = 2 ** (height + 1)
        size = 2 ** height
        table = group_table(height)
        term_k = grad_ck[place].astype(jnp.float32).reshape(nblocks, size, rows // factor, HD)
        term_v = grad_cv[place].astype(jnp.float32).reshape(nblocks, size, rows // factor, HD)
        total_k = jnp.zeros((nblocks, rows // factor, HD), jnp.float32).at[table].add(term_k)
        total_v = jnp.zeros((nblocks, rows // factor, HD), jnp.float32).at[table].add(term_v)
        grad_k = grad_k + jnp.repeat(total_k / factor, factor, axis=1)
        grad_v = grad_v + jnp.repeat(total_v / factor, factor, axis=1)
    return (attention.reshape(TOKENS, HD), grad_q.reshape(TOKENS, HD), grad_k.reshape(TOKENS, HD).astype(jnp.bfloat16), grad_v.reshape(TOKENS, HD).astype(jnp.bfloat16))

def reference(query, key, value, segment_ids, out_weight, cotangent):
    outputs = []
    grads_q = []
    grads_k = []
    grads_v = []
    grad_weight = jnp.zeros((HD, D), jnp.float32)
    for seq_index in range(SEQS):
        grad_attention = jnp.einsum('td,hd->th', cotangent[seq_index], out_weight, preferred_element_type=jnp.float32).astype(jnp.bfloat16)
        attention, grad_query, grad_key, grad_value = sequence_grads(query[seq_index], key[seq_index], value[seq_index], segment_ids[seq_index], grad_attention)
        outputs.append(jnp.dot(attention, out_weight, preferred_element_type=jnp.float32).astype(jnp.bfloat16))
        grads_q.append(grad_query)
        grads_k.append(grad_key)
        grads_v.append(grad_value)
        grad_weight = grad_weight + lax.dot_general(attention, cotangent[seq_index], (((0,), (0,)), ((), ())), preferred_element_type=jnp.float32)
    return (jnp.stack(outputs), jnp.stack(grads_q), jnp.stack(grads_k), jnp.stack(grads_v), grad_weight)
```

```python
from functools import partial
import math

import jax
import jax.numpy as jnp
import numpy as np
from jax import lax
from jax.experimental import pallas as pl
from jax.experimental.pallas import tpu as pltpu
from jax.sharding import PartitionSpec as P

HEADS = 8
HEAD_DIM = 128
HD = 1024
D = 2048
ROWS = 512
GROUPS = 2
PER = HEADS // GROUPS
COLS = PER * HEAD_DIM
FACTORS = (4, 8, 16)
COARSE = tuple(ROWS // factor for factor in FACTORS)
SCALE = 1.0 / math.sqrt(HEAD_DIM)
BIG = float(2**30)
F32 = jnp.float32
BF16 = jnp.bfloat16
VMEM_LIMIT = 48 * 1024 * 1024


def params(**kwargs):
    return pltpu.CompilerParams(vmem_limit_bytes=VMEM_LIMIT, **kwargs)


def swap(array, axis, bits):
    return lax.ppermute(array, axis, [(i, i ^ bits) for i in range(lax.axis_size(axis))])


def shift(array, axis, step):
    size = lax.axis_size(axis)
    return lax.ppermute(array, axis, [(i, (i + step) % size) for i in range(size)])


def dot_nt(a, b):
    return lax.dot_general(a, b, (((1,), (1,)), ((), ())), preferred_element_type=F32)


def dot_nn(a, b):
    return lax.dot_general(a, b, (((1,), (0,)), ((), ())), preferred_element_type=F32)


def dot_tn(a, b):
    return lax.dot_general(a, b, (((0,), (0,)), ((), ())), preferred_element_type=F32)


def iota(shape, dim):
    return lax.broadcasted_iota(jnp.int32, shape, dim)


def offset_parts(factor):
    rest = math.log(factor) / SCALE
    parts = []
    for _ in range(3):
        part = float(np.asarray(rest, dtype=jnp.bfloat16))
        parts.append(part)
        rest = rest - part
    return parts


def pool_matrices():
    pools, picks = [], []
    for factor, count in zip(FACTORS, COARSE):
        row, col = iota((count, ROWS), 0), iota((count, ROWS), 1)
        inside = (col >= row * factor) & (col < row * factor + factor)
        pools.append(jnp.where(inside, 1.0 / factor, 0.0))
        picks.append(jnp.where(col == row * factor, 1.0, 0.0))
    return jnp.concatenate(pools, 0).astype(BF16), jnp.concatenate(picks, 0).astype(BF16)


def pool_kernel(with_features, *refs):
    if with_features:
        seg_ref, refs = refs[0], refs[1:]
    keys, values = refs[:PER], refs[PER : 2 * PER]
    outs = refs[2 * PER : 2 * PER + 3]
    pool, pick = pool_matrices()
    starts = np.cumsum((0,) + COARSE)

    def put(rows, column):
        for place, out in enumerate(outs):
            out[:, column : column + HEAD_DIM] = rows[starts[place] : starts[place + 1]].astype(BF16)

    for place, ref in enumerate(keys + values):
        put(dot_nn(pool, ref[...]), place * HEAD_DIM)
    if with_features:
        query_feature, key_feature = refs[2 * PER + 3 :]
        seg = seg_ref[...]
        kind = iota((8, ROWS), 0)
        rows = jnp.where(kind < 2, jnp.where(seg == kind, 1.0, 0.0), jnp.where(kind == 2, 1.0, 0.0)).astype(BF16)
        i, j = iota((8, HEAD_DIM), 0), iota((8, HEAD_DIM), 1)
        to_key = jnp.where((i < 2) & (i == j), 1.0, 0.0).astype(BF16)
        wrong = ((i == 0) & (j == 1)) | ((i == 1) & (j == 0))
        ones = (i == 2) & (j >= 2) & (j < 5)
        to_query = jnp.where(wrong, -BIG, jnp.where(ones, 1.0, 0.0)).astype(BF16)
        own = dot_tn(rows, to_key).astype(BF16)
        key_feature[...] = own
        query_feature[...] = dot_tn(rows, to_query).astype(BF16)
        picked = dot_nn(pick, own)
        lane = iota((1, HEAD_DIM), 1)
        for place, (factor, out) in enumerate(zip(FACTORS, outs)):
            parts = offset_parts(factor)
            offset = jnp.where(lane == 2, parts[0], jnp.where(lane == 3, parts[1], jnp.where(lane == 4, parts[2], 0.0)))
            rows_here = picked[starts[place] : starts[place + 1]] + offset
            out[:, 2 * COLS : 2 * COLS + HEAD_DIM] = rows_here.astype(BF16)


def pool(key, value, seg, group):
    with_features = group == 0
    width = 2 * COLS + (HEAD_DIM if with_features else 0)
    heads = [pl.BlockSpec((ROWS, HEAD_DIM), lambda i, h=j * GROUPS + group: (0, h)) for j in range(PER)]
    whole = pl.BlockSpec(memory_space=pltpu.VMEM)
    shapes = [jax.ShapeDtypeStruct((count, width), BF16) for count in COARSE]
    if with_features:
        shapes = shapes + [jax.ShapeDtypeStruct((ROWS, HEAD_DIM), BF16)] * 2
    args = ([seg] if with_features else []) + [key] * PER + [value] * PER
    return pl.pallas_call(
        partial(pool_kernel, with_features),
        grid=(1,),
        out_shape=shapes,
        in_specs=([whole] if with_features else []) + heads + heads,
        out_specs=[whole] * len(shapes),
        compiler_params=params(),
        cost_estimate=pl.CostEstimate(flops=2 * 224 * ROWS * 2 * COLS, bytes_accessed=3 * ROWS * COLS * 2, transcendentals=0),
    )(*args)


CHUNKS = ((0, 256), (256, 256), (512, 128), (640, 128), (768, 128), (896, 128), (1024, 128), (1152, 128))
KEYS = 1280


def attention_kernel(*refs):
    refs = list(refs)
    q_ref, k_ref, v_ref, g_ref, fq_ref, fk_ref = refs[:6]
    ck, cv, cf = refs[6:12], refs[12:18], refs[18:24]
    refs = refs[24:]
    refs = refs[len(refs) - 10 :]
    o_ref, ot_ref, dq_ref, dk_ref, dv_ref, keep_ref, give_ref = refs[:7]
    scores, weights, work = refs[7:]
    q = q_ref[...]
    g = g_ref[...]
    query = jnp.concatenate([q, fq_ref[...]], 1)
    rate = SCALE * math.log2(math.e)

    def part(local, coarse, place):
        start, size = CHUNKS[place]
        return local[pl.ds(start, size), :] if place < 2 else coarse[place - 2][...]

    top = None
    for place, (start, size) in enumerate(CHUNKS):
        key = jnp.concatenate([part(k_ref, ck, place), part(fk_ref, cf, place)], 1)
        here = dot_nt(key, query) * rate
        scores[pl.ds(start, size), :] = here
        peak = jnp.max(here, 0, keepdims=True)
        top = peak if top is None else jnp.maximum(top, peak)
    total = None
    for start, size in CHUNKS:
        here = jnp.exp2(scores[pl.ds(start, size), :] - top)
        scores[pl.ds(start, size), :] = here
        add = jnp.sum(here, 0, keepdims=True)
        total = add if total is None else total + add
    inverse = 1.0 / total
    mixed = None
    for place, (start, size) in enumerate(CHUNKS):
        here = (scores[pl.ds(start, size), :] * inverse).astype(BF16)
        weights[pl.ds(start, size), :] = here
        add = dot_tn(part(v_ref, cv, place), here)
        mixed = add if mixed is None else mixed + add
    ot_ref[...] = mixed.astype(BF16)
    o_ref[...] = mixed.T.astype(BF16)
    delta = jnp.sum(g.astype(F32).T * mixed, 0, keepdims=True)
    grad_q = None
    for place, (start, size) in enumerate(CHUNKS):
        value, key = part(v_ref, cv, place), part(k_ref, ck, place)
        here = weights[pl.ds(start, size), :]
        slope = (here.astype(F32) * (dot_nt(value, g) - delta)).astype(BF16)
        grad_v = dot_nn(here, g)
        grad_k = dot_nn(slope, q) * SCALE
        add = dot_tn(key, slope)
        grad_q = add if grad_q is None else grad_q + add
        if place < 2:
            dk_ref[pl.ds(start, size), :] = grad_k
            dv_ref[pl.ds(start, size), :] = grad_v
        else:
            out, row = (keep_ref, start - 512) if place < 5 else (give_ref, start - 896)
            out[0, pl.ds(row, size), :] = grad_k.astype(BF16)
            out[1, pl.ds(row, size), :] = grad_v.astype(BF16)
    dq_ref[...] = (grad_q * SCALE).T.astype(BF16)


def attention(query, key, value, grad, fq, fk, pieces, features, earlier, group):
    head = pl.BlockSpec((ROWS, HEAD_DIM), lambda j: (0, j * GROUPS + group))
    fixed = pl.BlockSpec((ROWS, HEAD_DIM), lambda j: (0, 0))
    k_piece = pl.BlockSpec((128, HEAD_DIM), lambda j: (0, j))
    v_piece = pl.BlockSpec((128, HEAD_DIM), lambda j: (0, PER + j))
    f_piece = pl.BlockSpec((128, HEAD_DIM), lambda j: (0, 2 * PER))
    compact = pl.BlockSpec((ROWS, HEAD_DIM), lambda j: (0, j))
    back = pl.BlockSpec((2, 384, HEAD_DIM), lambda j: (0, 0, j))
    in_specs = [head] * 4 + [fixed] * 2 + [k_piece] * 6 + [v_piece] * 6 + [f_piece] * 6
    args = [query, key, value, grad, fq, fk] + pieces + pieces + features
    aliases = {}
    if earlier:
        in_specs = in_specs + [pl.BlockSpec(memory_space=pl.ANY)] * 2
        args = args + list(earlier)
        aliases = {24: 0, 25: 2}
    return pl.pallas_call(
        attention_kernel,
        grid=(PER,),
        in_specs=in_specs,
        out_specs=[
            head,
            pl.BlockSpec((HEAD_DIM, ROWS), lambda j: (j, 0)),
            head,
            compact,
            compact,
            back,
            back,
        ],
        out_shape=[
            jax.ShapeDtypeStruct((ROWS, HD), BF16),
            jax.ShapeDtypeStruct((COLS, ROWS), BF16),
            jax.ShapeDtypeStruct((ROWS, HD), BF16),
            jax.ShapeDtypeStruct((ROWS, COLS), F32),
            jax.ShapeDtypeStruct((ROWS, COLS), F32),
            jax.ShapeDtypeStruct((2, 384, COLS), BF16),
            jax.ShapeDtypeStruct((2, 384, COLS), BF16),
        ],
        scratch_shapes=[
            pltpu.VMEM((KEYS, ROWS), F32),
            pltpu.VMEM((KEYS, ROWS), BF16),
            pltpu.VMEM((8, 128), F32),
        ],
        input_output_aliases=aliases,
        compiler_params=params(),
        cost_estimate=pl.CostEstimate(
            flops=PER * 12 * ROWS * KEYS * HEAD_DIM, bytes_accessed=12 * ROWS * COLS * 2, transcendentals=PER * ROWS * KEYS
        ),
    )(*args)


def grad_weight_kernel(place_ref, ot_ref, c_ref, keep_ref, give_ref, lhs):
    @pl.when(pl.program_id(0) == 0)
    def _():
        core, y = place_ref[0], place_ref[1]
        for slot in range(2):
            half = core if slot == 0 else 1 - core
            for step in range(4):
                target = lax.rem(y + step, 4)
                for j in range(PER):
                    source = pl.multiple_of(j * 128 + half * 64 + target * 16, 16)
                    lhs[pl.ds(((slot * 4 + step) * PER + j) * 16, 16), :] = ot_ref[pl.ds(source, 16), :]

    out = dot_nn(lhs[...], c_ref[...])
    keep_ref[...] = out[: COLS // 2].astype(BF16)
    give_ref[...] = out[COLS // 2 :].astype(BF16)


def grad_weight_part(place, ot, cotangent):
    tile = 512
    shape = jax.ShapeDtypeStruct((COLS // 2, D), BF16)
    out = pl.BlockSpec((COLS // 2, tile), lambda n, s: (0, n))
    return pl.pallas_call(
        grad_weight_kernel,
        grid_spec=pltpu.PrefetchScalarGridSpec(
            num_scalar_prefetch=1,
            grid=(D // tile,),
            in_specs=[
                pl.BlockSpec((COLS, ROWS), lambda n, s: (0, 0)),
                pl.BlockSpec((ROWS, tile), lambda n, s: (0, n)),
            ],
            out_specs=[out, out],
            scratch_shapes=[pltpu.VMEM((COLS, ROWS), BF16)],
        ),
        out_shape=[shape, shape],
        compiler_params=params(),
        cost_estimate=pl.CostEstimate(flops=2 * COLS * ROWS * D, bytes_accessed=6 * 1024 * 1024, transcendentals=0),
    )(place, ot, cotangent)


def split_sum_kernel(count, axis, bounds, *refs):
    ins, outs = refs[:count], refs[count:]
    for (start, size), out in zip(bounds, outs):
        at = (slice(None),) * axis + (pl.ds(start, size),)
        total = ins[0][at].astype(F32)
        for ref in ins[1:]:
            total = total + ref[at].astype(F32)
        out[...] = total.astype(out.dtype)


def split_sum(arrays, axis, sizes):
    shape = arrays[0].shape
    starts = np.cumsum([0] + list(sizes))
    bounds = [(int(start), int(size)) for start, size in zip(starts, sizes)]
    whole = pl.BlockSpec(memory_space=pltpu.VMEM)
    outs = [jax.ShapeDtypeStruct(shape[:axis] + (size,) + shape[axis + 1 :], BF16) for size in sizes]
    count = math.prod(shape)
    return pl.pallas_call(
        partial(split_sum_kernel, len(arrays), axis, bounds),
        in_specs=[whole] * len(arrays),
        out_specs=[whole] * len(sizes),
        out_shape=outs,
        compiler_params=params(),
        cost_estimate=pl.CostEstimate(flops=count * len(arrays), bytes_accessed=2 * count * (len(arrays) + 1), transcendentals=0),
    )(*arrays)


def turn_sum_kernel(rows, place_ref, a_ref, b_ref, c_ref, d_ref, *outs):
    x = place_ref[2]
    for step, out in enumerate(outs):
        at = pl.ds(pl.multiple_of(lax.rem(x + step, 4) * rows, 16), rows)
        total = (a_ref[at, :].astype(F32) + b_ref[at, :].astype(F32)) + (c_ref[at, :].astype(F32) + d_ref[at, :].astype(F32))
        out[...] = total.astype(BF16)


def turn_sum(place, arrays):
    rows = arrays[0].shape[0] // 4
    whole = pl.BlockSpec(memory_space=pltpu.VMEM)
    out = jax.ShapeDtypeStruct((rows, D), BF16)
    return pl.pallas_call(
        partial(turn_sum_kernel, rows),
        in_specs=[pl.BlockSpec(memory_space=pltpu.SMEM)] + [whole] * 4,
        out_specs=[whole] * 4,
        out_shape=[out] * 4,
        compiler_params=params(),
        cost_estimate=pl.CostEstimate(flops=16 * rows * D, bytes_accessed=40 * rows * D, transcendentals=0),
    )(place, *arrays)


def finish_kernel(*refs):
    dk_ref, dv_ref, one, two, three, four = refs[:6]
    outs = refs[len(refs) - 2 :]
    token, row = iota((ROWS, 256), 0), iota((ROWS, 256), 1)
    spread = jnp.zeros((ROWS, 256), F32)
    start = 0
    for factor, count in ((4, 128), (8, 64), (16, 32), (16, 32)):
        local = row - start
        inside = (local >= 0) & (local < count) & (token >= local * factor) & (token < local * factor + factor)
        spread = jnp.where(inside, 1.0 / factor, spread)
        start = start + count
    spread = spread.astype(BF16)
    for place, (own, out) in enumerate(zip((dk_ref, dv_ref), outs)):
        rows = jnp.concatenate([ref[place] for ref in (one, two, three, four)], 0)
        out[...] = (own[...] + dot_nn(spread, rows)).astype(BF16)


def finish(dk, dv, returned, earlier, group):
    head = pl.BlockSpec((ROWS, HEAD_DIM), lambda j: (0, j * GROUPS + group))
    compact = pl.BlockSpec((ROWS, HEAD_DIM), lambda j: (0, j))
    in_specs = [compact] * 2 + [pl.BlockSpec((2, r.shape[1], HEAD_DIM), lambda j: (0, 0, j)) for r in returned]
    args = [dk, dv] + list(returned)
    aliases = {}
    if earlier:
        in_specs = in_specs + [pl.BlockSpec(memory_space=pl.ANY)] * 2
        args = args + list(earlier)
        aliases = {6: 0, 7: 1}
    shape = jax.ShapeDtypeStruct((ROWS, HD), BF16)
    return pl.pallas_call(
        finish_kernel,
        grid=(PER,),
        in_specs=in_specs,
        out_specs=[head, head],
        out_shape=[shape, shape],
        input_output_aliases=aliases,
        compiler_params=params(),
        cost_estimate=pl.CostEstimate(flops=4 * ROWS * 256 * COLS, bytes_accessed=14 * ROWS * COLS, transcendentals=0),
    )(*args)


def body(query, key, value, segment_ids, out_weight, cotangent):
    query, key, value = query[0], key[0], value[0]
    cotangent = cotangent[0]
    index = lax.axis_index("ctx")
    other = lax.axis_index("dp")
    core, x = jnp.bitwise_and(index, 1), jnp.right_shift(index, 2)
    z_lo = jnp.bitwise_and(jnp.right_shift(index, 1), 1)
    y, z_hi = jnp.right_shift(other, 1), jnp.bitwise_and(other, 1)
    place = jnp.stack([core, y, x]).astype(jnp.int32)

    pooled = []
    for group in range(GROUPS):
        outs = pool(key, value, segment_ids, group)
        if group == 0:
            fq, fk = outs[3:]
        pooled.append(outs[:3])
    pieces = []
    for one, two, three in pooled:
        from_z = swap(one, "ctx", 2)
        from_x = jnp.concatenate([swap(two, "ctx", 4), swap(three, "ctx", 12), swap(three, "ctx", 8)], 0)
        from_xz = swap(from_x, "ctx", 2)
        mine = [from_z, from_x, from_xz]
        pieces.append(mine + [swap(member, "ctx", 1) for member in mine])
    grad_attention = lax.dot_general(
        cotangent, out_weight, (((1,), (1,)), ((), ())), preferred_element_type=F32
    ).astype(BF16)

    earlier, ended, ends = (), (), []
    for group in range(GROUPS):
        o, ot, dq, dk, dv, keep, give = attention(
            query, key, value, grad_attention, fq, fk, pieces[group], pieces[0], earlier, group
        )
        earlier = (o, dq)
        own_one, own_two, own_xz = split_sum([keep, swap(give, "ctx", 1)], 1, (128, 128, 128))
        back_xz = swap(own_xz, "ctx", 2)
        back_z = swap(own_one, "ctx", 2)
        two, three, four = split_sum([own_two, back_xz], 1, (64, 32, 32))
        returned = [back_z, swap(two, "ctx", 4), swap(three, "ctx", 12), swap(four, "ctx", 8)]
        ended = finish(dk, dv, returned, ended, group)

        kept, given = grad_weight_part(place, ot, cotangent)
        quarter = COLS // 8
        parts = split_sum([kept, swap(given, "ctx", 1)], 0, (quarter,) * 4)
        parts = [parts[0]] + [shift(parts[step], "dp", 2 * step) for step in (1, 2, 3)]
        parts = turn_sum(place, parts)
        parts = [parts[0]] + [shift(parts[step], "ctx", 4 * step) for step in (1, 2, 3)]
        total = parts[0].astype(F32)
        for member in parts[1:]:
            total = total + member.astype(F32)
        ends.append(total)
    ends = jnp.concatenate(ends, 0).reshape(2, 16, D)
    kept = lax.dynamic_index_in_dim(ends, z_lo, 0, keepdims=False)
    given = lax.dynamic_index_in_dim(ends, 1 - z_lo, 0, keepdims=False)
    ends = (kept + swap(given.astype(BF16), "ctx", 2).astype(F32)).reshape(2, 8, D)
    kept = lax.dynamic_index_in_dim(ends, z_hi, 0, keepdims=False)
    given = lax.dynamic_index_in_dim(ends, 1 - z_hi, 0, keepdims=False)
    grad_weight = kept + swap(given, "dp", 1)

    output = lax.dot_general(o, out_weight, (((1,), (0,)), ((), ())), preferred_element_type=F32).astype(BF16)
    return output[None], dq[None], ended[0][None], ended[1][None], grad_weight


def solution(mesh):
    in_specs = (
        P("dp", "ctx", None),
        P("dp", "ctx", None),
        P("dp", "ctx", None),
        P("dp", "ctx"),
        P(),
        P("dp", "ctx", None),
    )
    out_specs = (
        P("dp", "ctx", None),
        P("dp", "ctx", None),
        P("dp", "ctx", None),
        P("dp", "ctx", None),
        P(("ctx", "dp"), None),
    )
    return jax.shard_map(body, mesh=mesh, in_specs=in_specs, out_specs=out_specs, check_vma=False)
```

```python
from functools import partial
import math

import jax
import jax.numpy as jnp
import numpy as np
from jax import lax
from jax.experimental import pallas as pl
from jax.experimental.pallas import tpu as pltpu
from jax.sharding import PartitionSpec as P

HEADS = 8
HEAD_DIM = 128
HD = 1024
D = 2048
ROWS = 512
GROUPS = 1
PER = HEADS // GROUPS
COLS = PER * HEAD_DIM
FACTORS = (4, 8, 16)
COARSE = tuple(ROWS // factor for factor in FACTORS)
SCALE = 1.0 / math.sqrt(HEAD_DIM)
BIG = float(2**30)
F32 = jnp.float32
BF16 = jnp.bfloat16


def params(mebibytes):
    return pltpu.CompilerParams(vmem_limit_bytes=mebibytes * 2**20)


def swap(array, axis, bits):
    return lax.ppermute(array, axis, [(i, i ^ bits) for i in range(lax.axis_size(axis))])


def shift(array, axis, step):
    size = lax.axis_size(axis)
    return lax.ppermute(array, axis, [(i, (i + step) % size) for i in range(size)])


def dot_nt(a, b):
    return lax.dot_general(a, b, (((1,), (1,)), ((), ())), preferred_element_type=F32)


def dot_nn(a, b):
    return lax.dot_general(a, b, (((1,), (0,)), ((), ())), preferred_element_type=F32)


def dot_tn(a, b):
    return lax.dot_general(a, b, (((0,), (0,)), ((), ())), preferred_element_type=F32)


def iota(shape, dim):
    return lax.broadcasted_iota(jnp.int32, shape, dim)


def offset_parts(factor):
    rest = math.log(factor) / SCALE
    parts = []
    for _ in range(3):
        part = float(np.asarray(rest, dtype=jnp.bfloat16))
        parts.append(part)
        rest = rest - part
    return parts


def pool_matrices():
    pools, picks = [], []
    for factor, count in zip(FACTORS, COARSE):
        row, col = iota((count, ROWS), 0), iota((count, ROWS), 1)
        inside = (col >= row * factor) & (col < row * factor + factor)
        pools.append(jnp.where(inside, 1.0 / factor, 0.0))
        picks.append(jnp.where(col == row * factor, 1.0, 0.0))
    return jnp.concatenate(pools, 0).astype(BF16), jnp.concatenate(picks, 0).astype(BF16)


def pool_kernel(with_features, *refs):
    if with_features:
        seg_ref, refs = refs[0], refs[1:]
    keys, values = refs[:PER], refs[PER : 2 * PER]
    outs = refs[2 * PER : 2 * PER + 3]
    pool, pick = pool_matrices()
    starts = np.cumsum((0,) + COARSE)

    def put(rows, column):
        for place, out in enumerate(outs):
            out[:, column : column + HEAD_DIM] = rows[starts[place] : starts[place + 1]].astype(BF16)

    for place, ref in enumerate(keys + values):
        put(dot_nn(pool, ref[...]), place * HEAD_DIM)
    if with_features:
        query_feature, key_feature = refs[2 * PER + 3 :]
        seg = seg_ref[...]
        kind = iota((8, ROWS), 0)
        rows = jnp.where(kind < 2, jnp.where(seg == kind, 1.0, 0.0), jnp.where(kind == 2, 1.0, 0.0)).astype(BF16)
        i, j = iota((8, HEAD_DIM), 0), iota((8, HEAD_DIM), 1)
        to_key = jnp.where((i < 2) & (i == j), 1.0, 0.0).astype(BF16)
        wrong = ((i == 0) & (j == 1)) | ((i == 1) & (j == 0))
        ones = (i == 2) & (j >= 2) & (j < 5)
        to_query = jnp.where(wrong, -BIG, jnp.where(ones, 1.0, 0.0)).astype(BF16)
        own = dot_tn(rows, to_key).astype(BF16)
        key_feature[...] = own
        query_feature[...] = dot_tn(rows, to_query).astype(BF16)
        picked = dot_nn(pick, own)
        lane = iota((1, HEAD_DIM), 1)
        for place, (factor, out) in enumerate(zip(FACTORS, outs)):
            parts = offset_parts(factor)
            offset = jnp.where(lane == 2, parts[0], jnp.where(lane == 3, parts[1], jnp.where(lane == 4, parts[2], 0.0)))
            rows_here = picked[starts[place] : starts[place + 1]] + offset
            out[:, 2 * COLS : 2 * COLS + HEAD_DIM] = rows_here.astype(BF16)


def pool(key, value, seg, group):
    with_features = group == 0
    width = 2 * COLS + (HEAD_DIM if with_features else 0)
    heads = [pl.BlockSpec((ROWS, HEAD_DIM), lambda i, h=j * GROUPS + group: (0, h)) for j in range(PER)]
    whole = pl.BlockSpec(memory_space=pltpu.VMEM)
    shapes = [jax.ShapeDtypeStruct((count, width), BF16) for count in COARSE]
    if with_features:
        shapes = shapes + [jax.ShapeDtypeStruct((ROWS, HEAD_DIM), BF16)] * 2
    args = ([seg] if with_features else []) + [key] * PER + [value] * PER
    return pl.pallas_call(
        partial(pool_kernel, with_features),
        grid=(1,),
        out_shape=shapes,
        in_specs=([whole] if with_features else []) + heads + heads,
        out_specs=[whole] * len(shapes),
        compiler_params=params(16),
        cost_estimate=pl.CostEstimate(flops=2 * 224 * ROWS * 2 * COLS, bytes_accessed=3 * ROWS * COLS * 2, transcendentals=0),
    )(*args)


KEYS = 1280
PAIRS = 3
COARSE_ROWS = 768


def pair(refs, place):
    return jnp.concatenate([refs[2 * place][...], refs[2 * place + 1][...]], 0)


def forward_kernel(*refs):
    q_ref, k_ref, v_ref, g_ref, fq_ref, fk_ref = refs[:6]
    ck, cv, cf = refs[6:12], refs[12:18], refs[18:24]
    p_ref, o_ref, ot_ref, delta_ref, scores = refs[24:]
    query = jnp.concatenate([q_ref[...], fq_ref[...]], 1)
    rate = SCALE * math.log2(math.e)
    starts = range(0, KEYS, 256)

    def part(local, coarse, place):
        return local[pl.ds(place * 256, 256), :] if place < 2 else pair(coarse, place - 2)

    top = None
    for place, start in enumerate(starts):
        key = jnp.concatenate([part(k_ref, ck, place), part(fk_ref, cf, place)], 1)
        here = dot_nt(key, query) * rate
        scores[pl.ds(start, 256), :] = here
        peak = jnp.max(here, 0, keepdims=True)
        top = peak if top is None else jnp.maximum(top, peak)
    total = None
    for start in starts:
        here = jnp.exp2(scores[pl.ds(start, 256), :] - top)
        scores[pl.ds(start, 256), :] = here
        add = jnp.sum(here, 0, keepdims=True)
        total = add if total is None else total + add
    inverse = 1.0 / total
    mixed = None
    for place, start in enumerate(starts):
        here = (scores[pl.ds(start, 256), :] * inverse).astype(BF16)
        p_ref[0, pl.ds(start, 256), :] = here
        add = dot_tn(part(v_ref, cv, place), here)
        mixed = add if mixed is None else mixed + add
    ot_ref[...] = mixed.astype(BF16)
    o_ref[...] = mixed.T.astype(BF16)
    delta = jnp.sum(g_ref[...].astype(F32).T * mixed, 0, keepdims=True)
    delta_ref[0] = jnp.broadcast_to(delta, (8, ROWS))


HEAD = pl.BlockSpec((ROWS, HEAD_DIM), lambda j: (0, j))
FIXED = pl.BlockSpec((ROWS, HEAD_DIM), lambda j: (0, 0))
K_PIECE = pl.BlockSpec((128, HEAD_DIM), lambda j: (0, j))
V_PIECE = pl.BlockSpec((128, HEAD_DIM), lambda j: (0, PER + j))
F_PIECE = pl.BlockSpec((128, HEAD_DIM), lambda j: (0, 2 * PER))
DELTA = pl.BlockSpec((1, 8, ROWS), lambda j: (j, 0, 0))
ANY = pl.BlockSpec(memory_space=pl.ANY)


def forward(query, key, value, grad, fq, fk, pieces):
    return pl.pallas_call(
        forward_kernel,
        grid=(HEADS,),
        in_specs=[HEAD] * 4 + [FIXED] * 2 + [K_PIECE] * 6 + [V_PIECE] * 6 + [F_PIECE] * 6,
        out_specs=[
            pl.BlockSpec((1, KEYS, ROWS), lambda j: (j, 0, 0)),
            HEAD,
            pl.BlockSpec((HEAD_DIM, ROWS), lambda j: (j, 0)),
            DELTA,
        ],
        out_shape=[
            jax.ShapeDtypeStruct((HEADS, KEYS, ROWS), BF16),
            jax.ShapeDtypeStruct((ROWS, HD), BF16),
            jax.ShapeDtypeStruct((HD, ROWS), BF16),
            jax.ShapeDtypeStruct((HEADS, 8, ROWS), F32),
        ],
        scratch_shapes=[pltpu.VMEM((KEYS, ROWS), F32)],
        compiler_params=params(20),
        cost_estimate=pl.CostEstimate(
            flops=HEADS * 4 * 4 * ROWS * KEYS * HEAD_DIM, bytes_accessed=20 * 2**20, transcendentals=HEADS * ROWS * KEYS
        ),
    )(query, key, value, grad, fq, fk, *pieces, *pieces, *pieces)


def slope_of(weight, value, grad, delta):
    return (weight.astype(F32) * (dot_nt(value, grad) - delta)).astype(BF16)


def coarse_kernel(*refs):
    q_ref, g_ref, delta_ref = refs[:3]
    weights, ck, cv = refs[3:6], refs[6:12], refs[12:18]
    keep_ref, give_ref, dq_ref = refs[19:]
    q, g = q_ref[...], g_ref[...]
    delta = delta_ref[0, 0:1, :]
    grad_q = None
    for place in range(PAIRS):
        weight, key, value = weights[place][0], pair(ck, place), pair(cv, place)
        slope = slope_of(weight, value, g, delta)
        grads = ((dot_nn(slope, q) * SCALE).astype(BF16), dot_nn(weight, g).astype(BF16))
        for side, grad in enumerate(grads):
            for half in range(2):
                piece = 2 * place + half
                out, row = (keep_ref, piece * 128) if piece < 3 else (give_ref, (piece - 3) * 128)
                out[side, pl.ds(row, 128), :] = grad[half * 128 : half * 128 + 128]
        add = dot_tn(key, slope)
        grad_q = add if grad_q is None else grad_q + add
    dq_ref[...] = grad_q


def coarse_backward(query, grad, delta, weights, pieces, after):
    back = pl.BlockSpec((2, 384, HEAD_DIM), lambda j: (0, 0, j))
    chunk = [pl.BlockSpec((1, 256, ROWS), lambda j, c=c: (j, c, 0)) for c in (2, 3, 4)]
    return pl.pallas_call(
        coarse_kernel,
        grid=(HEADS,),
        in_specs=[HEAD] * 2 + [DELTA] + chunk + [K_PIECE] * 6 + [V_PIECE] * 6 + [ANY],
        out_specs=[back, back, pl.BlockSpec((HEAD_DIM, ROWS), lambda j: (j, 0))],
        out_shape=[
            jax.ShapeDtypeStruct((2, 384, HD), BF16),
            jax.ShapeDtypeStruct((2, 384, HD), BF16),
            jax.ShapeDtypeStruct((HD, ROWS), F32),
        ],
        compiler_params=params(20),
        cost_estimate=pl.CostEstimate(
            flops=HEADS * 4 * 4 * ROWS * COARSE_ROWS * HEAD_DIM, bytes_accessed=16 * 2**20, transcendentals=0
        ),
    )(query, grad, delta, weights, weights, weights, *pieces, *pieces, after)


def local_kernel(q_ref, k_ref, v_ref, g_ref, delta_ref, p_ref, part_ref, _, dq_ref, dk_ref, dv_ref):
    q, g = q_ref[...], g_ref[...]
    delta = delta_ref[0, 0:1, :]
    grad_q = part_ref[...]
    for start in (0, 256):
        at = pl.ds(start, 256)
        weight = p_ref[0, at, :]
        slope = slope_of(weight, v_ref[at, :], g, delta)
        dk_ref[at, :] = dot_nn(slope, q) * SCALE
        dv_ref[at, :] = dot_nn(weight, g)
        grad_q = grad_q + dot_tn(k_ref[at, :], slope)
    dq_ref[...] = (grad_q * SCALE).T.astype(BF16)


def local_backward(query, key, value, grad, delta, weights, partial_q, after):
    return pl.pallas_call(
        local_kernel,
        grid=(HEADS,),
        in_specs=[HEAD] * 4
        + [DELTA, pl.BlockSpec((1, ROWS, ROWS), lambda j: (j, 0, 0)), pl.BlockSpec((HEAD_DIM, ROWS), lambda j: (j, 0)), ANY],
        out_specs=[HEAD] * 3,
        out_shape=[
            jax.ShapeDtypeStruct((ROWS, HD), BF16),
            jax.ShapeDtypeStruct((ROWS, HD), F32),
            jax.ShapeDtypeStruct((ROWS, HD), F32),
        ],
        compiler_params=params(16),
        cost_estimate=pl.CostEstimate(
            flops=HEADS * 4 * 4 * ROWS * ROWS * HEAD_DIM, bytes_accessed=16 * 2**20, transcendentals=0
        ),
    )(query, key, value, grad, delta, weights, partial_q, after)


def project_kernel(a_ref, w_ref, _, out_ref):
    out_ref[...] = dot_nn(a_ref[...], w_ref[...]).astype(BF16)


def project(attention, weight, after):
    tile = 512
    return pl.pallas_call(
        project_kernel,
        grid=(D // tile,),
        in_specs=[
            pl.BlockSpec((ROWS, HD), lambda n: (0, 0)),
            pl.BlockSpec((HD, tile), lambda n: (0, n)),
            ANY,
        ],
        out_specs=pl.BlockSpec((ROWS, tile), lambda n: (0, n)),
        out_shape=jax.ShapeDtypeStruct((ROWS, D), BF16),
        compiler_params=params(12),
        cost_estimate=pl.CostEstimate(flops=2 * ROWS * HD * D, bytes_accessed=7 * 2**20, transcendentals=0),
    )(attention, weight, after)


def stack_kernel(*refs):
    *ins, out = refs
    start = 0
    for ref in ins:
        out[pl.ds(start, ref.shape[0]), :] = ref[...]
        start = start + ref.shape[0]


def stack(arrays):
    rows, columns = sum(array.shape[0] for array in arrays), arrays[0].shape[1]
    whole = pl.BlockSpec(memory_space=pltpu.VMEM)
    return pl.pallas_call(
        stack_kernel,
        in_specs=[whole] * len(arrays),
        out_specs=whole,
        out_shape=jax.ShapeDtypeStruct((rows, columns), BF16),
        compiler_params=params(4),
        cost_estimate=pl.CostEstimate(flops=0, bytes_accessed=4 * rows * columns, transcendentals=0),
    )(*arrays)


def grad_weight_kernel(place_ref, ot_ref, c_ref, keep_ref, give_ref, lhs):
    @pl.when(pl.program_id(0) == 0)
    def _():
        core, y = place_ref[0], place_ref[1]
        for slot in range(2):
            half = core if slot == 0 else 1 - core
            for step in range(4):
                target = lax.rem(y + step, 4)
                for j in range(PER):
                    source = pl.multiple_of(j * 128 + half * 64 + target * 16, 16)
                    lhs[pl.ds(((slot * 4 + step) * PER + j) * 16, 16), :] = ot_ref[pl.ds(source, 16), :]

    out = dot_nn(lhs[...], c_ref[...])
    keep_ref[...] = out[: COLS // 2].astype(BF16)
    give_ref[...] = out[COLS // 2 :].astype(BF16)


def grad_weight_part(place, ot, cotangent):
    tile = 512
    shape = jax.ShapeDtypeStruct((COLS // 2, D), BF16)
    out = pl.BlockSpec((COLS // 2, tile), lambda n, s: (0, n))
    return pl.pallas_call(
        grad_weight_kernel,
        grid_spec=pltpu.PrefetchScalarGridSpec(
            num_scalar_prefetch=1,
            grid=(D // tile,),
            in_specs=[
                pl.BlockSpec((COLS, ROWS), lambda n, s: (0, 0)),
                pl.BlockSpec((ROWS, tile), lambda n, s: (0, n)),
            ],
            out_specs=[out, out],
            scratch_shapes=[pltpu.VMEM((COLS, ROWS), BF16)],
        ),
        out_shape=[shape, shape],
        compiler_params=params(16),
        cost_estimate=pl.CostEstimate(flops=2 * COLS * ROWS * D, bytes_accessed=6 * 1024 * 1024, transcendentals=0),
    )(place, ot, cotangent)


def split_sum_kernel(count, axis, bounds, *refs):
    ins, outs = refs[:count], refs[count:]
    for (start, size), out in zip(bounds, outs):
        at = (slice(None),) * axis + (pl.ds(start, size),)
        total = ins[0][at].astype(F32)
        for ref in ins[1:]:
            total = total + ref[at].astype(F32)
        out[...] = total.astype(out.dtype)


def split_sum(arrays, axis, sizes):
    shape = arrays[0].shape
    starts = np.cumsum([0] + list(sizes))
    bounds = [(int(start), int(size)) for start, size in zip(starts, sizes)]
    whole = pl.BlockSpec(memory_space=pltpu.VMEM)
    outs = [jax.ShapeDtypeStruct(shape[:axis] + (size,) + shape[axis + 1 :], BF16) for size in sizes]
    count = math.prod(shape)
    return pl.pallas_call(
        partial(split_sum_kernel, len(arrays), axis, bounds),
        in_specs=[whole] * len(arrays),
        out_specs=[whole] * len(sizes),
        out_shape=outs,
        compiler_params=params(16),
        cost_estimate=pl.CostEstimate(flops=count * len(arrays), bytes_accessed=2 * count * (len(arrays) + 1), transcendentals=0),
    )(*arrays)


def turn_sum_kernel(rows, place_ref, a_ref, b_ref, c_ref, d_ref, *outs):
    x = place_ref[2]
    for step, out in enumerate(outs):
        at = pl.ds(pl.multiple_of(lax.rem(x + step, 4) * rows, 16), rows)
        total = (a_ref[at, :].astype(F32) + b_ref[at, :].astype(F32)) + (c_ref[at, :].astype(F32) + d_ref[at, :].astype(F32))
        out[...] = total.astype(BF16)


def turn_sum(place, arrays):
    rows = arrays[0].shape[0] // 4
    whole = pl.BlockSpec(memory_space=pltpu.VMEM)
    out = jax.ShapeDtypeStruct((rows, D), BF16)
    return pl.pallas_call(
        partial(turn_sum_kernel, rows),
        in_specs=[pl.BlockSpec(memory_space=pltpu.SMEM)] + [whole] * 4,
        out_specs=[whole] * 4,
        out_shape=[out] * 4,
        compiler_params=params(16),
        cost_estimate=pl.CostEstimate(flops=16 * rows * D, bytes_accessed=40 * rows * D, transcendentals=0),
    )(place, *arrays)


def finish_kernel(*refs):
    dk_ref, dv_ref, one, two, three, four = refs[:6]
    outs = refs[len(refs) - 2 :]
    token, row = iota((ROWS, 256), 0), iota((ROWS, 256), 1)
    spread = jnp.zeros((ROWS, 256), F32)
    start = 0
    for factor, count in ((4, 128), (8, 64), (16, 32), (16, 32)):
        local = row - start
        inside = (local >= 0) & (local < count) & (token >= local * factor) & (token < local * factor + factor)
        spread = jnp.where(inside, 1.0 / factor, spread)
        start = start + count
    spread = spread.astype(BF16)
    for place, (own, out) in enumerate(zip((dk_ref, dv_ref), outs)):
        rows = jnp.concatenate([ref[place] for ref in (one, two, three, four)], 0)
        out[...] = (own[...] + dot_nn(spread, rows)).astype(BF16)


def finish(dk, dv, returned, earlier, group):
    head = pl.BlockSpec((ROWS, HEAD_DIM), lambda j: (0, j * GROUPS + group))
    compact = pl.BlockSpec((ROWS, HEAD_DIM), lambda j: (0, j))
    in_specs = [compact] * 2 + [pl.BlockSpec((2, r.shape[1], HEAD_DIM), lambda j: (0, 0, j)) for r in returned]
    args = [dk, dv] + list(returned)
    aliases = {}
    if earlier:
        in_specs = in_specs + [pl.BlockSpec(memory_space=pl.ANY)] * 2
        args = args + list(earlier)
        aliases = {6: 0, 7: 1}
    shape = jax.ShapeDtypeStruct((ROWS, HD), BF16)
    return pl.pallas_call(
        finish_kernel,
        grid=(PER,),
        in_specs=in_specs,
        out_specs=[head, head],
        out_shape=[shape, shape],
        input_output_aliases=aliases,
        compiler_params=params(16),
        cost_estimate=pl.CostEstimate(flops=4 * ROWS * 256 * COLS, bytes_accessed=14 * ROWS * COLS, transcendentals=0),
    )(*args)


def body(query, key, value, segment_ids, out_weight, cotangent):
    query, key, value = query[0], key[0], value[0]
    cotangent = cotangent[0]
    index = lax.axis_index("ctx")
    other = lax.axis_index("dp")
    core, x = jnp.bitwise_and(index, 1), jnp.right_shift(index, 2)
    z_lo = jnp.bitwise_and(jnp.right_shift(index, 1), 1)
    y, z_hi = jnp.right_shift(other, 1), jnp.bitwise_and(other, 1)
    place = jnp.stack([core, y, x]).astype(jnp.int32)

    one, two, three, fq, fk = pool(key, value, segment_ids, 0)
    from_z = swap(one, "ctx", 2)
    from_x = stack([swap(two, "ctx", 4), swap(three, "ctx", 12), swap(three, "ctx", 8)])
    from_xz = swap(from_x, "ctx", 2)
    mine = [from_z, from_x, from_xz]
    pieces = mine + [swap(member, "ctx", 1) for member in mine]
    grad_attention = lax.dot_general(
        cotangent, out_weight, (((1,), (1,)), ((), ())), preferred_element_type=F32
    ).astype(BF16)

    weights, attention, attention_t, delta = forward(query, key, value, grad_attention, fq, fk, pieces)
    kept, given = grad_weight_part(place, attention_t, cotangent)
    keep, give, partial_q = coarse_backward(query, grad_attention, delta, weights, pieces, given)
    quarter = COLS // 8
    parts = split_sum([kept, swap(given, "ctx", 1)], 0, (quarter,) * 4)
    own_one, own_two, own_xz = split_sum([keep, swap(give, "ctx", 1)], 1, (128, 128, 128))
    back_xz = swap(own_xz, "ctx", 2)
    back_z = swap(own_one, "ctx", 2)
    grad_query, dk, dv = local_backward(query, key, value, grad_attention, delta, weights, partial_q, own_one)
    output = project(attention, out_weight, grad_query)
    two, three, four = split_sum([own_two, back_xz], 1, (64, 32, 32))
    returned = [back_z, swap(two, "ctx", 4), swap(three, "ctx", 12), swap(four, "ctx", 8)]
    grad_key, grad_value = finish(dk, dv, returned, (), 0)

    parts = [parts[0]] + [shift(parts[step], "dp", 2 * step) for step in (1, 2, 3)]
    parts = turn_sum(place, parts)
    parts = [parts[0]] + [shift(parts[step], "ctx", 4 * step) for step in (1, 2, 3)]
    ends = parts[0].astype(F32)
    for member in parts[1:]:
        ends = ends + member.astype(F32)
    ends = ends.reshape(2, 16, D)
    kept = lax.dynamic_index_in_dim(ends, z_lo, 0, keepdims=False)
    given = lax.dynamic_index_in_dim(ends, 1 - z_lo, 0, keepdims=False)
    ends = (kept + swap(given.astype(BF16), "ctx", 2).astype(F32)).reshape(2, 8, D)
    kept = lax.dynamic_index_in_dim(ends, z_hi, 0, keepdims=False)
    given = lax.dynamic_index_in_dim(ends, 1 - z_hi, 0, keepdims=False)
    grad_weight = kept + swap(given, "dp", 1)

    return output[None], grad_query[None], grad_key[None], grad_value[None], grad_weight


def solution(mesh):
    in_specs = (
        P("dp", "ctx", None),
        P("dp", "ctx", None),
        P("dp", "ctx", None),
        P("dp", "ctx"),
        P(),
        P("dp", "ctx", None),
    )
    out_specs = (
        P("dp", "ctx", None),
        P("dp", "ctx", None),
        P("dp", "ctx", None),
        P("dp", "ctx", None),
        P(("ctx", "dp"), None),
    )
    return jax.shard_map(body, mesh=mesh, in_specs=in_specs, out_specs=out_specs, check_vma=False)
```

```python
from functools import partial
import math

import jax
import jax.numpy as jnp
import numpy as np
from jax import lax
from jax.experimental import pallas as pl
from jax.experimental.pallas import tpu as pltpu
from jax.sharding import PartitionSpec as P

HEADS = 8
HEAD_DIM = 128
HD = 1024
D = 2048
ROWS = 512
GROUPS = 1
PER = HEADS // GROUPS
COLS = PER * HEAD_DIM
FACTORS = (4, 8, 16)
COARSE = tuple(ROWS // factor for factor in FACTORS)
SCALE = 1.0 / math.sqrt(HEAD_DIM)
BIG = float(2**30)
F32 = jnp.float32
BF16 = jnp.bfloat16


def params(mebibytes):
    return pltpu.CompilerParams(vmem_limit_bytes=mebibytes * 2**20)


def swap(array, axis, bits):
    return lax.ppermute(array, axis, [(i, i ^ bits) for i in range(lax.axis_size(axis))])


def shift(array, axis, step):
    size = lax.axis_size(axis)
    return lax.ppermute(array, axis, [(i, (i + step) % size) for i in range(size)])


def dot_nt(a, b):
    return lax.dot_general(a, b, (((1,), (1,)), ((), ())), preferred_element_type=F32)


def dot_nn(a, b):
    return lax.dot_general(a, b, (((1,), (0,)), ((), ())), preferred_element_type=F32)


def dot_tn(a, b):
    return lax.dot_general(a, b, (((0,), (0,)), ((), ())), preferred_element_type=F32)


def iota(shape, dim):
    return lax.broadcasted_iota(jnp.int32, shape, dim)


def offset_parts(factor):
    rest = math.log(factor) / SCALE
    parts = []
    for _ in range(3):
        part = float(np.asarray(rest, dtype=jnp.bfloat16))
        parts.append(part)
        rest = rest - part
    return parts


def pool_matrix(factor, weight):
    count = ROWS // factor
    row, col = iota((count, ROWS), 0), iota((count, ROWS), 1)
    inside = (col >= row * factor) & (col < row * factor + weight)
    return jnp.where(inside, 1.0 / weight, 0.0).astype(BF16)


def pool_kernel(seg_hbm, key_hbm, value_hbm, one, two, three, fq_ref, fk_ref, seg_ref, key_ref, value_ref, sems):
    copies = [
        pltpu.make_async_copy(source, target, sems.at[place])
        for place, (source, target) in enumerate(((seg_hbm, seg_ref), (key_hbm, key_ref), (value_hbm, value_ref)))
    ]
    for copy in copies:
        copy.start()
    outs = (one, two, three)
    starts = np.cumsum((0,) + COARSE)
    pool = jnp.concatenate([pool_matrix(factor, factor) for factor in FACTORS], 0)
    pick = jnp.concatenate([pool_matrix(factor, 1) for factor in FACTORS], 0)
    copies[0].wait()
    seg = seg_ref[...]
    kind = iota((8, ROWS), 0)
    rows = jnp.where(kind < 2, jnp.where(seg == kind, 1.0, 0.0), jnp.where(kind == 2, 1.0, 0.0)).astype(BF16)
    i, j = iota((8, HEAD_DIM), 0), iota((8, HEAD_DIM), 1)
    to_key = jnp.where((i < 2) & (i == j), 1.0, 0.0).astype(BF16)
    wrong = ((i == 0) & (j == 1)) | ((i == 1) & (j == 0))
    ones = (i == 2) & (j >= 2) & (j < 5)
    to_query = jnp.where(wrong, -BIG, jnp.where(ones, 1.0, 0.0)).astype(BF16)
    own = dot_tn(rows, to_key).astype(BF16)
    fk_ref[...] = own
    fq_ref[...] = dot_tn(rows, to_query).astype(BF16)
    picked = dot_nn(pick, own)
    lane = iota((1, HEAD_DIM), 1)
    for place, (factor, out) in enumerate(zip(FACTORS, outs)):
        parts = offset_parts(factor)
        offset = jnp.where(lane == 2, parts[0], jnp.where(lane == 3, parts[1], jnp.where(lane == 4, parts[2], 0.0)))
        out[:, 2 * HD :] = (picked[starts[place] : starts[place + 1]] + offset).astype(BF16)
    for copy, ref, column in zip(copies[1:], (key_ref, value_ref), (0, HD)):
        copy.wait()
        for start in range(0, HD, 256):
            mean = dot_nn(pool, ref[:, start : start + 256])
            for place, out in enumerate(outs):
                out[:, column + start : column + start + 256] = mean[starts[place] : starts[place + 1]].astype(BF16)


WIDTH = 2 * HD + HEAD_DIM
POOL_LIMIT = 60
WHOLE = pl.BlockSpec(memory_space=pltpu.VMEM)
ANY = pl.BlockSpec(memory_space=pl.ANY)
HBM = pl.BlockSpec(memory_space=pltpu.HBM)
MARK = jax.ShapeDtypeStruct((8, 128), F32)


def pool(seg, key, value):
    feature = jax.ShapeDtypeStruct((ROWS, HEAD_DIM), BF16)
    token = pltpu.VMEM((ROWS, HD), BF16)
    return pl.pallas_call(
        pool_kernel,
        in_specs=[HBM] * 3,
        out_specs=[WHOLE] * 5,
        out_shape=[jax.ShapeDtypeStruct((count, WIDTH), BF16) for count in COARSE] + [feature, feature],
        scratch_shapes=[pltpu.VMEM((1, ROWS), jnp.int32), token, token, pltpu.SemaphoreType.DMA((3,))],
        compiler_params=params(POOL_LIMIT),
        cost_estimate=pl.CostEstimate(flops=2 * 224 * ROWS * 2 * HD, bytes_accessed=2 * 2**20, transcendentals=0),
    )(seg, key, value)


def pause_kernel(*refs):
    refs[-1][...] = jnp.zeros_like(refs[-1])


def pause(after):
    return pl.pallas_call(
        pause_kernel,
        in_specs=[ANY] * len(after),
        out_specs=WHOLE,
        out_shape=MARK,
        compiler_params=params(1),
        cost_estimate=pl.CostEstimate(flops=2 * 10**10, bytes_accessed=0, transcendentals=0),
    )(*after)


COARSE_ROWS = 768
RATE = SCALE * math.log2(math.e)


def columns(h):
    return pl.ds(pl.multiple_of(h * HEAD_DIM, HEAD_DIM), HEAD_DIM)


def pair(refs, place, at):
    return jnp.concatenate([refs[2 * place][:, at], refs[2 * place + 1][:, at]], 0)


def joined(total, add):
    return add if total is None else total + add


def each_head(step):
    lax.fori_loop(0, HEADS, lambda h, carry: (step(h), carry)[1], 0)


def local_forward_kernel(*refs):
    q_ref, k_ref, v_ref, fq_ref, fk_ref = refs[:5]
    p_ref, mixed_ref, stat_ref, scores = refs[-4:]

    def step(h):
        at = columns(h)
        query = jnp.concatenate([q_ref[:, at], fq_ref[...]], 1)
        top = None
        for start in (0, 256):
            rows = pl.ds(start, 256)
            here = dot_nt(jnp.concatenate([k_ref[rows, at], fk_ref[rows, :]], 1), query) * RATE
            scores[rows, :] = here
            peak = jnp.max(here, 0, keepdims=True)
            top = peak if top is None else jnp.maximum(top, peak)
        total, mixed = None, None
        for start in (0, 256):
            rows = pl.ds(start, 256)
            here = jnp.exp2(scores[rows, :] - top)
            total = joined(total, jnp.sum(here, 0, keepdims=True))
            here = here.astype(BF16)
            p_ref[h, rows, :] = here
            mixed = joined(mixed, dot_tn(v_ref[rows, at], here))
        mixed_ref[at, :] = mixed
        stat_ref[h, 0:1, :] = top
        stat_ref[h, 1:2, :] = total

    each_head(step)


def local_forward(query, key, value, fq, fk, after):
    return pl.pallas_call(
        local_forward_kernel,
        in_specs=[WHOLE] * 5 + [ANY] * len(after),
        out_specs=[WHOLE] * 3,
        out_shape=[
            jax.ShapeDtypeStruct((HEADS, ROWS, ROWS), BF16),
            jax.ShapeDtypeStruct((HD, ROWS), F32),
            jax.ShapeDtypeStruct((HEADS, 8, ROWS), F32),
        ],
        scratch_shapes=[pltpu.VMEM((ROWS, ROWS), F32)],
        compiler_params=params(12),
        cost_estimate=pl.CostEstimate(
            flops=HEADS * 16 * ROWS * ROWS * HEAD_DIM, bytes_accessed=9 * 2**20, transcendentals=HEADS * ROWS * ROWS
        ),
    )(query, key, value, fq, fk, *after)


def coarse_forward_kernel(*refs):
    q_ref, g_ref, fq_ref, mixed_ref, stat_ref = refs[:5]
    pieces = refs[5:11]
    p_ref, o_ref, ot_ref, row_ref, scores = refs[11:]

    def step(h):
        at = columns(h)
        query = jnp.concatenate([q_ref[:, at], fq_ref[...]], 1)
        before, total = stat_ref[h, 0:1, :], stat_ref[h, 1:2, :]
        top = before
        for place in range(3):
            key = jnp.concatenate([pair(pieces, place, at), pair(pieces, place, slice(2 * HD, WIDTH))], 1)
            here = dot_nt(key, query) * RATE
            scores[pl.ds(place * 256, 256), :] = here
            top = jnp.maximum(top, jnp.max(here, 0, keepdims=True))
        factor = jnp.exp2(before - top)
        total = total * factor
        for place in range(3):
            rows = pl.ds(place * 256, 256)
            here = jnp.exp2(scores[rows, :] - top)
            scores[rows, :] = here
            total = total + jnp.sum(here, 0, keepdims=True)
        inverse = 1.0 / total
        factor = factor * inverse
        mixed = mixed_ref[at, :] * factor
        for place in range(3):
            rows = pl.ds(place * 256, 256)
            here = (scores[rows, :] * inverse).astype(BF16)
            p_ref[h, rows, :] = here
            mixed = mixed + dot_tn(pair(pieces, place, columns(HEADS + h)), here)
        ot_ref[at, :] = mixed.astype(BF16)
        o_ref[:, at] = mixed.T.astype(BF16)
        row_ref[h, 0:1, :] = jnp.sum(g_ref[:, at].astype(F32).T * mixed, 0, keepdims=True)
        row_ref[h, 1:2, :] = factor

    each_head(step)


def coarse_forward(query, grad, fq, mixed, stats, pieces):
    return pl.pallas_call(
        coarse_forward_kernel,
        in_specs=[WHOLE] * 11,
        out_specs=[WHOLE] * 4,
        out_shape=[
            jax.ShapeDtypeStruct((HEADS, COARSE_ROWS, ROWS), BF16),
            jax.ShapeDtypeStruct((ROWS, HD), BF16),
            jax.ShapeDtypeStruct((HD, ROWS), BF16),
            jax.ShapeDtypeStruct((HEADS, 8, ROWS), F32),
        ],
        scratch_shapes=[pltpu.VMEM((COARSE_ROWS, ROWS), F32)],
        compiler_params=params(12),
        cost_estimate=pl.CostEstimate(
            flops=HEADS * 16 * ROWS * COARSE_ROWS * HEAD_DIM,
            bytes_accessed=16 * 2**20,
            transcendentals=HEADS * ROWS * COARSE_ROWS,
        ),
    )(query, grad, fq, mixed, stats, *pieces)


def slope_of(weight, value, grad, delta):
    return (weight.astype(F32) * (dot_nt(value, grad) - delta)).astype(BF16)


def coarse_backward_kernel(*refs):
    q_ref, g_ref, row_ref, p_ref = refs[:4]
    pieces = refs[4:10]
    keep_ref, give_ref, dq_ref = refs[-3:]

    def step(h):
        at = columns(h)
        q, g = q_ref[:, at], g_ref[:, at]
        delta = row_ref[h, 0:1, :]
        grad_q = None
        for place in range(3):
            weight = p_ref[h, pl.ds(place * 256, 256), :]
            key, value = pair(pieces, place, at), pair(pieces, place, columns(HEADS + h))
            slope = slope_of(weight, value, g, delta)
            grads = ((dot_nn(slope, q) * SCALE).astype(BF16), dot_nn(weight, g).astype(BF16))
            for side, grad in enumerate(grads):
                for half in range(2):
                    piece = 2 * place + half
                    out, row = (keep_ref, piece * 128) if piece < 3 else (give_ref, (piece - 3) * 128)
                    out[side, pl.ds(row, 128), at] = grad[half * 128 : half * 128 + 128]
            grad_q = joined(grad_q, dot_tn(key, slope))
        dq_ref[at, :] = grad_q

    each_head(step)


def coarse_backward(query, grad, rows, weights, pieces, after):
    return pl.pallas_call(
        coarse_backward_kernel,
        in_specs=[WHOLE] * 10 + [ANY] * len(after),
        out_specs=[WHOLE] * 3,
        out_shape=[
            jax.ShapeDtypeStruct((2, 384, HD), BF16),
            jax.ShapeDtypeStruct((2, 384, HD), BF16),
            jax.ShapeDtypeStruct((HD, ROWS), F32),
        ],
        compiler_params=params(12),
        cost_estimate=pl.CostEstimate(
            flops=HEADS * 16 * ROWS * COARSE_ROWS * HEAD_DIM, bytes_accessed=16 * 2**20, transcendentals=0
        ),
    )(query, grad, rows, weights, *pieces, *after)


def local_backward_kernel(*refs):
    q_ref, k_ref, v_ref, g_ref, row_ref, p_ref, part_ref = refs[:7]
    dq_ref, dk_ref, dv_ref, mark_ref = refs[-4:]
    mark_ref[...] = jnp.zeros_like(mark_ref)

    def step(h):
        at = columns(h)
        q, g = q_ref[:, at], g_ref[:, at]
        delta, factor = row_ref[h, 0:1, :], row_ref[h, 1:2, :]
        grad_q = part_ref[at, :]
        for start in (0, 256):
            rows = pl.ds(start, 256)
            weight = p_ref[h, rows, :].astype(F32) * factor
            slope = (weight * (dot_nt(v_ref[rows, at], g) - delta)).astype(BF16)
            dk_ref[rows, at] = dot_nn(slope, q) * SCALE
            dv_ref[rows, at] = dot_nn(weight.astype(BF16), g)
            grad_q = grad_q + dot_tn(k_ref[rows, at], slope)
        dq_ref[:, at] = (grad_q * SCALE).T.astype(BF16)

    each_head(step)


def local_backward(query, key, value, grad, rows, weights, partial_q, after):
    return pl.pallas_call(
        local_backward_kernel,
        in_specs=[WHOLE] * 7 + [ANY] * len(after),
        out_specs=[WHOLE] * 4,
        out_shape=[
            jax.ShapeDtypeStruct((ROWS, HD), BF16),
            jax.ShapeDtypeStruct((ROWS, HD), F32),
            jax.ShapeDtypeStruct((ROWS, HD), F32),
            MARK,
        ],
        compiler_params=params(12),
        cost_estimate=pl.CostEstimate(
            flops=HEADS * 16 * ROWS * ROWS * HEAD_DIM, bytes_accessed=16 * 2**20, transcendentals=0
        ),
    )(query, key, value, grad, rows, weights, partial_q, *after)


def project_kernel(a_ref, w_ref, _, out_ref, mark_ref):
    mark_ref[...] = jnp.zeros_like(mark_ref)
    out_ref[...] = dot_nn(a_ref[...], w_ref[...]).astype(BF16)


def project(attention, weight, after):
    tile = 512
    return pl.pallas_call(
        project_kernel,
        grid=(D // tile,),
        in_specs=[
            pl.BlockSpec((ROWS, HD), lambda n: (0, 0)),
            pl.BlockSpec((HD, tile), lambda n: (0, n)),
            ANY,
        ],
        out_specs=[pl.BlockSpec((ROWS, tile), lambda n: (0, n)), pl.BlockSpec((8, 128), lambda n: (0, 0))],
        out_shape=[jax.ShapeDtypeStruct((ROWS, D), BF16), MARK],
        compiler_params=params(12),
        cost_estimate=pl.CostEstimate(flops=2 * ROWS * HD * D, bytes_accessed=7 * 2**20, transcendentals=0),
    )(attention, weight, after)


def stack_kernel(count, *refs):
    out, start = refs[-1], 0
    for ref in refs[:count]:
        out[pl.ds(start, ref.shape[0]), :] = ref[...]
        start = start + ref.shape[0]


def stack(arrays, after):
    rows, width = sum(array.shape[0] for array in arrays), arrays[0].shape[1]
    return pl.pallas_call(
        partial(stack_kernel, len(arrays)),
        in_specs=[WHOLE] * len(arrays) + [ANY] * len(after),
        out_specs=WHOLE,
        out_shape=jax.ShapeDtypeStruct((rows, width), BF16),
        compiler_params=params(4),
        cost_estimate=pl.CostEstimate(flops=0, bytes_accessed=4 * rows * width, transcendentals=0),
    )(*arrays, *after)


def grad_weight_kernel(place_ref, ot_ref, c_ref, keep_ref, give_ref, lhs):
    @pl.when(pl.program_id(0) == 0)
    def _():
        core, y = place_ref[0], place_ref[1]
        for slot in range(2):
            half = core if slot == 0 else 1 - core
            for step in range(4):
                target = lax.rem(y + step, 4)
                for j in range(PER):
                    source = pl.multiple_of(j * 128 + half * 64 + target * 16, 16)
                    lhs[pl.ds(((slot * 4 + step) * PER + j) * 16, 16), :] = ot_ref[pl.ds(source, 16), :]

    out = dot_nn(lhs[...], c_ref[...])
    keep_ref[...] = out[: COLS // 2].astype(BF16)
    give_ref[...] = out[COLS // 2 :].astype(BF16)


def grad_weight_part(place, ot, cotangent):
    tile = 512
    shape = jax.ShapeDtypeStruct((COLS // 2, D), BF16)
    out = pl.BlockSpec((COLS // 2, tile), lambda n, s: (0, n))
    return pl.pallas_call(
        grad_weight_kernel,
        grid_spec=pltpu.PrefetchScalarGridSpec(
            num_scalar_prefetch=1,
            grid=(D // tile,),
            in_specs=[
                pl.BlockSpec((COLS, ROWS), lambda n, s: (0, 0)),
                pl.BlockSpec((ROWS, tile), lambda n, s: (0, n)),
            ],
            out_specs=[out, out],
            scratch_shapes=[pltpu.VMEM((COLS, ROWS), BF16)],
        ),
        out_shape=[shape, shape],
        compiler_params=params(16),
        cost_estimate=pl.CostEstimate(flops=2 * COLS * ROWS * D, bytes_accessed=6 * 1024 * 1024, transcendentals=0),
    )(place, ot, cotangent)


def split_sum_kernel(count, axis, bounds, *refs):
    ins, outs = refs[:count], refs[len(refs) - len(bounds) :]
    for (start, size), out in zip(bounds, outs):
        at = (slice(None),) * axis + (pl.ds(start, size),)
        total = ins[0][at].astype(F32)
        for ref in ins[1:]:
            total = total + ref[at].astype(F32)
        out[...] = total.astype(out.dtype)


def split_sum(arrays, axis, sizes, after=()):
    shape = arrays[0].shape
    starts = np.cumsum([0] + list(sizes))
    bounds = [(int(start), int(size)) for start, size in zip(starts, sizes)]
    whole = pl.BlockSpec(memory_space=pltpu.VMEM)
    outs = [jax.ShapeDtypeStruct(shape[:axis] + (size,) + shape[axis + 1 :], BF16) for size in sizes]
    count = math.prod(shape)
    return pl.pallas_call(
        partial(split_sum_kernel, len(arrays), axis, bounds),
        in_specs=[whole] * len(arrays) + [ANY] * len(after),
        out_specs=[whole] * len(sizes),
        out_shape=outs,
        compiler_params=params(16),
        cost_estimate=pl.CostEstimate(flops=count * len(arrays), bytes_accessed=2 * count * (len(arrays) + 1), transcendentals=0),
    )(*arrays, *after)


def turn_sum_kernel(rows, place_ref, a_ref, b_ref, c_ref, d_ref, *refs):
    x = place_ref[2]
    for step, out in enumerate(refs[len(refs) - 4 :]):
        at = pl.ds(pl.multiple_of(lax.rem(x + step, 4) * rows, 16), rows)
        total = (a_ref[at, :].astype(F32) + b_ref[at, :].astype(F32)) + (c_ref[at, :].astype(F32) + d_ref[at, :].astype(F32))
        out[...] = total.astype(BF16)


def turn_sum(place, arrays, after):
    rows = arrays[0].shape[0] // 4
    whole = pl.BlockSpec(memory_space=pltpu.VMEM)
    out = jax.ShapeDtypeStruct((rows, D), BF16)
    return pl.pallas_call(
        partial(turn_sum_kernel, rows),
        in_specs=[pl.BlockSpec(memory_space=pltpu.SMEM)] + [whole] * 4 + [ANY] * len(after),
        out_specs=[whole] * 4,
        out_shape=[out] * 4,
        compiler_params=params(16),
        cost_estimate=pl.CostEstimate(flops=16 * rows * D, bytes_accessed=40 * rows * D, transcendentals=0),
    )(place, *arrays, *after)


def finish_kernel(*refs):
    dk_ref, dv_ref, one, two, three, four = refs[:6]
    outs, mark_ref = refs[-3:-1], refs[-1]
    mark_ref[...] = jnp.zeros_like(mark_ref)
    token, row = iota((256, 128), 0), iota((256, 128), 1)
    spread = jnp.zeros((256, 128), F32)
    start = 0
    for factor, count in ((4, 64), (8, 32), (16, 16), (16, 16)):
        local = row - start
        inside = (local >= 0) & (local < count) & (token >= local * factor) & (token < local * factor + factor)
        spread = jnp.where(inside, 1.0 / factor, spread)
        start = start + count
    spread = spread.astype(BF16)
    for place, (own, out) in enumerate(zip((dk_ref, dv_ref), outs)):
        rows = jnp.concatenate([ref[place] for ref in (one, two, three, four)], 0)
        out[...] = (own[...] + dot_nn(spread, rows)).astype(BF16)


def finish(dk, dv, returned, after):
    half = pl.BlockSpec((256, HD), lambda i: (i, 0))
    shape = jax.ShapeDtypeStruct((ROWS, HD), BF16)
    return pl.pallas_call(
        finish_kernel,
        grid=(2,),
        in_specs=[half] * 2
        + [pl.BlockSpec((2, r.shape[1] // 2, HD), lambda i: (0, i, 0)) for r in returned]
        + [ANY] * len(after),
        out_specs=[half, half, pl.BlockSpec((8, 128), lambda i: (0, 0))],
        out_shape=[shape, shape, MARK],
        compiler_params=params(16),
        cost_estimate=pl.CostEstimate(flops=4 * ROWS * 128 * HD, bytes_accessed=10 * 2**20, transcendentals=0),
    )(dk, dv, *returned, *after)


def x_sum_kernel(place_ref, a_ref, b_ref, c_ref, d_ref, *refs):
    kept, given = refs[len(refs) - 2 :]
    z = place_ref[3]
    for out, half in ((kept, z), (given, 1 - z)):
        at = pl.ds(pl.multiple_of(half * 16, 16), 16)
        total = (a_ref[at, :].astype(F32) + b_ref[at, :].astype(F32)) + (c_ref[at, :].astype(F32) + d_ref[at, :].astype(F32))
        out[...] = total.astype(out.dtype)


def x_sum(place, arrays, after):
    return pl.pallas_call(
        x_sum_kernel,
        in_specs=[pl.BlockSpec(memory_space=pltpu.SMEM)] + [WHOLE] * 4 + [ANY] * len(after),
        out_specs=[WHOLE] * 2,
        out_shape=[jax.ShapeDtypeStruct((16, D), F32), jax.ShapeDtypeStruct((16, D), BF16)],
        compiler_params=params(4),
        cost_estimate=pl.CostEstimate(flops=128 * D, bytes_accessed=10 * 32 * D, transcendentals=0),
    )(place, *arrays, *after)


def z_sum_kernel(place_ref, a_ref, b_ref, kept, given):
    z = place_ref[4]
    total = a_ref[...] + b_ref[...].astype(F32)
    lower, upper = total[:8], total[8:]
    kept[...] = jnp.where(z == 0, lower, upper)
    given[...] = jnp.where(z == 0, upper, lower)


def z_sum(place, kept, received):
    shape = jax.ShapeDtypeStruct((8, D), F32)
    return pl.pallas_call(
        z_sum_kernel,
        in_specs=[pl.BlockSpec(memory_space=pltpu.SMEM)] + [WHOLE] * 2,
        out_specs=[WHOLE] * 2,
        out_shape=[shape, shape],
        compiler_params=params(4),
        cost_estimate=pl.CostEstimate(flops=32 * D, bytes_accessed=160 * D, transcendentals=0),
    )(place, kept, received)


def body(query, key, value, segment_ids, out_weight, cotangent):
    query, key, value = query[0], key[0], value[0]
    cotangent = cotangent[0]
    index = lax.axis_index("ctx")
    other = lax.axis_index("dp")
    core, x = jnp.bitwise_and(index, 1), jnp.right_shift(index, 2)
    z_lo = jnp.bitwise_and(jnp.right_shift(index, 1), 1)
    y, z_hi = jnp.right_shift(other, 1), jnp.bitwise_and(other, 1)
    place = jnp.stack([core, y, x, z_lo, z_hi]).astype(jnp.int32)

    one, two, three, fq, fk = pool(segment_ids, key, value)
    from_z = swap(one, "ctx", 2)
    two, three, mark = lax.optimization_barrier((two, three, pause([three])))
    grad_attention = lax.dot_general(
        cotangent, out_weight, (((1,), (1,)), ((), ())), preferred_element_type=F32
    ).astype(BF16)
    from_x = stack([swap(two, "ctx", 4), swap(three, "ctx", 12), swap(three, "ctx", 8)], [grad_attention, from_z, mark])
    from_xz = swap(from_x, "ctx", 2)
    local_weights, mixed, stats = local_forward(query, key, value, fq, fk, [from_x])
    from_xz, stats = lax.optimization_barrier((from_xz, stats))
    mine = [from_z, from_x, from_xz]
    pieces = mine + [swap(member, "ctx", 1) for member in mine]

    weights, attention, attention_t, rows = coarse_forward(query, grad_attention, fq, mixed, stats, pieces)
    kept, given = grad_weight_part(place, attention_t, cotangent)
    keep, give, partial_q = coarse_backward(query, grad_attention, rows, weights, pieces, [given])
    parts = split_sum([kept, swap(given, "ctx", 1)], 0, (128,) * 4, [keep])
    own_one, own_two, own_xz = split_sum([keep, swap(give, "ctx", 1)], 1, (128, 128, 128), [parts[0]])
    back_xz = swap(own_xz, "ctx", 2)
    back_z = swap(own_one, "ctx", 2)
    grad_query, dk, dv, mark = local_backward(
        query, key, value, grad_attention, rows, local_weights, partial_q, [own_one]
    )
    output, mark = project(attention, out_weight, mark)
    two, three, four = split_sum([own_two, back_xz], 1, (64, 32, 32), [mark])
    returned = [back_z, swap(two, "ctx", 4), swap(three, "ctx", 12), swap(four, "ctx", 8)]
    parts = [parts[0]] + [shift(parts[step], "dp", 2 * step) for step in (1, 2, 3)]
    parts = turn_sum(place, parts, [two])
    grad_key, grad_value, mark = finish(dk, dv, returned, [parts[0]])
    parts = [parts[0]] + [shift(parts[step], "ctx", 4 * step) for step in (1, 2, 3)]
    kept, given = x_sum(place, parts, [mark])
    kept, given = z_sum(place, kept, swap(given, "ctx", 2))
    grad_weight = kept + swap(given, "dp", 1)
    return output[None], grad_query[None], grad_key[None], grad_value[None], grad_weight


def solution(mesh):
    in_specs = (
        P("dp", "ctx", None),
        P("dp", "ctx", None),
        P("dp", "ctx", None),
        P("dp", "ctx"),
        P(),
        P("dp", "ctx", None),
    )
    out_specs = (
        P("dp", "ctx", None),
        P("dp", "ctx", None),
        P("dp", "ctx", None),
        P("dp", "ctx", None),
        P(("ctx", "dp"), None),
    )
    return jax.shard_map(body, mesh=mesh, in_specs=in_specs, out_specs=out_specs, check_vma=False)
```

```python
from functools import partial
import math

import jax
import jax.numpy as jnp
import numpy as np
from jax import lax
from jax.experimental import pallas as pl
from jax.experimental.pallas import tpu as pltpu
from jax.sharding import PartitionSpec as P

HEADS = 8
HEAD_DIM = 128
HD = 1024
D = 2048
ROWS = 512
GROUPS = 1
PER = HEADS // GROUPS
COLS = PER * HEAD_DIM
FACTORS = (4, 8, 16)
COARSE = tuple(ROWS // factor for factor in FACTORS)
SCALE = 1.0 / math.sqrt(HEAD_DIM)
BIG = float(2**30)
F32 = jnp.float32
BF16 = jnp.bfloat16
SMALL = pl.CostEstimate(flops=1024, bytes_accessed=1024, transcendentals=0)


def params(mebibytes):
    return pltpu.CompilerParams(vmem_limit_bytes=mebibytes * 2**20)


def swap(array, axis, bits):
    return lax.ppermute(array, axis, [(i, i ^ bits) for i in range(lax.axis_size(axis))])


def shift(array, axis, step):
    size = lax.axis_size(axis)
    return lax.ppermute(array, axis, [(i, (i + step) % size) for i in range(size)])


def dot_nt(a, b):
    return lax.dot_general(a, b, (((1,), (1,)), ((), ())), preferred_element_type=F32)


def dot_nn(a, b):
    return lax.dot_general(a, b, (((1,), (0,)), ((), ())), preferred_element_type=F32)


def dot_tn(a, b):
    return lax.dot_general(a, b, (((0,), (0,)), ((), ())), preferred_element_type=F32)


def iota(shape, dim):
    return lax.broadcasted_iota(jnp.int32, shape, dim)


def offset_parts(factor):
    rest = math.log(factor) / SCALE
    parts = []
    for _ in range(3):
        part = float(np.asarray(rest, dtype=jnp.bfloat16))
        parts.append(part)
        rest = rest - part
    return parts


def pool_matrix(factor, weight):
    count = ROWS // factor
    row, col = iota((count, ROWS), 0), iota((count, ROWS), 1)
    inside = (col >= row * factor) & (col < row * factor + weight)
    return jnp.where(inside, 1.0 / weight, 0.0).astype(BF16)


def pool_kernel(place_ref, seg_hbm, key_hbm, value_hbm, one, two, three, fq_ref, fk_ref, mark_ref, seg_ref, key_ref, value_ref, sems):
    copies = [
        pltpu.make_async_copy(source, target, sems.at[place])
        for place, (source, target) in enumerate(((seg_hbm, seg_ref), (key_hbm, key_ref), (value_hbm, value_ref)))
    ]
    for copy in copies:
        copy.start()
    mark_ref[...] = jnp.zeros_like(mark_ref)
    outs = (one, two, three)
    starts = np.cumsum((0,) + COARSE)
    pool = jnp.concatenate([pool_matrix(factor, factor) for factor in FACTORS], 0)
    pick = jnp.concatenate([pool_matrix(factor, 1) for factor in FACTORS], 0)
    copies[0].wait()
    seg = seg_ref[...]
    kind = iota((8, ROWS), 0)
    rows = jnp.where(kind < 2, jnp.where(seg == kind, 1.0, 0.0), jnp.where(kind == 2, 1.0, 0.0)).astype(BF16)
    i, j = iota((8, HEAD_DIM), 0), iota((8, HEAD_DIM), 1)
    to_key = jnp.where((i < 2) & (i == j), 1.0, 0.0).astype(BF16)
    wrong = ((i == 0) & (j == 1)) | ((i == 1) & (j == 0))
    ones = (i == 2) & (j >= 2) & (j < 5)
    to_query = jnp.where(wrong, -BIG, jnp.where(ones, 1.0, 0.0)).astype(BF16)
    own = dot_tn(rows, to_key).astype(BF16)
    fk_ref[...] = own
    fq_ref[...] = dot_tn(rows, to_query).astype(BF16)
    picked = dot_nn(pick, own)
    lane = iota((1, HEAD_DIM), 1)
    for place, (factor, out) in enumerate(zip(FACTORS, outs)):
        parts = offset_parts(factor)
        offset = jnp.where(lane == 2, parts[0], jnp.where(lane == 3, parts[1], jnp.where(lane == 4, parts[2], 0.0)))
        out[:, 2 * HD :] = (picked[starts[place] : starts[place + 1]] + offset).astype(BF16)
    for copy, ref, column in zip(copies[1:], (key_ref, value_ref), (0, HD)):
        copy.wait()
        for start in range(0, HD, 256):
            mean = dot_nn(pool, ref[:, start : start + 256])
            for place, out in enumerate(outs):
                out[:, column + start : column + start + 256] = mean[starts[place] : starts[place + 1]].astype(BF16)


WIDTH = 2 * HD + HEAD_DIM
POOL_LIMIT = 52
WHOLE = pl.BlockSpec(memory_space=pltpu.VMEM)
ANY = pl.BlockSpec(memory_space=pl.ANY)
HBM = pl.BlockSpec(memory_space=pltpu.HBM)
MARK = jax.ShapeDtypeStruct((8, 128), F32)


def pool(place, seg, key, value):
    feature = jax.ShapeDtypeStruct((ROWS, HEAD_DIM), BF16)
    token = pltpu.VMEM((ROWS, HD), BF16)
    return pl.pallas_call(
        pool_kernel,
        in_specs=[pl.BlockSpec(memory_space=pltpu.SMEM)] + [HBM] * 3,
        out_specs=[WHOLE] * 6,
        out_shape=[jax.ShapeDtypeStruct((count, WIDTH), BF16) for count in COARSE] + [feature, feature, MARK],
        scratch_shapes=[pltpu.VMEM((1, ROWS), jnp.int32), token, token, pltpu.SemaphoreType.DMA((3,))],
        compiler_params=params(POOL_LIMIT),
        cost_estimate=SMALL,
    )(place, seg, key, value)


def pause_kernel(*refs):
    refs[-1][...] = jnp.zeros_like(refs[-1])


def pause(after):
    return pl.pallas_call(
        pause_kernel,
        in_specs=[ANY] * len(after),
        out_specs=WHOLE,
        out_shape=MARK,
        compiler_params=params(1),
        cost_estimate=SMALL,
    )(*after)


COARSE_ROWS = 768
FIRST = 4
RATE = SCALE * math.log2(math.e)


def columns(h):
    return slice(h * HEAD_DIM, h * HEAD_DIM + HEAD_DIM)


def pair(refs, place, at):
    return jnp.concatenate([refs[2 * place][:, at], refs[2 * place + 1][:, at]], 0)


def joined(total, add):
    return add if total is None else total + add


def each_head(step):
    for h in range(HEADS):
        step(h)


def local_forward_kernel(*refs):
    q_ref, k_ref, v_ref, fq_ref, fk_ref = refs[:5]
    p_ref, mixed_ref, stat_ref, scores = refs[-4:]

    def step(h):
        at = columns(h)
        query = jnp.concatenate([q_ref[:, at], fq_ref[...]], 1)
        top = None
        for start in (0, 256):
            rows = pl.ds(start, 256)
            here = dot_nt(jnp.concatenate([k_ref[rows, at], fk_ref[rows, :]], 1), query) * RATE
            scores[rows, :] = here
            peak = jnp.max(here, 0, keepdims=True)
            top = peak if top is None else jnp.maximum(top, peak)
        total, mixed = None, None
        for start in (0, 256):
            rows = pl.ds(start, 256)
            here = jnp.exp2(scores[rows, :] - top)
            total = joined(total, jnp.sum(here, 0, keepdims=True))
            here = here.astype(BF16)
            p_ref[h, rows, :] = here
            mixed = joined(mixed, dot_tn(v_ref[rows, at], here))
        mixed_ref[at, :] = mixed
        stat_ref[h, 0:1, :] = top
        stat_ref[h, 1:2, :] = total

    each_head(step)


def local_forward(query, key, value, fq, fk, after):
    return pl.pallas_call(
        local_forward_kernel,
        in_specs=[WHOLE] * 5 + [ANY] * len(after),
        out_specs=[WHOLE] * 3,
        out_shape=[
            jax.ShapeDtypeStruct((HEADS, ROWS, ROWS), BF16),
            jax.ShapeDtypeStruct((HD, ROWS), F32),
            jax.ShapeDtypeStruct((HEADS, 8, ROWS), F32),
        ],
        scratch_shapes=[pltpu.VMEM((ROWS, ROWS), F32)],
        compiler_params=params(12),
        cost_estimate=SMALL,
    )(query, key, value, fq, fk, *after)


def coarse_forward_kernel(*refs):
    q_ref, g_ref, fq_ref, mixed_ref, stat_ref = refs[:5]
    pieces = refs[5:11]
    p_ref, o_ref, ot_ref, row_ref, scores = refs[11:]

    def step(h):
        at = columns(h)
        query = jnp.concatenate([q_ref[:, at], fq_ref[...]], 1)
        before, total = stat_ref[h, 0:1, :], stat_ref[h, 1:2, :]
        top = before
        for place in range(3):
            key = jnp.concatenate([pair(pieces, place, at), pair(pieces, place, slice(2 * HD, WIDTH))], 1)
            here = dot_nt(key, query) * RATE
            scores[pl.ds(place * 256, 256), :] = here
            top = jnp.maximum(top, jnp.max(here, 0, keepdims=True))
        factor = jnp.exp2(before - top)
        total, mixed = total * factor, None
        for place in range(3):
            rows = pl.ds(place * 256, 256)
            here = jnp.exp2(scores[rows, :] - top)
            total = total + jnp.sum(here, 0, keepdims=True)
            here = here.astype(BF16)
            p_ref[h, rows, :] = here
            mixed = joined(mixed, dot_tn(pair(pieces, place, columns(HEADS + h)), here))
        inverse = 1.0 / total
        mixed = (mixed + mixed_ref[at, :] * factor) * inverse
        factor = factor * inverse
        ot_ref[at, :] = mixed.astype(BF16)
        o_ref[:, at] = mixed.T.astype(BF16)
        row_ref[h, 0:1, :] = jnp.sum(g_ref[:, at].astype(F32).T * mixed, 0, keepdims=True)
        row_ref[h, 1:2, :] = factor
        row_ref[h, 2:3, :] = inverse

    each_head(step)


def coarse_forward(query, grad, fq, mixed, stats, pieces):
    return pl.pallas_call(
        coarse_forward_kernel,
        in_specs=[WHOLE] * 11,
        out_specs=[WHOLE] * 4,
        out_shape=[
            jax.ShapeDtypeStruct((HEADS, COARSE_ROWS, ROWS), BF16),
            jax.ShapeDtypeStruct((ROWS, HD), BF16),
            jax.ShapeDtypeStruct((HD, ROWS), BF16),
            jax.ShapeDtypeStruct((HEADS, 8, ROWS), F32),
        ],
        scratch_shapes=[pltpu.VMEM((COARSE_ROWS, ROWS), F32)],
        compiler_params=params(12),
        cost_estimate=SMALL,
    )(query, grad, fq, mixed, stats, *pieces)


def scaled(grad, factor):
    grad = grad.astype(F32).T * factor
    return grad.astype(BF16), grad.T.astype(BF16)


def coarse_backward_kernel(heads, *refs):
    q_ref, g_ref, row_ref, p_ref = refs[:4]
    pieces = refs[4:10]
    keep_ref, give_ref, dq_ref, mark_ref = refs[-4:]
    mark_ref[...] = jnp.zeros_like(mark_ref)
    for h in heads:
        at, to = columns(h), columns(h - heads[0])
        q = q_ref[:, at]
        delta, factor = row_ref[h, 0:1, :], row_ref[h, 2:3, :]
        across, g = scaled(g_ref[:, at], factor)
        delta = delta * factor
        grad_q = None
        for place in range(3):
            weight = p_ref[h, pl.ds(place * 256, 256), :]
            key, value = pair(pieces, place, at), pair(pieces, place, columns(HEADS + h))
            slope = (weight.astype(F32) * (dot_nn(value, across) - delta)).astype(BF16)
            grads = ((dot_nn(slope, q) * SCALE).astype(BF16), dot_nn(weight, g).astype(BF16))
            for side, grad in enumerate(grads):
                for half in range(2):
                    piece = 2 * place + half
                    out, row = (keep_ref, piece * 128) if piece < 3 else (give_ref, (piece - 3) * 128)
                    out[side, pl.ds(row, 128), to] = grad[half * 128 : half * 128 + 128]
            grad_q = joined(grad_q, dot_tn(key, slope))
        dq_ref[to, :] = grad_q


def coarse_backward(query, grad, rows, weights, pieces, heads, after):
    width = len(heads) * HEAD_DIM
    return pl.pallas_call(
        partial(coarse_backward_kernel, heads),
        in_specs=[WHOLE] * 10 + [ANY] * len(after),
        out_specs=[WHOLE] * 4,
        out_shape=[
            jax.ShapeDtypeStruct((2, 384, width), BF16),
            jax.ShapeDtypeStruct((2, 384, width), BF16),
            jax.ShapeDtypeStruct((width, ROWS), F32),
            MARK,
        ],
        compiler_params=params(12),
        cost_estimate=SMALL,
    )(query, grad, rows, weights, *pieces, *after)


def local_backward_kernel(*refs):
    q_ref, k_ref, v_ref, g_ref, row_ref, p_ref, part_refs = *refs[:6], refs[6:8]
    dq_ref, dk_ref, dv_ref, mark_ref = refs[-4:]
    mark_ref[...] = jnp.zeros_like(mark_ref)

    def step(h):
        at = columns(h)
        q = q_ref[:, at]
        delta, factor = row_ref[h, 0:1, :], row_ref[h, 1:2, :]
        across, g = scaled(g_ref[:, at], factor)
        delta = delta * factor
        grad_q = part_refs[0][at, :] if h < FIRST else part_refs[1][columns(h - FIRST), :]
        for start in (0, 256):
            rows = pl.ds(start, 256)
            weight = p_ref[h, rows, :]
            slope = (weight.astype(F32) * (dot_nn(v_ref[rows, at], across) - delta)).astype(BF16)
            dk_ref[rows, at] = (dot_nn(slope, q) * SCALE).astype(BF16)
            dv_ref[rows, at] = dot_nn(weight, g).astype(BF16)
            grad_q = grad_q + dot_tn(k_ref[rows, at], slope)
        dq_ref[:, at] = (grad_q * SCALE).T.astype(BF16)

    each_head(step)


def local_backward(query, key, value, grad, rows, weights, partials, after):
    return pl.pallas_call(
        local_backward_kernel,
        in_specs=[WHOLE] * 8 + [ANY] * len(after),
        out_specs=[WHOLE] * 4,
        out_shape=[
            jax.ShapeDtypeStruct((ROWS, HD), BF16),
            jax.ShapeDtypeStruct((ROWS, HD), BF16),
            jax.ShapeDtypeStruct((ROWS, HD), BF16),
            MARK,
        ],
        compiler_params=params(12),
        cost_estimate=SMALL,
    )(query, key, value, grad, rows, weights, *partials, *after)


def grad_attention_kernel(c_ref, w_ref, out_ref):
    for start in range(0, HD, 256):
        out_ref[:, start : start + 256] = dot_nt(c_ref[...], w_ref[start : start + 256, :]).astype(BF16)


def grad_attention_of(cotangent, weight):
    return pl.pallas_call(
        grad_attention_kernel,
        in_specs=[WHOLE] * 2,
        out_specs=WHOLE,
        out_shape=jax.ShapeDtypeStruct((ROWS, HD), BF16),
        compiler_params=params(8),
        cost_estimate=SMALL,
    )(cotangent, weight)


def project_kernel(a_ref, w_ref, _, out_ref, mark_ref):
    mark_ref[...] = jnp.zeros_like(mark_ref)
    for start in range(0, D, 512):
        out_ref[:, start : start + 512] = dot_nn(a_ref[...], w_ref[:, start : start + 512]).astype(BF16)


def project(attention, weight, after):
    return pl.pallas_call(
        project_kernel,
        in_specs=[WHOLE] * 2 + [ANY],
        out_specs=[WHOLE] * 2,
        out_shape=[jax.ShapeDtypeStruct((ROWS, D), BF16), MARK],
        compiler_params=params(8),
        cost_estimate=SMALL,
    )(attention, weight, after)


def stack_kernel(count, *refs):
    out, start = refs[-1], 0
    for ref in refs[:count]:
        out[pl.ds(start, ref.shape[0]), :] = ref[...]
        start = start + ref.shape[0]


def stack(arrays, after):
    rows, width = sum(array.shape[0] for array in arrays), arrays[0].shape[1]
    return pl.pallas_call(
        partial(stack_kernel, len(arrays)),
        in_specs=[WHOLE] * len(arrays) + [ANY] * len(after),
        out_specs=WHOLE,
        out_shape=jax.ShapeDtypeStruct((rows, width), BF16),
        compiler_params=params(4),
        cost_estimate=SMALL,
    )(*arrays, *after)


def grad_weight_kernel(place_ref, ot_ref, c_ref, keep_ref, give_ref, mark_ref, lhs):
    mark_ref[...] = jnp.zeros_like(mark_ref)
    core, y = place_ref[0], place_ref[1]
    for slot in range(2):
        half = core if slot == 0 else 1 - core
        for step in range(4):
            target = lax.rem(y + step, 4)
            for j in range(HEADS):
                source = pl.multiple_of(j * 128 + half * 64 + target * 16, 16)
                row = ((slot * 4 + step) * HEADS + j) * 16
                lhs[row : row + 16, :] = ot_ref[pl.ds(source, 16), :]
    for out, row in ((give_ref, HD // 2), (keep_ref, 0)):
        for start in range(0, D, 512):
            at = slice(start, start + 512)
            out[:, at] = dot_nn(lhs[row : row + HD // 2, :], c_ref[:, at]).astype(BF16)


def grad_weight_part(place, ot, cotangent):
    shape = jax.ShapeDtypeStruct((HD // 2, D), BF16)
    return pl.pallas_call(
        grad_weight_kernel,
        in_specs=[pl.BlockSpec(memory_space=pltpu.SMEM)] + [WHOLE] * 2,
        out_specs=[WHOLE] * 3,
        out_shape=[shape, shape, MARK],
        scratch_shapes=[pltpu.VMEM((HD, ROWS), BF16)],
        compiler_params=params(8),
        cost_estimate=SMALL,
    )(place, ot, cotangent)


def split_sum_kernel(count, axis, bounds, *refs):
    ins, outs = refs[:count], refs[len(refs) - len(bounds) :]
    for (start, size), out in zip(bounds, outs):
        at = (slice(None),) * axis + (pl.ds(start, size),)
        total = ins[0][at].astype(F32)
        for ref in ins[1:]:
            total = total + ref[at].astype(F32)
        out[...] = total.astype(out.dtype)


def split_sum(arrays, axis, sizes, after=()):
    shape = arrays[0].shape
    starts = np.cumsum([0] + list(sizes))
    bounds = [(int(start), int(size)) for start, size in zip(starts, sizes)]
    whole = pl.BlockSpec(memory_space=pltpu.VMEM)
    outs = [jax.ShapeDtypeStruct(shape[:axis] + (size,) + shape[axis + 1 :], BF16) for size in sizes]
    count = math.prod(shape)
    return pl.pallas_call(
        partial(split_sum_kernel, len(arrays), axis, bounds),
        in_specs=[whole] * len(arrays) + [ANY] * len(after),
        out_specs=[whole] * len(sizes),
        out_shape=outs,
        compiler_params=params(16),
        cost_estimate=SMALL,
    )(*arrays, *after)


def add_all(refs, at):
    terms = [ref[at].astype(F32) for ref in refs]
    return (terms[0] + terms[1]) + (terms[2] + terms[3])


def relay_kernel(one_ref, three_ref, lower_ref, upper_ref, *refs):
    up, down = refs[len(refs) - 2 :]
    up[:64, :] = (one_ref[:64, :].astype(F32) + lower_ref[...].astype(F32)).astype(BF16)
    up[64:, :] = one_ref[64:, :]
    down[:64, :] = three_ref[:64, :]
    down[64:, :] = (three_ref[64:, :].astype(F32) + upper_ref[...].astype(F32)).astype(BF16)


def relay(arrays, after):
    return pl.pallas_call(
        relay_kernel,
        in_specs=[WHOLE] * 4 + [ANY] * len(after),
        out_specs=[WHOLE] * 2,
        out_shape=[jax.ShapeDtypeStruct((128, D), BF16)] * 2,
        compiler_params=params(8),
        cost_estimate=SMALL,
    )(*arrays, *after)


def y_sum_kernel(place_ref, *refs):
    for step, out in enumerate(refs[len(refs) - 4 :]):
        at = pl.ds(pl.multiple_of(lax.rem(place_ref[2] + step, 4) * 32, 32), 32)
        out[...] = (refs[0][at, :].astype(F32) + refs[1][at, :].astype(F32) + refs[2][at, :].astype(F32)).astype(BF16)


def y_sum(place, arrays, after):
    return pl.pallas_call(
        y_sum_kernel,
        in_specs=[pl.BlockSpec(memory_space=pltpu.SMEM)] + [WHOLE] * 3 + [ANY] * len(after),
        out_specs=[WHOLE] * 4,
        out_shape=[jax.ShapeDtypeStruct((32, D), BF16)] * 4,
        compiler_params=params(8),
        cost_estimate=SMALL,
    )(place, *arrays, *after)


def back_sum_kernel(*refs):
    outs = refs[len(refs) - 3 :]
    column = 0
    for keep, received in ((refs[0], refs[1]), (refs[2], refs[3])):
        width = keep.shape[2]
        for place, out in enumerate(outs):
            at = (slice(None), slice(place * 128, place * 128 + 128), slice(None))
            total = keep[at].astype(F32) + received[at].astype(F32)
            out[:, :, column : column + width] = total.astype(BF16)
        column = column + width


def back_sum(arrays, after):
    return pl.pallas_call(
        back_sum_kernel,
        in_specs=[WHOLE] * 4 + [ANY] * len(after),
        out_specs=[WHOLE] * 3,
        out_shape=[jax.ShapeDtypeStruct((2, 128, HD), BF16)] * 3,
        compiler_params=params(8),
        cost_estimate=SMALL,
    )(*arrays, *after)


def second_sum_kernel(own_ref, received_ref, *refs):
    near, far = refs[len(refs) - 2 :]

    def rows(start, stop):
        return (own_ref[:, start:stop, :].astype(F32) + received_ref[:, start:stop, :].astype(F32)).astype(BF16)

    near[:, :64, :] = rows(0, 64)
    near[:, 64:, :] = rows(96, 128)
    far[...] = rows(64, 96)


def second_sum(own, received, after):
    return pl.pallas_call(
        second_sum_kernel,
        in_specs=[WHOLE] * 2 + [ANY] * len(after),
        out_specs=[WHOLE] * 2,
        out_shape=[jax.ShapeDtypeStruct((2, 96, HD), BF16), jax.ShapeDtypeStruct((2, 32, HD), BF16)],
        compiler_params=params(8),
        cost_estimate=SMALL,
    )(own, received, *after)


def third_sum_kernel(far_ref, near_ref, *refs):
    refs[-1][...] = (far_ref[...].astype(F32) + near_ref[:, 64:, :].astype(F32)).astype(BF16)


def third_sum(far, near, after):
    return pl.pallas_call(
        third_sum_kernel,
        in_specs=[WHOLE] * 2 + [ANY] * len(after),
        out_specs=WHOLE,
        out_shape=jax.ShapeDtypeStruct((2, 32, HD), BF16),
        compiler_params=params(8),
        cost_estimate=SMALL,
    )(far, near, *after)


def finish_kernel(*refs):
    dk_ref, dv_ref, one, two, three = refs[:5]
    outs, mark_ref = refs[-3:-1], refs[-1]
    mark_ref[...] = jnp.zeros_like(mark_ref)
    token, row = iota((256, 128), 0), iota((256, 128), 1)
    spread = jnp.zeros((256, 128), F32)
    start = 0
    for factor, count in ((4, 64), (8, 32), (16, 16)):
        local = row - start
        inside = (local >= 0) & (local < count) & (token >= local * factor) & (token < local * factor + factor)
        spread = jnp.where(inside, 1.0 / factor, spread)
        start = start + count
    spread = spread.astype(BF16)
    for place, (own, out) in enumerate(zip((dk_ref, dv_ref), outs)):
        rows = jnp.concatenate([one[place], two[place], three[place], jnp.zeros((16, HD), BF16)], 0)
        out[...] = (own[...].astype(F32) + dot_nn(spread, rows)).astype(BF16)


def finish(dk, dv, one, two, three, after):
    half = pl.BlockSpec((256, HD), lambda i: (i, 0))
    shape = jax.ShapeDtypeStruct((ROWS, HD), BF16)
    coarse = [pl.BlockSpec((2, rows, HD), lambda i: (0, i, 0)) for rows in (64, 32, 16)]
    return pl.pallas_call(
        finish_kernel,
        grid=(2,),
        in_specs=[half] * 2 + coarse + [ANY] * len(after),
        out_specs=[half, half, pl.BlockSpec((8, 128), lambda i: (0, 0))],
        out_shape=[shape, shape, MARK],
        compiler_params=params(16),
        cost_estimate=SMALL,
    )(dk, dv, one, two, three, *after)


def add_all(refs, at):
    terms = [ref[at].astype(F32) for ref in refs]
    return (terms[0] + terms[1]) + (terms[2] + terms[3])


def last_sum_kernel(place_ref, *refs):
    outs = refs[len(refs) - 4 :]
    z_lo, z_hi = place_ref[3], place_ref[4]
    sums = add_all(refs[:4], slice(None))
    for lo in range(2):
        for hi in range(2):
            rows = sums[lo * 16 + hi * 8 : lo * 16 + hi * 8 + 8]
            for place, out in enumerate(outs):

                @pl.when((lax.rem(z_lo + place % 2, 2) == lo) & (lax.rem(z_hi + place // 2, 2) == hi))
                def _():
                    out[...] = rows


def last_sum(place, arrays, after):
    return pl.pallas_call(
        last_sum_kernel,
        in_specs=[pl.BlockSpec(memory_space=pltpu.SMEM)] + [WHOLE] * 4 + [ANY] * len(after),
        out_specs=[WHOLE] * 4,
        out_shape=[jax.ShapeDtypeStruct((8, D), F32)] * 4,
        compiler_params=params(4),
        cost_estimate=SMALL,
    )(place, *arrays, *after)


def total_kernel(*refs):
    refs[-1][...] = add_all(refs[:4], slice(None))


def total(arrays, after):
    return pl.pallas_call(
        total_kernel,
        in_specs=[WHOLE] * 4 + [ANY] * len(after),
        out_specs=WHOLE,
        out_shape=jax.ShapeDtypeStruct((8, D), F32),
        compiler_params=params(4),
        cost_estimate=SMALL,
    )(*arrays, *after)


def body(query, key, value, segment_ids, out_weight, cotangent):
    query, key, value = query[0], key[0], value[0]
    cotangent = cotangent[0]
    index = lax.axis_index("ctx")
    other = lax.axis_index("dp")
    core, x = jnp.bitwise_and(index, 1), jnp.right_shift(index, 2)
    z_lo = jnp.bitwise_and(jnp.right_shift(index, 1), 1)
    y, z_hi = jnp.right_shift(other, 1), jnp.bitwise_and(other, 1)
    place = jnp.stack([core, y, x, z_lo, z_hi]).astype(jnp.int32)

    one, two, three, fq, fk, mark = pool(place, segment_ids, key, value)
    from_z = swap(one, "ctx", 2)
    two, three, mark = lax.optimization_barrier((two, three, pause([mark])))
    grad_attention = grad_attention_of(cotangent, out_weight)
    from_x = stack([swap(two, "ctx", 4), swap(three, "ctx", 12), swap(three, "ctx", 8)], [grad_attention, pause([from_z]), mark])
    from_xz = swap(from_x, "ctx", 2)
    local_weights, mixed, stats = local_forward(query, key, value, fq, fk, [from_x])
    from_xz, stats = lax.optimization_barrier((from_xz, stats))
    mine = [from_z, from_x, from_xz]
    pieces = mine + [swap(member, "ctx", 1) for member in mine]

    weights, attention, attention_t, rows = coarse_forward(query, grad_attention, fq, mixed, stats, pieces)
    kept, given, mark = grad_weight_part(place, attention_t, cotangent)
    one = coarse_backward(query, grad_attention, rows, weights, pieces, range(FIRST), [mark])
    parts = split_sum([kept, swap(given, "ctx", 1)], 0, (128, 128, 64, 64, 128), [one[3]])
    lower, upper = shift(parts[2], "dp", 2), shift(parts[3], "dp", -2)
    rest = coarse_backward(query, grad_attention, rows, weights, pieces, range(FIRST, HEADS), [parts[0]])
    grad_query, dk, dv, mark = local_backward(
        query, key, value, grad_attention, rows, local_weights, [one[2], rest[2]], [rest[3]]
    )
    up, down = relay([parts[1], parts[4], lower, upper], [mark])
    own_one, own_two, own_xz = back_sum([one[0], swap(one[1], "ctx", 1), rest[0], swap(rest[1], "ctx", 1)], [up])
    back_xz = swap(own_xz, "ctx", 2)
    back_z = swap(own_one, "ctx", 2)
    output, mark = project(attention, out_weight, own_one)
    near, far = second_sum(own_two, back_xz, [mark])
    near = swap(near, "ctx", 4)
    parts = y_sum(place, [parts[0], shift(up, "dp", 2), shift(down, "dp", -2)], [far])
    far = third_sum(far, near, [parts[0]])
    parts = [parts[0]] + [shift(parts[step], "ctx", 4 * step) for step in (1, 2, 3)]
    parts = last_sum(place, parts, [far])
    grad_key, grad_value, mark = finish(dk, dv, back_z, near, swap(far, "ctx", 12), [parts[0]])
    count = lax.axis_size("dp")
    both = [(i, (i // count ^ 2) * count + (i % count ^ 1)) for i in range(lax.axis_size("ctx") * count)]
    grad_weight = total(
        [parts[0], swap(parts[1], "ctx", 2), swap(parts[2], "dp", 1), lax.ppermute(parts[3], ("ctx", "dp"), both)],
        [mark],
    )
    return output[None], grad_query[None], grad_key[None], grad_value[None], grad_weight


def solution(mesh):
    in_specs = (
        P("dp", "ctx", None),
        P("dp", "ctx", None),
        P("dp", "ctx", None),
        P("dp", "ctx"),
        P(),
        P("dp", "ctx", None),
    )
    out_specs = (
        P("dp", "ctx", None),
        P("dp", "ctx", None),
        P("dp", "ctx", None),
        P("dp", "ctx", None),
        P(("ctx", "dp"), None),
    )
    return jax.shard_map(body, mesh=mesh, in_specs=in_specs, out_specs=out_specs, check_vma=False)
```

```python
from functools import partial
import math

import jax
import jax.numpy as jnp
import numpy as np
from jax import lax
from jax.experimental import pallas as pl
from jax.experimental.pallas import tpu as pltpu
from jax.sharding import PartitionSpec as P

HEADS = 8
HEAD_DIM = 128
HD = 1024
D = 2048
ROWS = 512
GROUPS = 1
PER = HEADS // GROUPS
COLS = PER * HEAD_DIM
FACTORS = (4, 8, 16)
COARSE = tuple(ROWS // factor for factor in FACTORS)
SCALE = 1.0 / math.sqrt(HEAD_DIM)
BIG = float(2**30)
F32 = jnp.float32
BF16 = jnp.bfloat16
SMALL = pl.CostEstimate(flops=1024, bytes_accessed=1024, transcendentals=0)


def params(mebibytes):
    return pltpu.CompilerParams(vmem_limit_bytes=mebibytes * 2**20)


def swap(array, axis, bits):
    return lax.ppermute(array, axis, [(i, i ^ bits) for i in range(lax.axis_size(axis))])


def shift(array, axis, step):
    size = lax.axis_size(axis)
    return lax.ppermute(array, axis, [(i, (i + step) % size) for i in range(size)])


def dot_nt(a, b):
    return lax.dot_general(a, b, (((1,), (1,)), ((), ())), preferred_element_type=F32)


def dot_nn(a, b):
    return lax.dot_general(a, b, (((1,), (0,)), ((), ())), preferred_element_type=F32)


def dot_tn(a, b):
    return lax.dot_general(a, b, (((0,), (0,)), ((), ())), preferred_element_type=F32)


def iota(shape, dim):
    return lax.broadcasted_iota(jnp.int32, shape, dim)


def offset_parts(factor):
    rest = math.log(factor) / SCALE
    parts = []
    for _ in range(3):
        part = float(np.asarray(rest, dtype=jnp.bfloat16))
        parts.append(part)
        rest = rest - part
    return parts


def pool_matrix(factor, weight):
    count = ROWS // factor
    row, col = iota((count, ROWS), 0), iota((count, ROWS), 1)
    inside = (col >= row * factor) & (col < row * factor + weight)
    return jnp.where(inside, 1.0 / weight, 0.0).astype(BF16)


def pool_kernel(place_ref, seg_hbm, key_hbm, value_hbm, one, two, three, fq_ref, fk_ref, mark_ref, seg_ref, key_ref, value_ref, sems):
    copies = [
        pltpu.make_async_copy(source, target, sems.at[place])
        for place, (source, target) in enumerate(((seg_hbm, seg_ref), (key_hbm, key_ref), (value_hbm, value_ref)))
    ]
    for copy in copies:
        copy.start()
    mark_ref[...] = jnp.zeros_like(mark_ref)
    outs = (one, two, three)
    starts = np.cumsum((0,) + COARSE)
    pool = jnp.concatenate([pool_matrix(factor, factor) for factor in FACTORS], 0)
    pick = jnp.concatenate([pool_matrix(factor, 1) for factor in FACTORS], 0)
    copies[0].wait()
    seg = seg_ref[...]
    kind = iota((8, ROWS), 0)
    rows = jnp.where(kind < 2, jnp.where(seg == kind, 1.0, 0.0), jnp.where(kind == 2, 1.0, 0.0)).astype(BF16)
    i, j = iota((8, HEAD_DIM), 0), iota((8, HEAD_DIM), 1)
    to_key = jnp.where((i < 2) & (i == j), 1.0, 0.0).astype(BF16)
    wrong = ((i == 0) & (j == 1)) | ((i == 1) & (j == 0))
    ones = (i == 2) & (j >= 2) & (j < 5)
    to_query = jnp.where(wrong, -BIG, jnp.where(ones, 1.0, 0.0)).astype(BF16)
    own = dot_tn(rows, to_key).astype(BF16)
    fk_ref[...] = own
    fq_ref[...] = dot_tn(rows, to_query).astype(BF16)
    picked = dot_nn(pick, own)
    lane = iota((1, HEAD_DIM), 1)
    for place, (factor, out) in enumerate(zip(FACTORS, outs)):
        parts = offset_parts(factor)
        offset = jnp.where(lane == 2, parts[0], jnp.where(lane == 3, parts[1], jnp.where(lane == 4, parts[2], 0.0)))
        out[:, 2 * HD :] = (picked[starts[place] : starts[place + 1]] + offset).astype(BF16)
    for copy, ref, column in zip(copies[1:], (key_ref, value_ref), (0, HD)):
        copy.wait()
        for start in range(0, HD, 256):
            mean = dot_nn(pool, ref[:, start : start + 256])
            for place, out in enumerate(outs):
                out[:, column + start : column + start + 256] = mean[starts[place] : starts[place + 1]].astype(BF16)


WIDTH = 2 * HD + HEAD_DIM
POOL_LIMIT = 52
WHOLE = pl.BlockSpec(memory_space=pltpu.VMEM)
ANY = pl.BlockSpec(memory_space=pl.ANY)
HBM = pl.BlockSpec(memory_space=pltpu.HBM)
MARK = jax.ShapeDtypeStruct((8, 128), F32)


def pool(place, seg, key, value):
    feature = jax.ShapeDtypeStruct((ROWS, HEAD_DIM), BF16)
    token = pltpu.VMEM((ROWS, HD), BF16)
    return pl.pallas_call(
        pool_kernel,
        in_specs=[pl.BlockSpec(memory_space=pltpu.SMEM)] + [HBM] * 3,
        out_specs=[WHOLE] * 6,
        out_shape=[jax.ShapeDtypeStruct((count, WIDTH), BF16) for count in COARSE] + [feature, feature, MARK],
        scratch_shapes=[pltpu.VMEM((1, ROWS), jnp.int32), token, token, pltpu.SemaphoreType.DMA((3,))],
        compiler_params=params(POOL_LIMIT),
        cost_estimate=SMALL,
    )(place, seg, key, value)


def pause_kernel(*refs):
    refs[-1][...] = jnp.zeros_like(refs[-1])


def pause(after):
    return pl.pallas_call(
        pause_kernel,
        in_specs=[ANY] * len(after),
        out_specs=WHOLE,
        out_shape=MARK,
        compiler_params=params(1),
        cost_estimate=SMALL,
    )(*after)


COARSE_ROWS = 768
FIRST = 7
RATE = SCALE * math.log2(math.e)


def columns(h):
    if isinstance(h, int):
        return slice(h * HEAD_DIM, h * HEAD_DIM + HEAD_DIM)
    return pl.ds(pl.multiple_of(h * HEAD_DIM, HEAD_DIM), HEAD_DIM)


def pair(refs, place, at):
    return jnp.concatenate([refs[2 * place][:, at], refs[2 * place + 1][:, at]], 0)


def joined(total, add):
    return add if total is None else total + add


def each_head(step, heads, unroll):
    if unroll == len(heads):
        for h in heads:
            step(h)
    else:
        lax.fori_loop(heads[0], heads[-1] + 1, lambda h, carry: (step(h), carry)[1], 0, unroll=unroll)


EARLY = 1024
LATE = 256


def early_forward_kernel(*refs):
    q_ref, k_ref, v_ref, fq_ref, fk_ref = refs[:5]
    pieces = refs[5:9]
    p_ref, mixed_ref, stat_ref, scores = refs[-4:]

    def step(h):
        at, beside = columns(h), columns(HEADS + h)
        query = jnp.concatenate([q_ref[:, at], fq_ref[...]], 1)
        top = None
        for place in range(4):
            rows = pl.ds(place * 256, 256)
            if place < 2:
                key = jnp.concatenate([k_ref[rows, at], fk_ref[rows, :]], 1)
            else:
                key = jnp.concatenate([pair(pieces, place - 2, at), pair(pieces, place - 2, slice(2 * HD, WIDTH))], 1)
            here = dot_nt(key, query) * RATE
            scores[rows, :] = here
            peak = jnp.max(here, 0, keepdims=True)
            top = peak if top is None else jnp.maximum(top, peak)
        total, mixed = None, None
        for place in range(4):
            rows = pl.ds(place * 256, 256)
            here = jnp.exp2(scores[rows, :] - top)
            total = joined(total, jnp.sum(here, 0, keepdims=True))
            here = here.astype(BF16)
            p_ref[h, rows, :] = here
            value = v_ref[rows, at] if place < 2 else pair(pieces, place - 2, beside)
            mixed = joined(mixed, dot_tn(value, here))
        mixed_ref[at, :] = mixed
        stat_ref[h, 0:1, :] = top
        stat_ref[h, 1:2, :] = total

    each_head(step, range(HEADS), 2)


def early_forward(query, key, value, fq, fk, pieces, after):
    return pl.pallas_call(
        early_forward_kernel,
        in_specs=[WHOLE] * 9 + [ANY] * len(after),
        out_specs=[WHOLE] * 3,
        out_shape=[
            jax.ShapeDtypeStruct((HEADS, EARLY, ROWS), BF16),
            jax.ShapeDtypeStruct((HD, ROWS), F32),
            jax.ShapeDtypeStruct((HEADS, 8, ROWS), F32),
        ],
        scratch_shapes=[pltpu.VMEM((EARLY, ROWS), F32)],
        compiler_params=params(12),
        cost_estimate=SMALL,
    )(query, key, value, fq, fk, *pieces, *after)


def late_forward_kernel(*refs):
    q_ref, across_ref, fq_ref, mixed_ref, stat_ref = refs[:5]
    pieces = refs[5:7]
    p_ref, ot_ref, row_ref = refs[7:]

    feature = pair(pieces, 0, slice(2 * HD, WIDTH))
    scores = []
    for h in range(HEADS):
        query = jnp.concatenate([q_ref[:, columns(h)], fq_ref[...]], 1)
        scores.append(dot_nt(jnp.concatenate([pair(pieces, 0, columns(h)), feature], 1), query) * RATE)
    for h in range(HEADS):
        before, total = stat_ref[h, 0:1, :], stat_ref[h, 1:2, :]
        top = jnp.maximum(before, jnp.max(scores[h], 0, keepdims=True))
        factor = jnp.exp2(before - top)
        here = jnp.exp2(scores[h] - top)
        inverse = 1.0 / (total * factor + jnp.sum(here, 0, keepdims=True))
        row_ref[h, 1:2, :] = factor * inverse
        p_ref[h] = (here * inverse).astype(BF16)
    for h in range(HEADS):
        at = columns(h)
        mixed = dot_tn(pair(pieces, 0, columns(HEADS + h)), p_ref[h]) + mixed_ref[at, :] * row_ref[h, 1:2, :]
        ot_ref[at, :] = mixed.astype(BF16)
        row_ref[h, 0:1, :] = jnp.sum(across_ref[at, :].astype(F32) * mixed, 0, keepdims=True)


def late_forward(query, across, fq, mixed, stats, pieces):
    return pl.pallas_call(
        late_forward_kernel,
        in_specs=[WHOLE] * 7,
        out_specs=[WHOLE] * 3,
        out_shape=[
            jax.ShapeDtypeStruct((HEADS, LATE, ROWS), BF16),
            jax.ShapeDtypeStruct((HD, ROWS), BF16),
            jax.ShapeDtypeStruct((HEADS, 8, ROWS), F32),
        ],
        compiler_params=params(12),
        cost_estimate=SMALL,
    )(query, across, fq, mixed, stats, *pieces)


def scaled(across, factor):
    across = (across.astype(F32) * factor).astype(BF16)
    return across, across.T


def coarse_backward_kernel(heads, *refs):
    q_ref, g_ref, across_ref, row_ref, early_ref, late_ref = refs[:6]
    pieces = refs[6:12]
    keep_ref, give_ref, dq_ref, mark_ref = refs[-4:]
    mark_ref[...] = jnp.zeros_like(mark_ref)

    def step(h):
        at, to = columns(h), columns(h - heads[0])
        q, g = q_ref[:, at], g_ref[:, at]
        delta, factor = row_ref[h, 0:1, :], row_ref[h, 1:2, :]
        across, scaled_g = scaled(across_ref[at, :], factor)
        scaled_delta = delta * factor
        grad_q = None
        for place in range(3):
            key, value = pair(pieces, place, at), pair(pieces, place, columns(HEADS + h))
            if place < 2:
                weight = early_ref[h, pl.ds(512 + place * 256, 256), :]
                slope = dot_nn(value, across) - scaled_delta
                grad_v = dot_nn(weight, scaled_g)
            else:
                weight = late_ref[h]
                slope = dot_nn(value, across_ref[at, :]) - delta
                grad_v = dot_nn(weight, g)
            slope = (weight.astype(F32) * slope).astype(BF16)
            grads = ((dot_nn(slope, q) * SCALE).astype(BF16), grad_v.astype(BF16))
            for side, grad in enumerate(grads):
                for half in range(2):
                    out, row = ((keep_ref, give_ref)[half], place * 128) if place == 2 else ((keep_ref, give_ref)[place], half * 128)
                    out[side, pl.ds(row, 128), to] = grad[half * 128 : half * 128 + 128]
            grad_q = joined(grad_q, dot_tn(key, slope))
        dq_ref[to, :] = grad_q

    each_head(step, heads, len(heads))


def coarse_backward(query, grad, across, rows, early, late, pieces, heads, after):
    width = len(heads) * HEAD_DIM
    return pl.pallas_call(
        partial(coarse_backward_kernel, heads),
        in_specs=[WHOLE] * 12 + [ANY] * len(after),
        out_specs=[WHOLE] * 4,
        out_shape=[
            jax.ShapeDtypeStruct((2, 384, width), BF16),
            jax.ShapeDtypeStruct((2, 384, width), BF16),
            jax.ShapeDtypeStruct((width, ROWS), F32),
            MARK,
        ],
        compiler_params=params(12),
        cost_estimate=SMALL,
    )(query, grad, across, rows, early, late, *pieces, *after)


def local_backward_kernel(heads, parts, before, *refs):
    q_ref, k_ref, v_ref, across_ref, row_ref, p_ref = refs[:6]
    part_refs = refs[6 : 6 + len(parts)]
    dq_ref, dk_ref, dv_ref, mark_ref = refs[-4:]
    mark_ref[...] = jnp.zeros_like(mark_ref)
    for ref, out in zip(refs[6 + len(parts) : 6 + len(parts) + before], (dq_ref, dk_ref, dv_ref)):
        out[:, : heads[0] * HEAD_DIM] = ref[...]

    def step(part, first, h):
        at = columns(h)
        q = q_ref[:, at]
        delta, factor = row_ref[h, 0:1, :], row_ref[h, 1:2, :]
        across, g = scaled(across_ref[at, :], factor)
        delta = delta * factor
        grad_q = part[columns(h - first), :]
        for start in (0, 256):
            rows = pl.ds(start, 256)
            weight = p_ref[h, rows, :]
            slope = (weight.astype(F32) * (dot_nn(v_ref[rows, at], across) - delta)).astype(BF16)
            dk_ref[rows, at] = (dot_nn(slope, q) * SCALE).astype(BF16)
            dv_ref[rows, at] = dot_nn(weight, g).astype(BF16)
            grad_q = grad_q + dot_tn(k_ref[rows, at], slope)
        dq_ref[:, at] = (grad_q * SCALE).astype(BF16).T

    for part, (first, last) in zip(part_refs, parts):
        inside = [h for h in heads if first <= h < last]
        each_head(partial(step, part, first), inside, len(inside))


def local_backward(query, key, value, across, rows, weights, partials, heads, earlier, after):
    partials = [part for part in partials if part[0] <= heads[-1] and heads[0] < part[1]]
    token = jax.ShapeDtypeStruct((ROWS, (heads[-1] + 1) * HEAD_DIM), BF16)
    return pl.pallas_call(
        partial(local_backward_kernel, heads, [part[:2] for part in partials], len(earlier)),
        in_specs=[WHOLE] * (6 + len(partials) + len(earlier)) + [ANY] * len(after),
        out_specs=[WHOLE] * 4,
        out_shape=[token, token, token, MARK],
        compiler_params=params(12),
        cost_estimate=SMALL,
    )(query, key, value, across, rows, weights, *[part[2] for part in partials], *earlier, *after)


def grad_attention_kernel(c_ref, w_ref, out_ref, across_ref):
    for start in range(0, HD, 256):
        out = dot_nt(c_ref[...], w_ref[start : start + 256, :]).astype(BF16)
        out_ref[:, start : start + 256] = out
        across_ref[start : start + 256, :] = out.T


def grad_attention_of(cotangent, weight):
    return pl.pallas_call(
        grad_attention_kernel,
        in_specs=[WHOLE] * 2,
        out_specs=[WHOLE] * 2,
        out_shape=[jax.ShapeDtypeStruct((ROWS, HD), BF16), jax.ShapeDtypeStruct((HD, ROWS), BF16)],
        compiler_params=params(8),
        cost_estimate=SMALL,
    )(cotangent, weight)


def project_kernel(a_ref, w_ref, _, out_ref, mark_ref):
    mark_ref[...] = jnp.zeros_like(mark_ref)
    for start in range(0, D, 512):
        out_ref[:, start : start + 512] = dot_tn(a_ref[...], w_ref[:, start : start + 512]).astype(BF16)


def project(attention, weight, after):
    return pl.pallas_call(
        project_kernel,
        in_specs=[WHOLE] * 2 + [ANY],
        out_specs=[WHOLE] * 2,
        out_shape=[jax.ShapeDtypeStruct((ROWS, D), BF16), MARK],
        compiler_params=params(8),
        cost_estimate=SMALL,
    )(attention, weight, after)


def stack_kernel(count, *refs):
    out, start = refs[-1], 0
    for ref in refs[:count]:
        out[pl.ds(start, ref.shape[0]), :] = ref[...]
        start = start + ref.shape[0]


def stack(arrays, after):
    rows, width = sum(array.shape[0] for array in arrays), arrays[0].shape[1]
    return pl.pallas_call(
        partial(stack_kernel, len(arrays)),
        in_specs=[WHOLE] * len(arrays) + [ANY] * len(after),
        out_specs=WHOLE,
        out_shape=jax.ShapeDtypeStruct((rows, width), BF16),
        compiler_params=params(4),
        cost_estimate=SMALL,
    )(*arrays, *after)


def grad_weight_kernel(place_ref, ot_ref, c_ref, keep_ref, give_ref, mark_ref, lhs):
    mark_ref[...] = jnp.zeros_like(mark_ref)
    core, y = place_ref[0], place_ref[1]
    for slot in range(2):
        half = core if slot == 0 else 1 - core
        for step in range(4):
            target = lax.rem(y + step, 4)
            for j in range(HEADS):
                source = pl.multiple_of(j * 128 + half * 64 + target * 16, 16)
                row = ((slot * 4 + step) * HEADS + j) * 16
                lhs[row : row + 16, :] = ot_ref[pl.ds(source, 16), :]
    for out, row in ((give_ref, HD // 2), (keep_ref, 0)):
        for start in range(0, D, 512):
            at = slice(start, start + 512)
            out[:, at] = dot_nn(lhs[row : row + HD // 2, :], c_ref[:, at]).astype(BF16)


def grad_weight_part(place, ot, cotangent):
    shape = jax.ShapeDtypeStruct((HD // 2, D), BF16)
    return pl.pallas_call(
        grad_weight_kernel,
        in_specs=[pl.BlockSpec(memory_space=pltpu.SMEM)] + [WHOLE] * 2,
        out_specs=[WHOLE] * 3,
        out_shape=[shape, shape, MARK],
        scratch_shapes=[pltpu.VMEM((HD, ROWS), BF16)],
        compiler_params=params(8),
        cost_estimate=SMALL,
    )(place, ot, cotangent)


def split_sum_kernel(count, axis, bounds, *refs):
    ins, outs = refs[:count], refs[len(refs) - len(bounds) :]
    for (start, size), out in zip(bounds, outs):
        at = (slice(None),) * axis + (pl.ds(start, size),)
        total = ins[0][at].astype(F32)
        for ref in ins[1:]:
            total = total + ref[at].astype(F32)
        out[...] = total.astype(out.dtype)


def split_sum(arrays, axis, sizes, after=()):
    shape = arrays[0].shape
    starts = np.cumsum([0] + list(sizes))
    bounds = [(int(start), int(size)) for start, size in zip(starts, sizes)]
    whole = pl.BlockSpec(memory_space=pltpu.VMEM)
    outs = [jax.ShapeDtypeStruct(shape[:axis] + (size,) + shape[axis + 1 :], BF16) for size in sizes]
    count = math.prod(shape)
    return pl.pallas_call(
        partial(split_sum_kernel, len(arrays), axis, bounds),
        in_specs=[whole] * len(arrays) + [ANY] * len(after),
        out_specs=[whole] * len(sizes),
        out_shape=outs,
        compiler_params=params(16),
        cost_estimate=SMALL,
    )(*arrays, *after)


def add_all(refs, at):
    terms = [ref[at].astype(F32) for ref in refs]
    return (terms[0] + terms[1]) + (terms[2] + terms[3])


def relay_kernel(one_ref, three_ref, lower_ref, upper_ref, *refs):
    up, down = refs[len(refs) - 2 :]
    up[:64, :] = (one_ref[:64, :].astype(F32) + lower_ref[...].astype(F32)).astype(BF16)
    up[64:, :] = one_ref[64:, :]
    down[:64, :] = three_ref[:64, :]
    down[64:, :] = (three_ref[64:, :].astype(F32) + upper_ref[...].astype(F32)).astype(BF16)


def relay(arrays, after):
    return pl.pallas_call(
        relay_kernel,
        in_specs=[WHOLE] * 4 + [ANY] * len(after),
        out_specs=[WHOLE] * 2,
        out_shape=[jax.ShapeDtypeStruct((128, D), BF16)] * 2,
        compiler_params=params(8),
        cost_estimate=SMALL,
    )(*arrays, *after)


def y_sum_kernel(place_ref, *refs):
    for step, out in enumerate(refs[len(refs) - 4 :]):
        at = pl.ds(pl.multiple_of(lax.rem(place_ref[2] + step, 4) * 32, 32), 32)
        out[...] = (refs[0][at, :].astype(F32) + refs[1][at, :].astype(F32) + refs[2][at, :].astype(F32)).astype(BF16)


def y_sum(place, arrays, after):
    return pl.pallas_call(
        y_sum_kernel,
        in_specs=[pl.BlockSpec(memory_space=pltpu.SMEM)] + [WHOLE] * 3 + [ANY] * len(after),
        out_specs=[WHOLE] * 4,
        out_shape=[jax.ShapeDtypeStruct((32, D), BF16)] * 4,
        compiler_params=params(8),
        cost_estimate=SMALL,
    )(place, *arrays, *after)


def back_sum_kernel(*refs):
    outs = refs[len(refs) - 3 :]
    column = 0
    for keep, received in ((refs[0], refs[1]), (refs[2], refs[3])):
        width = keep.shape[2]
        for place, out in enumerate(outs):
            at = (slice(None), slice(place * 128, place * 128 + 128), slice(None))
            total = keep[at].astype(F32) + received[at].astype(F32)
            out[:, :, column : column + width] = total.astype(BF16)
        column = column + width


def back_sum(arrays, after):
    return pl.pallas_call(
        back_sum_kernel,
        in_specs=[WHOLE] * 4 + [ANY] * len(after),
        out_specs=[WHOLE] * 3,
        out_shape=[jax.ShapeDtypeStruct((2, 128, HD), BF16)] * 3,
        compiler_params=params(8),
        cost_estimate=SMALL,
    )(*arrays, *after)


def second_sum_kernel(own_ref, received_ref, *refs):
    near, far = refs[len(refs) - 2 :]

    def rows(start, stop):
        return (own_ref[:, start:stop, :].astype(F32) + received_ref[:, start:stop, :].astype(F32)).astype(BF16)

    near[:, :64, :] = rows(0, 64)
    near[:, 64:, :] = rows(96, 128)
    far[...] = rows(64, 96)


def second_sum(own, received, after):
    return pl.pallas_call(
        second_sum_kernel,
        in_specs=[WHOLE] * 2 + [ANY] * len(after),
        out_specs=[WHOLE] * 2,
        out_shape=[jax.ShapeDtypeStruct((2, 96, HD), BF16), jax.ShapeDtypeStruct((2, 32, HD), BF16)],
        compiler_params=params(8),
        cost_estimate=SMALL,
    )(own, received, *after)


def third_sum_kernel(far_ref, near_ref, *refs):
    refs[-1][...] = (far_ref[...].astype(F32) + near_ref[:, 64:, :].astype(F32)).astype(BF16)


def third_sum(far, near, after):
    return pl.pallas_call(
        third_sum_kernel,
        in_specs=[WHOLE] * 2 + [ANY] * len(after),
        out_specs=WHOLE,
        out_shape=jax.ShapeDtypeStruct((2, 32, HD), BF16),
        compiler_params=params(8),
        cost_estimate=SMALL,
    )(far, near, *after)


def finish_kernel(*refs):
    dk_ref, dv_ref, one, two, three = refs[:5]
    outs, mark_ref = refs[-3:-1], refs[-1]
    mark_ref[...] = jnp.zeros_like(mark_ref)
    token, row = iota((256, 128), 0), iota((256, 128), 1)
    spread = jnp.zeros((256, 128), F32)
    start = 0
    for factor, count in ((4, 64), (8, 32), (16, 16)):
        local = row - start
        inside = (local >= 0) & (local < count) & (token >= local * factor) & (token < local * factor + factor)
        spread = jnp.where(inside, 1.0 / factor, spread)
        start = start + count
    spread = spread.astype(BF16)
    for place, (own, out) in enumerate(zip((dk_ref, dv_ref), outs)):
        rows = jnp.concatenate([one[place], two[place], three[place], jnp.zeros((16, HD), BF16)], 0)
        out[...] = (own[...].astype(F32) + dot_nn(spread, rows)).astype(BF16)


def finish(dk, dv, one, two, three, after):
    half = pl.BlockSpec((256, HD), lambda i: (i, 0))
    shape = jax.ShapeDtypeStruct((ROWS, HD), BF16)
    coarse = [pl.BlockSpec((2, rows, HD), lambda i: (0, i, 0)) for rows in (64, 32, 16)]
    return pl.pallas_call(
        finish_kernel,
        grid=(2,),
        in_specs=[half] * 2 + coarse + [ANY] * len(after),
        out_specs=[half, half, pl.BlockSpec((8, 128), lambda i: (0, 0))],
        out_shape=[shape, shape, MARK],
        compiler_params=params(16),
        cost_estimate=SMALL,
    )(dk, dv, one, two, three, *after)


def add_all(refs, at):
    terms = [ref[at].astype(F32) for ref in refs]
    return (terms[0] + terms[1]) + (terms[2] + terms[3])


def last_sum_kernel(place_ref, *refs):
    outs = refs[len(refs) - 4 :]
    z_lo, z_hi = place_ref[3], place_ref[4]
    sums = add_all(refs[:4], slice(None))
    for lo in range(2):
        for hi in range(2):
            rows = sums[lo * 16 + hi * 8 : lo * 16 + hi * 8 + 8]
            for place, out in enumerate(outs):

                @pl.when((lax.rem(z_lo + place % 2, 2) == lo) & (lax.rem(z_hi + place // 2, 2) == hi))
                def _():
                    out[...] = rows


def last_sum(place, arrays, after):
    return pl.pallas_call(
        last_sum_kernel,
        in_specs=[pl.BlockSpec(memory_space=pltpu.SMEM)] + [WHOLE] * 4 + [ANY] * len(after),
        out_specs=[WHOLE] * 4,
        out_shape=[jax.ShapeDtypeStruct((8, D), F32)] * 4,
        compiler_params=params(4),
        cost_estimate=SMALL,
    )(place, *arrays, *after)


def total_kernel(*refs):
    refs[-1][...] = add_all(refs[:4], slice(None))


def total(arrays, after):
    return pl.pallas_call(
        total_kernel,
        in_specs=[WHOLE] * 4 + [ANY] * len(after),
        out_specs=WHOLE,
        out_shape=jax.ShapeDtypeStruct((8, D), F32),
        compiler_params=params(4),
        cost_estimate=SMALL,
    )(*arrays, *after)


def body(query, key, value, segment_ids, out_weight, cotangent):
    query, key, value = query[0], key[0], value[0]
    cotangent = cotangent[0]
    index = lax.axis_index("ctx")
    other = lax.axis_index("dp")
    core, x = jnp.bitwise_and(index, 1), jnp.right_shift(index, 2)
    z_lo = jnp.bitwise_and(jnp.right_shift(index, 1), 1)
    y, z_hi = jnp.right_shift(other, 1), jnp.bitwise_and(other, 1)
    place = jnp.stack([core, y, x, z_lo, z_hi]).astype(jnp.int32)

    one, two, three, fq, fk, mark = pool(place, segment_ids, key, value)
    from_z = swap(one, "ctx", 2)
    two, three, mark = lax.optimization_barrier((two, three, pause([mark])))
    grad_attention, grad_across = grad_attention_of(cotangent, out_weight)
    from_x = stack([swap(two, "ctx", 4), swap(three, "ctx", 12), swap(three, "ctx", 8)], [grad_attention, mark])
    from_xz = swap(from_x, "ctx", 2)
    sooner = [from_z, from_x, swap(from_z, "ctx", 1), swap(from_x, "ctx", 1)]
    early, mixed, stats = early_forward(query, key, value, fq, fk, sooner, [])
    from_xz, stats = lax.optimization_barrier((from_xz, stats))
    later = [from_xz, swap(from_xz, "ctx", 1)]
    pieces = sooner + later

    late, attention, rows = late_forward(query, grad_across, fq, mixed, stats, later)
    kept, given, mark = grad_weight_part(place, attention, cotangent)
    one = coarse_backward(query, grad_attention, grad_across, rows, early, late, pieces, range(FIRST), [mark])
    parts = split_sum([kept, swap(given, "ctx", 1)], 0, (128, 128, 64, 64, 128), [one[3]])
    lower, upper = shift(parts[2], "dp", 2), shift(parts[3], "dp", -2)
    rest = coarse_backward(query, grad_attention, grad_across, rows, early, late, pieces, range(FIRST, HEADS), [parts[0]])
    own_one, own_two, own_xz = back_sum([one[0], swap(one[1], "ctx", 1), rest[0], swap(rest[1], "ctx", 1)], [])
    back_xz = swap(own_xz, "ctx", 2)
    back_z = swap(own_one, "ctx", 2)
    partials = [(0, FIRST, one[2]), (FIRST, HEADS, rest[2])]
    *earlier, mark = local_backward(
        query, key, value, grad_across, rows, early, partials, range(4), (), [own_one]
    )
    up, down = relay([parts[1], parts[4], lower, upper], [mark])
    near, far = second_sum(own_two, back_xz, [up])
    near = swap(near, "ctx", 4)
    grad_query, dk, dv, mark = local_backward(
        query, key, value, grad_across, rows, early, partials, range(4, HEADS), earlier, [far]
    )
    output, mark = project(attention, out_weight, mark)
    parts = y_sum(place, [parts[0], shift(up, "dp", 2), shift(down, "dp", -2)], [mark])
    far = third_sum(far, near, [parts[0]])
    parts = [parts[0]] + [shift(parts[step], "ctx", 4 * step) for step in (1, 2, 3)]
    parts = last_sum(place, parts, [far])
    grad_key, grad_value, mark = finish(dk, dv, back_z, near, swap(far, "ctx", 12), [parts[0]])
    count = lax.axis_size("dp")
    both = [(i, (i // count ^ 2) * count + (i % count ^ 1)) for i in range(lax.axis_size("ctx") * count)]
    grad_weight = total(
        [parts[0], swap(parts[1], "ctx", 2), swap(parts[2], "dp", 1), lax.ppermute(parts[3], ("ctx", "dp"), both)],
        [mark],
    )
    return output[None], grad_query[None], grad_key[None], grad_value[None], grad_weight


def solution(mesh):
    in_specs = (
        P("dp", "ctx", None),
        P("dp", "ctx", None),
        P("dp", "ctx", None),
        P("dp", "ctx"),
        P(),
        P("dp", "ctx", None),
    )
    out_specs = (
        P("dp", "ctx", None),
        P("dp", "ctx", None),
        P("dp", "ctx", None),
        P("dp", "ctx", None),
        P(("ctx", "dp"), None),
    )
    return jax.shard_map(body, mesh=mesh, in_specs=in_specs, out_specs=out_specs, check_vma=False)
```

```python
from functools import partial
import math

import jax
import jax.numpy as jnp
import numpy as np
from jax import lax
from jax.experimental import pallas as pl
from jax.experimental.pallas import tpu as pltpu
from jax.sharding import PartitionSpec as P

HEADS = 8
HEAD_DIM = 128
HD = 1024
D = 2048
ROWS = 512
GROUPS = 1
PER = HEADS // GROUPS
COLS = PER * HEAD_DIM
FACTORS = (4, 8, 16)
COARSE = tuple(ROWS // factor for factor in FACTORS)
SCALE = 1.0 / math.sqrt(HEAD_DIM)
BIG = float(2**30)
F32 = jnp.float32
BF16 = jnp.bfloat16
LARGE = pl.CostEstimate(flops=2 * 10**10, bytes_accessed=1024, transcendentals=0)
SMALL = pl.CostEstimate(flops=1024, bytes_accessed=1024, transcendentals=0)


def params(mebibytes):
    return pltpu.CompilerParams(vmem_limit_bytes=int(mebibytes * 2**20))


def swap(array, axis, bits):
    return lax.ppermute(array, axis, [(i, i ^ bits) for i in range(lax.axis_size(axis))])


def shift(array, axis, step):
    size = lax.axis_size(axis)
    return lax.ppermute(array, axis, [(i, (i + step) % size) for i in range(size)])


def position(place_ref):
    place = place_ref[0]
    return place >> 5, (place >> 4) & 1, (place >> 3) & 1, (place >> 1) & 3, place & 1


def dot_nt(a, b):
    return lax.dot_general(a, b, (((1,), (1,)), ((), ())), preferred_element_type=F32)


def dot_nn(a, b):
    return lax.dot_general(a, b, (((1,), (0,)), ((), ())), preferred_element_type=F32)


def dot_tn(a, b):
    return lax.dot_general(a, b, (((0,), (0,)), ((), ())), preferred_element_type=F32)


def iota(shape, dim):
    return lax.broadcasted_iota(jnp.int32, shape, dim)


def offset_parts(factor):
    rest = math.log(factor) / SCALE
    parts = []
    for _ in range(3):
        part = float(np.asarray(rest, dtype=jnp.bfloat16))
        parts.append(part)
        rest = rest - part
    return parts


def pool_matrix(factor, weight):
    count = ROWS // factor
    row, col = iota((count, ROWS), 0), iota((count, ROWS), 1)
    inside = (col >= row * factor) & (col < row * factor + weight)
    return jnp.where(inside, 1.0 / weight, 0.0).astype(BF16)


def pool_kernel(place_ref, seg_hbm, key_hbm, value_hbm, one, two, three, fq_ref, fk_ref, mark_ref, seg_ref, key_ref, value_ref, sems):
    copies = [
        pltpu.make_async_copy(source, target, sems.at[place])
        for place, (source, target) in enumerate(((seg_hbm, seg_ref), (key_hbm, key_ref), (value_hbm, value_ref)))
    ]
    for copy in copies:
        copy.start()
    mark_ref[...] = jnp.zeros_like(mark_ref)
    outs = (one, two, three)
    starts = np.cumsum((0,) + COARSE)
    pool = jnp.concatenate([pool_matrix(factor, factor) for factor in FACTORS], 0)
    pick = jnp.concatenate([pool_matrix(factor, 1) for factor in FACTORS], 0)
    copies[0].wait()
    seg = seg_ref[...]
    kind = iota((8, ROWS), 0)
    rows = jnp.where(kind < 2, jnp.where(seg == kind, 1.0, 0.0), jnp.where(kind == 2, 1.0, 0.0)).astype(BF16)
    i, j = iota((8, HEAD_DIM), 0), iota((8, HEAD_DIM), 1)
    to_key = jnp.where((i < 2) & (i == j), 1.0, 0.0).astype(BF16)
    wrong = ((i == 0) & (j == 1)) | ((i == 1) & (j == 0))
    ones = (i == 2) & (j >= 2) & (j < 5)
    to_query = jnp.where(wrong, -BIG, jnp.where(ones, 1.0, 0.0)).astype(BF16)
    own = dot_tn(rows, to_key).astype(BF16)
    fk_ref[...] = own
    fq_ref[...] = dot_tn(rows, to_query).astype(BF16)
    picked = dot_nn(pick, own)
    lane = iota((1, HEAD_DIM), 1)
    for place, (factor, out) in enumerate(zip(FACTORS, outs)):
        parts = offset_parts(factor)
        offset = jnp.where(lane == 2, parts[0], jnp.where(lane == 3, parts[1], jnp.where(lane == 4, parts[2], 0.0)))
        out[:, 2 * HD :] = (picked[starts[place] : starts[place + 1]] + offset).astype(BF16)
    for copy, ref, column in zip(copies[1:], (key_ref, value_ref), (0, HD)):
        copy.wait()
        for start in range(0, HD, 256):
            mean = dot_nn(pool, ref[:, start : start + 256])
            for place, out in enumerate(outs):
                out[:, column + start : column + start + 256] = mean[starts[place] : starts[place + 1]].astype(BF16)


WIDTH = 2 * HD + HEAD_DIM
POOL_LIMIT = 52
WHOLE = pl.BlockSpec(memory_space=pltpu.VMEM)
ANY = pl.BlockSpec(memory_space=pl.ANY)
HBM = pl.BlockSpec(memory_space=pltpu.HBM)
MARK = jax.ShapeDtypeStruct((8, 128), F32)


def pool(place, seg, key, value):
    feature = jax.ShapeDtypeStruct((ROWS, HEAD_DIM), BF16)
    token = pltpu.VMEM((ROWS, HD), BF16)
    return pl.pallas_call(
        pool_kernel,
        in_specs=[pl.BlockSpec(memory_space=pltpu.SMEM)] + [HBM] * 3,
        out_specs=[WHOLE] * 6,
        out_shape=[jax.ShapeDtypeStruct((count, WIDTH), BF16) for count in COARSE] + [feature, feature, MARK],
        scratch_shapes=[pltpu.VMEM((1, ROWS), jnp.int32), token, token, pltpu.SemaphoreType.DMA((3,))],
        compiler_params=params(POOL_LIMIT),
        cost_estimate=SMALL,
    )(place, seg, key, value)


def pause_kernel(*refs):
    refs[-1][...] = jnp.zeros_like(refs[-1])


def pause(after):
    return pl.pallas_call(
        pause_kernel,
        in_specs=[ANY] * len(after),
        out_specs=WHOLE,
        out_shape=MARK,
        compiler_params=params(1),
        cost_estimate=SMALL,
    )(*after)


COARSE_ROWS = 768
FIRST = 7
RATE = SCALE * math.log2(math.e)


def columns(h):
    if isinstance(h, int):
        return slice(h * HEAD_DIM, h * HEAD_DIM + HEAD_DIM)
    return pl.ds(pl.multiple_of(h * HEAD_DIM, HEAD_DIM), HEAD_DIM)


def pair(refs, place, at):
    return jnp.concatenate([refs[2 * place][:, at], refs[2 * place + 1][:, at]], 0)


def joined(total, add):
    return add if total is None else total + add


def each_head(step, heads, unroll):
    if unroll == len(heads):
        for h in heads:
            step(h)
    else:
        lax.fori_loop(heads[0], heads[-1] + 1, lambda h, carry: (step(h), carry)[1], 0, unroll=unroll)


EARLY = 1024
LATE = 256


def early_forward_kernel(*refs):
    q_ref, k_ref, v_ref, fq_ref, fk_ref = refs[:5]
    pieces = refs[5:9]
    p_ref, mixed_ref, stat_ref, scores = refs[-4:]

    def step(h):
        at, beside = columns(h), columns(HEADS + h)
        query = jnp.concatenate([q_ref[:, at], fq_ref[...]], 1)
        top = None
        for place in range(4):
            rows = pl.ds(place * 256, 256)
            if place < 2:
                key = jnp.concatenate([k_ref[rows, at], fk_ref[rows, :]], 1)
            else:
                key = jnp.concatenate([pair(pieces, place - 2, at), pair(pieces, place - 2, slice(2 * HD, WIDTH))], 1)
            here = dot_nt(key, query) * RATE
            scores[rows, :] = here
            peak = jnp.max(here, 0, keepdims=True)
            top = peak if top is None else jnp.maximum(top, peak)
        total, mixed = None, None
        for place in range(4):
            rows = pl.ds(place * 256, 256)
            here = jnp.exp2(scores[rows, :] - top)
            total = joined(total, jnp.sum(here, 0, keepdims=True))
            here = here.astype(BF16)
            p_ref[h, rows, :] = here
            value = v_ref[rows, at] if place < 2 else pair(pieces, place - 2, beside)
            mixed = joined(mixed, dot_tn(value, here))
        mixed_ref[at, :] = mixed
        stat_ref[h, 0:1, :] = top
        stat_ref[h, 1:2, :] = total

    each_head(step, range(HEADS), 2)


def early_forward(query, key, value, fq, fk, pieces, after):
    return pl.pallas_call(
        early_forward_kernel,
        in_specs=[WHOLE] * 9 + [ANY] * len(after),
        out_specs=[WHOLE] * 3,
        out_shape=[
            jax.ShapeDtypeStruct((HEADS, EARLY, ROWS), BF16),
            jax.ShapeDtypeStruct((HD, ROWS), F32),
            jax.ShapeDtypeStruct((HEADS, 8, ROWS), F32),
        ],
        scratch_shapes=[pltpu.VMEM((EARLY, ROWS), F32)],
        compiler_params=params(12),
        cost_estimate=SMALL,
    )(query, key, value, fq, fk, *pieces, *after)


def late_forward_kernel(*refs):
    q_ref, across_ref, fq_ref, mixed_ref, stat_ref = refs[:5]
    pieces = refs[5:7]
    p_ref, ot_ref, row_ref = refs[7:]

    feature = pair(pieces, 0, slice(2 * HD, WIDTH))
    scores = []
    for h in range(HEADS):
        query = jnp.concatenate([q_ref[:, columns(h)], fq_ref[...]], 1)
        scores.append(dot_nt(jnp.concatenate([pair(pieces, 0, columns(h)), feature], 1), query) * RATE)
    for h in range(HEADS):
        before, total = stat_ref[h, 0:1, :], stat_ref[h, 1:2, :]
        top = jnp.maximum(before, jnp.max(scores[h], 0, keepdims=True))
        factor = jnp.exp2(before - top)
        here = jnp.exp2(scores[h] - top)
        inverse = 1.0 / (total * factor + jnp.sum(here, 0, keepdims=True))
        row_ref[h, 1:2, :] = factor * inverse
        p_ref[h] = (here * inverse).astype(BF16)
    for h in range(HEADS):
        at = columns(h)
        mixed = dot_tn(pair(pieces, 0, columns(HEADS + h)), p_ref[h]) + mixed_ref[at, :] * row_ref[h, 1:2, :]
        ot_ref[at, :] = mixed.astype(BF16)
        row_ref[h, 0:1, :] = jnp.sum(across_ref[at, :].astype(F32) * mixed, 0, keepdims=True)


def late_forward(query, across, fq, mixed, stats, pieces):
    return pl.pallas_call(
        late_forward_kernel,
        in_specs=[WHOLE] * 7,
        out_specs=[WHOLE] * 3,
        out_shape=[
            jax.ShapeDtypeStruct((HEADS, LATE, ROWS), BF16),
            jax.ShapeDtypeStruct((HD, ROWS), BF16),
            jax.ShapeDtypeStruct((HEADS, 8, ROWS), F32),
        ],
        compiler_params=params(12),
        cost_estimate=SMALL,
    )(query, across, fq, mixed, stats, *pieces)


def scaled(across, factor):
    across = (across.astype(F32) * factor).astype(BF16)
    return across, across.T


def coarse_backward_kernel(heads, *refs):
    q_ref, g_ref, across_ref, row_ref, early_ref, late_ref = refs[:6]
    pieces = refs[6:12]
    keep_ref, give_ref, dq_ref, mark_ref = refs[-4:]
    mark_ref[...] = jnp.zeros_like(mark_ref)

    def step(h):
        at, to = columns(h), columns(h - heads[0])
        q, g = q_ref[:, at], g_ref[:, at]
        delta, factor = row_ref[h, 0:1, :], row_ref[h, 1:2, :]
        across, scaled_g = scaled(across_ref[at, :], factor)
        scaled_delta = delta * factor
        grad_q = None
        for place in range(3):
            key, value = pair(pieces, place, at), pair(pieces, place, columns(HEADS + h))
            if place < 2:
                weight = early_ref[h, pl.ds(512 + place * 256, 256), :]
                slope = dot_nn(value, across) - scaled_delta
                grad_v = dot_nn(weight, scaled_g)
            else:
                weight = late_ref[h]
                slope = dot_nn(value, across_ref[at, :]) - delta
                grad_v = dot_nn(weight, g)
            slope = (weight.astype(F32) * slope).astype(BF16)
            grads = ((dot_nn(slope, q) * SCALE).astype(BF16), grad_v.astype(BF16))
            for side, grad in enumerate(grads):
                for half in range(2):
                    out, row = ((keep_ref, give_ref)[half], place * 128) if place == 2 else ((keep_ref, give_ref)[place], half * 128)
                    out[side, pl.ds(row, 128), to] = grad[half * 128 : half * 128 + 128]
            grad_q = joined(grad_q, dot_tn(key, slope))
        dq_ref[to, :] = grad_q

    each_head(step, heads, len(heads))


def coarse_backward(query, grad, across, rows, early, late, pieces, heads, after):
    width = len(heads) * HEAD_DIM
    return pl.pallas_call(
        partial(coarse_backward_kernel, heads),
        in_specs=[WHOLE] * 12 + [ANY] * len(after),
        out_specs=[WHOLE] * 4,
        out_shape=[
            jax.ShapeDtypeStruct((2, 384, width), BF16),
            jax.ShapeDtypeStruct((2, 384, width), BF16),
            jax.ShapeDtypeStruct((width, ROWS), F32),
            MARK,
        ],
        compiler_params=params(12),
        cost_estimate=SMALL,
    )(query, grad, across, rows, early, late, *pieces, *after)


def local_backward_kernel(heads, parts, before, *refs):
    q_ref, k_ref, v_ref, across_ref, row_ref, p_ref = refs[:6]
    part_refs = refs[6 : 6 + len(parts)]
    dq_ref, dk_ref, dv_ref, mark_ref = refs[-4:]
    mark_ref[...] = jnp.zeros_like(mark_ref)
    for ref, out in zip(refs[6 + len(parts) : 6 + len(parts) + before], (dq_ref, dk_ref, dv_ref)):
        out[:, : heads[0] * HEAD_DIM] = ref[...]

    def step(part, first, h):
        at = columns(h)
        q = q_ref[:, at]
        delta, factor = row_ref[h, 0:1, :], row_ref[h, 1:2, :]
        across, g = scaled(across_ref[at, :], factor)
        delta = delta * factor
        grad_q = part[columns(h - first), :]
        for start in (0, 256):
            rows = pl.ds(start, 256)
            weight = p_ref[h, rows, :]
            slope = (weight.astype(F32) * (dot_nn(v_ref[rows, at], across) - delta)).astype(BF16)
            dk_ref[rows, at] = (dot_nn(slope, q) * SCALE).astype(BF16)
            dv_ref[rows, at] = dot_nn(weight, g).astype(BF16)
            grad_q = grad_q + dot_tn(k_ref[rows, at], slope)
        dq_ref[:, at] = (grad_q * SCALE).astype(BF16).T

    for part, (first, last) in zip(part_refs, parts):
        inside = [h for h in heads if first <= h < last]
        each_head(partial(step, part, first), inside, len(inside))


def local_backward(query, key, value, across, rows, weights, partials, heads, earlier, after):
    partials = [part for part in partials if part[0] <= heads[-1] and heads[0] < part[1]]
    token = jax.ShapeDtypeStruct((ROWS, (heads[-1] + 1) * HEAD_DIM), BF16)
    return pl.pallas_call(
        partial(local_backward_kernel, heads, [part[:2] for part in partials], len(earlier)),
        in_specs=[WHOLE] * (6 + len(partials) + len(earlier)) + [ANY] * len(after),
        out_specs=[WHOLE] * 4,
        out_shape=[token, token, token, MARK],
        compiler_params=params(12),
        cost_estimate=SMALL,
    )(query, key, value, across, rows, weights, *[part[2] for part in partials], *earlier, *after)


def grad_attention_kernel(c_ref, w_ref, out_ref, across_ref):
    for start in range(0, HD, 256):
        out = dot_nt(c_ref[...], w_ref[start : start + 256, :]).astype(BF16)
        out_ref[:, start : start + 256] = out
        across_ref[start : start + 256, :] = out.T


def grad_attention_of(cotangent, weight):
    return pl.pallas_call(
        grad_attention_kernel,
        in_specs=[WHOLE] * 2,
        out_specs=[WHOLE] * 2,
        out_shape=[jax.ShapeDtypeStruct((ROWS, HD), BF16), jax.ShapeDtypeStruct((HD, ROWS), BF16)],
        compiler_params=params(8),
        cost_estimate=SMALL,
    )(cotangent, weight)


def project_kernel(a_ref, w_ref, _, out_ref, mark_ref):
    mark_ref[...] = jnp.zeros_like(mark_ref)
    for start in range(0, D, 512):
        out_ref[:, start : start + 512] = dot_tn(a_ref[...], w_ref[:, start : start + 512]).astype(BF16)


def project(attention, weight, after):
    return pl.pallas_call(
        project_kernel,
        in_specs=[WHOLE] * 2 + [ANY],
        out_specs=[WHOLE] * 2,
        out_shape=[jax.ShapeDtypeStruct((ROWS, D), BF16), MARK],
        compiler_params=params(8),
        cost_estimate=LARGE,
    )(attention, weight, after)


def stack_kernel(count, *refs):
    out, start = refs[-1], 0
    for ref in refs[:count]:
        out[pl.ds(start, ref.shape[0]), :] = ref[...]
        start = start + ref.shape[0]


def stack(arrays, after):
    rows, width = sum(array.shape[0] for array in arrays), arrays[0].shape[1]
    return pl.pallas_call(
        partial(stack_kernel, len(arrays)),
        in_specs=[WHOLE] * len(arrays) + [ANY] * len(after),
        out_specs=WHOLE,
        out_shape=jax.ShapeDtypeStruct((rows, width), BF16),
        compiler_params=params(4),
        cost_estimate=SMALL,
    )(*arrays, *after)


def grad_weight_kernel(place_ref, ot_ref, c_ref, keep_ref, give_ref, mark_ref, lhs):
    mark_ref[...] = jnp.zeros_like(mark_ref)
    _, _, core, y, _ = position(place_ref)
    for slot in range(2):
        half = core if slot == 0 else 1 - core
        for step in range(4):
            target = lax.rem(y + step, 4)
            for j in range(HEADS):
                source = pl.multiple_of(j * 128 + half * 64 + target * 16, 16)
                row = ((slot * 4 + step) * HEADS + j) * 16
                lhs[row : row + 16, :] = ot_ref[pl.ds(source, 16), :]
    for out, row in ((give_ref, HD // 2), (keep_ref, 0)):
        for start in range(0, D, 512):
            at = slice(start, start + 512)
            out[:, at] = dot_nn(lhs[row : row + HD // 2, :], c_ref[:, at]).astype(BF16)


def grad_weight_part(place, ot, cotangent):
    shape = jax.ShapeDtypeStruct((HD // 2, D), BF16)
    return pl.pallas_call(
        grad_weight_kernel,
        in_specs=[pl.BlockSpec(memory_space=pltpu.SMEM)] + [WHOLE] * 2,
        out_specs=[WHOLE] * 3,
        out_shape=[shape, shape, MARK],
        scratch_shapes=[pltpu.VMEM((HD, ROWS), BF16)],
        compiler_params=params(8),
        cost_estimate=SMALL,
    )(place, ot, cotangent)


def split_sum_kernel(count, axis, bounds, *refs):
    ins, outs = refs[:count], refs[len(refs) - len(bounds) :]
    for (start, size), out in zip(bounds, outs):
        at = (slice(None),) * axis + (pl.ds(start, size),)
        total = ins[0][at].astype(F32)
        for ref in ins[1:]:
            total = total + ref[at].astype(F32)
        out[...] = total.astype(out.dtype)


def split_sum(arrays, axis, sizes, after=()):
    shape = arrays[0].shape
    starts = np.cumsum([0] + list(sizes))
    bounds = [(int(start), int(size)) for start, size in zip(starts, sizes)]
    whole = pl.BlockSpec(memory_space=pltpu.VMEM)
    outs = [jax.ShapeDtypeStruct(shape[:axis] + (size,) + shape[axis + 1 :], BF16) for size in sizes]
    count = math.prod(shape)
    return pl.pallas_call(
        partial(split_sum_kernel, len(arrays), axis, bounds),
        in_specs=[whole] * len(arrays) + [ANY] * len(after),
        out_specs=[whole] * len(sizes),
        out_shape=outs,
        compiler_params=params(16),
        cost_estimate=SMALL,
    )(*arrays, *after)


def add_all(refs, at):
    terms = [ref[at].astype(F32) for ref in refs]
    return (terms[0] + terms[1]) + (terms[2] + terms[3])


def relay_kernel(one_ref, three_ref, lower_ref, upper_ref, *refs):
    up, down = refs[len(refs) - 2 :]
    up[:64, :] = (one_ref[:64, :].astype(F32) + lower_ref[...].astype(F32)).astype(BF16)
    up[64:, :] = one_ref[64:, :]
    down[:64, :] = three_ref[:64, :]
    down[64:, :] = (three_ref[64:, :].astype(F32) + upper_ref[...].astype(F32)).astype(BF16)


def relay(arrays, after):
    return pl.pallas_call(
        relay_kernel,
        in_specs=[WHOLE] * 4 + [ANY] * len(after),
        out_specs=[WHOLE] * 2,
        out_shape=[jax.ShapeDtypeStruct((128, D), BF16)] * 2,
        compiler_params=params(8),
        cost_estimate=SMALL,
    )(*arrays, *after)


def y_sum_kernel(place_ref, *refs):
    for step, out in enumerate(refs[len(refs) - 4 :]):
        at = pl.ds(pl.multiple_of(lax.rem(position(place_ref)[0] + step, 4) * 32, 32), 32)
        out[...] = (refs[0][at, :].astype(F32) + refs[1][at, :].astype(F32) + refs[2][at, :].astype(F32)).astype(BF16)


def y_sum(place, arrays, after):
    return pl.pallas_call(
        y_sum_kernel,
        in_specs=[pl.BlockSpec(memory_space=pltpu.SMEM)] + [WHOLE] * 3 + [ANY] * len(after),
        out_specs=[WHOLE] * 4,
        out_shape=[jax.ShapeDtypeStruct((32, D), BF16)] * 4,
        compiler_params=params(8),
        cost_estimate=SMALL,
    )(place, *arrays, *after)


def back_sum_kernel(*refs):
    outs = refs[len(refs) - 3 :]
    column = 0
    for keep, received in ((refs[0], refs[1]), (refs[2], refs[3])):
        width = keep.shape[2]
        for place, out in enumerate(outs):
            at = (slice(None), slice(place * 128, place * 128 + 128), slice(None))
            total = keep[at].astype(F32) + received[at].astype(F32)
            out[:, :, column : column + width] = total.astype(BF16)
        column = column + width


def back_sum(arrays, after):
    return pl.pallas_call(
        back_sum_kernel,
        in_specs=[WHOLE] * 4 + [ANY] * len(after),
        out_specs=[WHOLE] * 3,
        out_shape=[jax.ShapeDtypeStruct((2, 128, HD), BF16)] * 3,
        compiler_params=params(8),
        cost_estimate=SMALL,
    )(*arrays, *after)


def second_sum_kernel(own_ref, received_ref, *refs):
    near, far = refs[len(refs) - 2 :]

    def rows(start, stop):
        return (own_ref[:, start:stop, :].astype(F32) + received_ref[:, start:stop, :].astype(F32)).astype(BF16)

    near[:, :64, :] = rows(0, 64)
    near[:, 64:, :] = rows(96, 128)
    far[...] = rows(64, 96)


def second_sum(own, received, after):
    return pl.pallas_call(
        second_sum_kernel,
        in_specs=[WHOLE] * 2 + [ANY] * len(after),
        out_specs=[WHOLE] * 2,
        out_shape=[jax.ShapeDtypeStruct((2, 96, HD), BF16), jax.ShapeDtypeStruct((2, 32, HD), BF16)],
        compiler_params=params(8),
        cost_estimate=SMALL,
    )(own, received, *after)


def third_sum_kernel(far_ref, near_ref, *refs):
    refs[-1][...] = (far_ref[...].astype(F32) + near_ref[:, 64:, :].astype(F32)).astype(BF16)


def third_sum(far, near, after):
    return pl.pallas_call(
        third_sum_kernel,
        in_specs=[WHOLE] * 2 + [ANY] * len(after),
        out_specs=WHOLE,
        out_shape=jax.ShapeDtypeStruct((2, 32, HD), BF16),
        compiler_params=params(8),
        cost_estimate=SMALL,
    )(far, near, *after)


def finish_kernel(*refs):
    dk_ref, dv_ref, one, two, three = refs[:5]
    outs, mark_ref = refs[-3:-1], refs[-1]
    mark_ref[...] = jnp.zeros_like(mark_ref)
    token, row = iota((256, 128), 0), iota((256, 128), 1)
    spread = jnp.zeros((256, 128), F32)
    start = 0
    for factor, count in ((4, 64), (8, 32), (16, 16)):
        local = row - start
        inside = (local >= 0) & (local < count) & (token >= local * factor) & (token < local * factor + factor)
        spread = jnp.where(inside, 1.0 / factor, spread)
        start = start + count
    spread = spread.astype(BF16)
    for place, (own, out) in enumerate(zip((dk_ref, dv_ref), outs)):
        rows = jnp.concatenate([one[place], two[place], three[place], jnp.zeros((16, HD), BF16)], 0)
        out[...] = (own[...].astype(F32) + dot_nn(spread, rows)).astype(BF16)


def finish(dk, dv, one, two, three, after):
    half = pl.BlockSpec((256, HD), lambda i: (i, 0))
    shape = jax.ShapeDtypeStruct((ROWS, HD), BF16)
    coarse = [pl.BlockSpec((2, rows, HD), lambda i: (0, i, 0)) for rows in (64, 32, 16)]
    return pl.pallas_call(
        finish_kernel,
        grid=(2,),
        in_specs=[half] * 2 + coarse + [ANY] * len(after),
        out_specs=[half, half, pl.BlockSpec((8, 128), lambda i: (0, 0))],
        out_shape=[shape, shape, MARK],
        compiler_params=params(16),
        cost_estimate=SMALL,
    )(dk, dv, one, two, three, *after)


def add_all(refs, at):
    terms = [ref[at].astype(F32) for ref in refs]
    return (terms[0] + terms[1]) + (terms[2] + terms[3])


def last_sum_kernel(place_ref, *refs):
    outs = refs[len(refs) - 4 :]
    _, z_lo, _, _, z_hi = position(place_ref)
    sums = add_all(refs[:4], slice(None))
    for lo in range(2):
        for hi in range(2):
            rows = sums[lo * 16 + hi * 8 : lo * 16 + hi * 8 + 8]
            for place, out in enumerate(outs):

                @pl.when((lax.rem(z_lo + place % 2, 2) == lo) & (lax.rem(z_hi + place // 2, 2) == hi))
                def _():
                    out[...] = rows


def last_sum(place, arrays, after):
    return pl.pallas_call(
        last_sum_kernel,
        in_specs=[pl.BlockSpec(memory_space=pltpu.SMEM)] + [WHOLE] * 4 + [ANY] * len(after),
        out_specs=[WHOLE] * 4,
        out_shape=[jax.ShapeDtypeStruct((8, D), F32)] * 4,
        compiler_params=params(4),
        cost_estimate=SMALL,
    )(place, *arrays, *after)


def total_kernel(*refs):
    refs[-1][...] = add_all(refs[:4], slice(None))


def total(arrays, after):
    return pl.pallas_call(
        total_kernel,
        in_specs=[WHOLE] * 4 + [ANY] * len(after),
        out_specs=WHOLE,
        out_shape=jax.ShapeDtypeStruct((8, D), F32),
        compiler_params=params(4),
        cost_estimate=SMALL,
    )(*arrays, *after)


def body(query, key, value, segment_ids, out_weight, cotangent):
    query, key, value = query[0], key[0], value[0]
    cotangent = cotangent[0]
    place = lax.axis_index(("ctx", "dp")).astype(jnp.int32).reshape(1)

    one, two, three, fq, fk, mark = pool(place, segment_ids, key, value)
    from_z = swap(one, "ctx", 2)
    two, three, mark = lax.optimization_barrier((two, three, pause([mark])))
    grad_attention, grad_across = grad_attention_of(cotangent, out_weight)
    from_x = stack([swap(two, "ctx", 4), swap(three, "ctx", 12), swap(three, "ctx", 8)], [grad_attention, mark])
    from_xz = swap(from_x, "ctx", 2)
    sooner = [from_z, from_x, swap(from_z, "ctx", 1), swap(from_x, "ctx", 1)]
    early, mixed, stats = early_forward(query, key, value, fq, fk, sooner, [])
    from_xz, stats = lax.optimization_barrier((from_xz, stats))
    later = [from_xz, swap(from_xz, "ctx", 1)]
    pieces = sooner + later

    late, attention, rows = late_forward(query, grad_across, fq, mixed, stats, later)
    kept, given, mark = grad_weight_part(place, attention, cotangent)
    one = coarse_backward(query, grad_attention, grad_across, rows, early, late, pieces, range(FIRST), [mark])
    parts = split_sum([kept, swap(given, "ctx", 1)], 0, (128, 128, 64, 64, 128), [one[3]])
    lower, upper = shift(parts[2], "dp", 2), shift(parts[3], "dp", -2)
    rest = coarse_backward(query, grad_attention, grad_across, rows, early, late, pieces, range(FIRST, HEADS), [parts[0]])
    own_one, own_two, own_xz = back_sum([one[0], swap(one[1], "ctx", 1), rest[0], swap(rest[1], "ctx", 1)], [])
    back_xz = swap(own_xz, "ctx", 2)
    back_z = swap(own_one, "ctx", 2)
    partials = [(0, FIRST, one[2]), (FIRST, HEADS, rest[2])]
    *earlier, mark = local_backward(
        query, key, value, grad_across, rows, early, partials, range(4), (), [own_one]
    )
    up, down = relay([parts[1], parts[4], lower, upper], [mark])
    output, mark = project(attention, out_weight, up)
    grad_query, dk, dv, mark = local_backward(
        query, key, value, grad_across, rows, early, partials, range(4, HEADS), earlier, [mark]
    )
    near, far = second_sum(own_two, back_xz, [mark])
    near = swap(near, "ctx", 4)
    parts = y_sum(place, [parts[0], shift(up, "dp", 2), shift(down, "dp", -2)], [far])
    far = third_sum(far, near, [parts[0]])
    parts = [parts[0]] + [shift(parts[step], "ctx", 4 * step) for step in (1, 2, 3)]
    parts = last_sum(place, parts, [far])
    grad_key, grad_value, mark = finish(dk, dv, back_z, near, swap(far, "ctx", 12), [parts[0]])
    count = lax.axis_size("dp")
    both = [(i, (i // count ^ 2) * count + (i % count ^ 1)) for i in range(lax.axis_size("ctx") * count)]
    grad_weight = total(
        [parts[0], swap(parts[1], "ctx", 2), swap(parts[2], "dp", 1), lax.ppermute(parts[3], ("ctx", "dp"), both)],
        [mark],
    )
    return output[None], grad_query[None], grad_key[None], grad_value[None], grad_weight


def solution(mesh):
    in_specs = (
        P("dp", "ctx", None),
        P("dp", "ctx", None),
        P("dp", "ctx", None),
        P("dp", "ctx"),
        P(),
        P("dp", "ctx", None),
    )
    out_specs = (
        P("dp", "ctx", None),
        P("dp", "ctx", None),
        P("dp", "ctx", None),
        P("dp", "ctx", None),
        P(("ctx", "dp"), None),
    )
    return jax.shard_map(body, mesh=mesh, in_specs=in_specs, out_specs=out_specs, check_vma=False)
```

```python
from functools import partial
import math

import jax
import jax.numpy as jnp
import numpy as np
from jax import lax
from jax.experimental import pallas as pl
from jax.experimental.pallas import tpu as pltpu
from jax.sharding import PartitionSpec as P

HEADS = 8
HEAD_DIM = 128
HD = 1024
D = 2048
ROWS = 512
GROUPS = 1
PER = HEADS // GROUPS
COLS = PER * HEAD_DIM
FACTORS = (4, 8, 16)
COARSE = tuple(ROWS // factor for factor in FACTORS)
SCALE = 1.0 / math.sqrt(HEAD_DIM)
BIG = float(2**30)
F32 = jnp.float32
BF16 = jnp.bfloat16
LARGE = pl.CostEstimate(flops=2 * 10**10, bytes_accessed=1024, transcendentals=0)
SMALL = pl.CostEstimate(flops=1024, bytes_accessed=1024, transcendentals=0)


def params(mebibytes):
    return pltpu.CompilerParams(vmem_limit_bytes=int(mebibytes * 2**20))


def swap(array, axis, bits):
    return lax.ppermute(array, axis, [(i, i ^ bits) for i in range(lax.axis_size(axis))])


def shift(array, axis, step):
    size = lax.axis_size(axis)
    return lax.ppermute(array, axis, [(i, (i + step) % size) for i in range(size)])


def position(place_ref):
    place = place_ref[0]
    return place >> 5, (place >> 4) & 1, (place >> 3) & 1, (place >> 1) & 3, place & 1


def dot_nt(a, b):
    return lax.dot_general(a, b, (((1,), (1,)), ((), ())), preferred_element_type=F32)


def dot_nn(a, b):
    return lax.dot_general(a, b, (((1,), (0,)), ((), ())), preferred_element_type=F32)


def dot_tn(a, b):
    return lax.dot_general(a, b, (((0,), (0,)), ((), ())), preferred_element_type=F32)


def iota(shape, dim):
    return lax.broadcasted_iota(jnp.int32, shape, dim)


def offset_parts(factor):
    rest = math.log(factor) / SCALE
    parts = []
    for _ in range(3):
        part = float(np.asarray(rest, dtype=jnp.bfloat16))
        parts.append(part)
        rest = rest - part
    return parts


def pool_matrix(factor, weight):
    count = ROWS // factor
    row, col = iota((count, ROWS), 0), iota((count, ROWS), 1)
    inside = (col >= row * factor) & (col < row * factor + weight)
    return jnp.where(inside, 1.0 / weight, 0.0).astype(BF16)


def pool_kernel(place_ref, seg_hbm, key_hbm, value_hbm, one, two, three, fq_ref, fk_ref, mark_ref, seg_ref, key_ref, value_ref, sems):
    copies = [
        pltpu.make_async_copy(source, target, sems.at[place])
        for place, (source, target) in enumerate(((seg_hbm, seg_ref), (key_hbm, key_ref), (value_hbm, value_ref)))
    ]
    for copy in copies:
        copy.start()
    mark_ref[...] = jnp.zeros_like(mark_ref)
    outs = (one, two, three)
    starts = np.cumsum((0,) + COARSE)
    pool = jnp.concatenate([pool_matrix(factor, factor) for factor in FACTORS], 0)
    pick = jnp.concatenate([pool_matrix(factor, 1) for factor in FACTORS], 0)
    copies[0].wait()
    seg = seg_ref[...]
    kind = iota((8, ROWS), 0)
    rows = jnp.where(kind < 2, jnp.where(seg == kind, 1.0, 0.0), jnp.where(kind == 2, 1.0, 0.0)).astype(BF16)
    i, j = iota((8, HEAD_DIM), 0), iota((8, HEAD_DIM), 1)
    to_key = jnp.where((i < 2) & (i == j), 1.0, 0.0).astype(BF16)
    wrong = ((i == 0) & (j == 1)) | ((i == 1) & (j == 0))
    ones = (i == 2) & (j >= 2) & (j < 5)
    to_query = jnp.where(wrong, -BIG, jnp.where(ones, 1.0, 0.0)).astype(BF16)
    own = dot_tn(rows, to_key).astype(BF16)
    fk_ref[...] = own
    fq_ref[...] = dot_tn(rows, to_query).astype(BF16)
    picked = dot_nn(pick, own)
    lane = iota((1, HEAD_DIM), 1)
    for place, (factor, out) in enumerate(zip(FACTORS, outs)):
        parts = offset_parts(factor)
        offset = jnp.where(lane == 2, parts[0], jnp.where(lane == 3, parts[1], jnp.where(lane == 4, parts[2], 0.0)))
        out[:, 2 * HD :] = (picked[starts[place] : starts[place + 1]] + offset).astype(BF16)
    for copy, ref, column in zip(copies[1:], (key_ref, value_ref), (0, HD)):
        copy.wait()
        for start in range(0, HD, 256):
            mean = dot_nn(pool, ref[:, start : start + 256])
            for place, out in enumerate(outs):
                out[:, column + start : column + start + 256] = mean[starts[place] : starts[place + 1]].astype(BF16)


WIDTH = 2 * HD + HEAD_DIM
POOL_LIMIT = 52
WHOLE = pl.BlockSpec(memory_space=pltpu.VMEM)
ANY = pl.BlockSpec(memory_space=pl.ANY)
HBM = pl.BlockSpec(memory_space=pltpu.HBM)
MARK = jax.ShapeDtypeStruct((8, 128), F32)


def pool(place, seg, key, value):
    feature = jax.ShapeDtypeStruct((ROWS, HEAD_DIM), BF16)
    token = pltpu.VMEM((ROWS, HD), BF16)
    return pl.pallas_call(
        pool_kernel,
        in_specs=[pl.BlockSpec(memory_space=pltpu.SMEM)] + [HBM] * 3,
        out_specs=[WHOLE] * 6,
        out_shape=[jax.ShapeDtypeStruct((count, WIDTH), BF16) for count in COARSE] + [feature, feature, MARK],
        scratch_shapes=[pltpu.VMEM((1, ROWS), jnp.int32), token, token, pltpu.SemaphoreType.DMA((3,))],
        compiler_params=params(POOL_LIMIT),
        cost_estimate=SMALL,
    )(place, seg, key, value)


def pause_kernel(*refs):
    refs[-1][...] = jnp.zeros_like(refs[-1])


def pause(after):
    return pl.pallas_call(
        pause_kernel,
        in_specs=[ANY] * len(after),
        out_specs=WHOLE,
        out_shape=MARK,
        compiler_params=params(1),
        cost_estimate=SMALL,
    )(*after)


COARSE_ROWS = 768
FIRST = 7
RATE = SCALE * math.log2(math.e)


def columns(h):
    if isinstance(h, int):
        return slice(h * HEAD_DIM, h * HEAD_DIM + HEAD_DIM)
    return pl.ds(pl.multiple_of(h * HEAD_DIM, HEAD_DIM), HEAD_DIM)


def pair(refs, place, at):
    return jnp.concatenate([refs[2 * place][:, at], refs[2 * place + 1][:, at]], 0)


def joined(total, add):
    return add if total is None else total + add


def each_head(step, heads, unroll):
    if unroll == len(heads):
        for h in heads:
            step(h)
    else:
        lax.fori_loop(heads[0], heads[-1] + 1, lambda h, carry: (step(h), carry)[1], 0, unroll=unroll)


EARLY = 1024
LATE = 256


def early_forward_kernel(*refs):
    q_ref, k_ref, v_ref, fq_ref, fk_ref = refs[:5]
    pieces = refs[5:9]
    p_ref, mixed_ref, stat_ref, scores = refs[-4:]

    def step(h):
        at, beside = columns(h), columns(HEADS + h)
        query = jnp.concatenate([q_ref[:, at], fq_ref[...]], 1)
        top = None
        for place in range(4):
            rows = pl.ds(place * 256, 256)
            if place < 2:
                key = jnp.concatenate([k_ref[rows, at], fk_ref[rows, :]], 1)
            else:
                key = jnp.concatenate([pair(pieces, place - 2, at), pair(pieces, place - 2, slice(2 * HD, WIDTH))], 1)
            here = dot_nt(key, query) * RATE
            scores[rows, :] = here
            peak = jnp.max(here, 0, keepdims=True)
            top = peak if top is None else jnp.maximum(top, peak)
        total, mixed = None, None
        for place in range(4):
            rows = pl.ds(place * 256, 256)
            here = jnp.exp2(scores[rows, :] - top)
            total = joined(total, jnp.sum(here, 0, keepdims=True))
            here = here.astype(BF16)
            p_ref[h, rows, :] = here
            value = v_ref[rows, at] if place < 2 else pair(pieces, place - 2, beside)
            mixed = joined(mixed, dot_tn(value, here))
        mixed_ref[at, :] = mixed
        stat_ref[h, 0:1, :] = top
        stat_ref[h, 1:2, :] = total

    each_head(step, range(HEADS), 2)


def early_forward(query, key, value, fq, fk, pieces, after):
    return pl.pallas_call(
        early_forward_kernel,
        in_specs=[WHOLE] * 9 + [ANY] * len(after),
        out_specs=[WHOLE] * 3,
        out_shape=[
            jax.ShapeDtypeStruct((HEADS, EARLY, ROWS), BF16),
            jax.ShapeDtypeStruct((HD, ROWS), F32),
            jax.ShapeDtypeStruct((HEADS, 8, ROWS), F32),
        ],
        scratch_shapes=[pltpu.VMEM((EARLY, ROWS), F32)],
        compiler_params=params(12),
        cost_estimate=SMALL,
    )(query, key, value, fq, fk, *pieces, *after)


def late_forward_kernel(*refs):
    q_ref, across_ref, fq_ref, mixed_ref, stat_ref = refs[:5]
    pieces = refs[5:7]
    p_ref, ot_ref, row_ref = refs[7:]

    feature = pair(pieces, 0, slice(2 * HD, WIDTH))
    scores = []
    for h in range(HEADS):
        query = jnp.concatenate([q_ref[:, columns(h)], fq_ref[...]], 1)
        scores.append(dot_nt(jnp.concatenate([pair(pieces, 0, columns(h)), feature], 1), query) * RATE)
    for h in range(HEADS):
        before, total = stat_ref[h, 0:1, :], stat_ref[h, 1:2, :]
        top = jnp.maximum(before, jnp.max(scores[h], 0, keepdims=True))
        factor = jnp.exp2(before - top)
        here = jnp.exp2(scores[h] - top)
        inverse = 1.0 / (total * factor + jnp.sum(here, 0, keepdims=True))
        row_ref[h, 1:2, :] = factor * inverse
        p_ref[h] = (here * inverse).astype(BF16)
    for h in range(HEADS):
        at = columns(h)
        mixed = dot_tn(pair(pieces, 0, columns(HEADS + h)), p_ref[h]) + mixed_ref[at, :] * row_ref[h, 1:2, :]
        ot_ref[at, :] = mixed.astype(BF16)
        row_ref[h, 0:1, :] = jnp.sum(across_ref[at, :].astype(F32) * mixed, 0, keepdims=True)


def late_forward(query, across, fq, mixed, stats, pieces):
    return pl.pallas_call(
        late_forward_kernel,
        in_specs=[WHOLE] * 7,
        out_specs=[WHOLE] * 3,
        out_shape=[
            jax.ShapeDtypeStruct((HEADS, LATE, ROWS), BF16),
            jax.ShapeDtypeStruct((HD, ROWS), BF16),
            jax.ShapeDtypeStruct((HEADS, 8, ROWS), F32),
        ],
        compiler_params=params(12),
        cost_estimate=SMALL,
    )(query, across, fq, mixed, stats, *pieces)


def scaled(across, factor):
    across = (across.astype(F32) * factor).astype(BF16)
    return across, across.T


def coarse_backward_kernel(heads, *refs):
    q_ref, g_ref, across_ref, row_ref, early_ref, late_ref = refs[:6]
    pieces = refs[6:12]
    keep_ref, give_ref, dq_ref, mark_ref = refs[-4:]
    mark_ref[...] = jnp.zeros_like(mark_ref)

    def step(h):
        at, to = columns(h), columns(h - heads[0])
        q, g = q_ref[:, at], g_ref[:, at]
        delta, factor = row_ref[h, 0:1, :], row_ref[h, 1:2, :]
        across, scaled_g = scaled(across_ref[at, :], factor)
        scaled_delta = delta * factor
        grad_q = None
        for place in range(3):
            key, value = pair(pieces, place, at), pair(pieces, place, columns(HEADS + h))
            if place < 2:
                weight = early_ref[h, pl.ds(512 + place * 256, 256), :]
                slope = dot_nn(value, across) - scaled_delta
                grad_v = dot_nn(weight, scaled_g)
            else:
                weight = late_ref[h]
                slope = dot_nn(value, across_ref[at, :]) - delta
                grad_v = dot_nn(weight, g)
            slope = (weight.astype(F32) * slope).astype(BF16)
            grads = ((dot_nn(slope, q) * SCALE).astype(BF16), grad_v.astype(BF16))
            for side, grad in enumerate(grads):
                for half in range(2):
                    out, row = ((keep_ref, give_ref)[half], place * 128) if place == 2 else ((keep_ref, give_ref)[place], half * 128)
                    out[side, pl.ds(row, 128), to] = grad[half * 128 : half * 128 + 128]
            grad_q = joined(grad_q, dot_tn(key, slope))
        dq_ref[to, :] = grad_q

    each_head(step, heads, len(heads))


def coarse_backward(query, grad, across, rows, early, late, pieces, heads, after):
    width = len(heads) * HEAD_DIM
    return pl.pallas_call(
        partial(coarse_backward_kernel, heads),
        in_specs=[WHOLE] * 12 + [ANY] * len(after),
        out_specs=[WHOLE] * 4,
        out_shape=[
            jax.ShapeDtypeStruct((2, 384, width), BF16),
            jax.ShapeDtypeStruct((2, 384, width), BF16),
            jax.ShapeDtypeStruct((width, ROWS), F32),
            MARK,
        ],
        compiler_params=params(12),
        cost_estimate=SMALL,
    )(query, grad, across, rows, early, late, *pieces, *after)


def local_backward_kernel(heads, parts, before, *refs):
    q_ref, k_ref, v_ref, across_ref, row_ref, p_ref = refs[:6]
    part_refs = refs[6 : 6 + len(parts)]
    dq_ref, dk_ref, dv_ref, mark_ref = refs[-4:]
    mark_ref[...] = jnp.zeros_like(mark_ref)
    for ref, out in zip(refs[6 + len(parts) : 6 + len(parts) + before], (dq_ref, dk_ref, dv_ref)):
        out[:, : heads[0] * HEAD_DIM] = ref[...]

    def step(part, first, h):
        at = columns(h)
        q = q_ref[:, at]
        delta, factor = row_ref[h, 0:1, :], row_ref[h, 1:2, :]
        across, g = scaled(across_ref[at, :], factor)
        delta = delta * factor
        grad_q = part[columns(h - first), :]
        for start in (0, 256):
            rows = pl.ds(start, 256)
            weight = p_ref[h, rows, :]
            slope = (weight.astype(F32) * (dot_nn(v_ref[rows, at], across) - delta)).astype(BF16)
            dk_ref[rows, at] = (dot_nn(slope, q) * SCALE).astype(BF16)
            dv_ref[rows, at] = dot_nn(weight, g).astype(BF16)
            grad_q = grad_q + dot_tn(k_ref[rows, at], slope)
        dq_ref[:, at] = (grad_q * SCALE).astype(BF16).T

    for part, (first, last) in zip(part_refs, parts):
        inside = [h for h in heads if first <= h < last]
        each_head(partial(step, part, first), inside, len(inside))


def local_backward(query, key, value, across, rows, weights, partials, heads, earlier, after):
    partials = [part for part in partials if part[0] <= heads[-1] and heads[0] < part[1]]
    token = jax.ShapeDtypeStruct((ROWS, (heads[-1] + 1) * HEAD_DIM), BF16)
    return pl.pallas_call(
        partial(local_backward_kernel, heads, [part[:2] for part in partials], len(earlier)),
        in_specs=[WHOLE] * (6 + len(partials) + len(earlier)) + [ANY] * len(after),
        out_specs=[WHOLE] * 4,
        out_shape=[token, token, token, MARK],
        compiler_params=params(12),
        cost_estimate=SMALL,
    )(query, key, value, across, rows, weights, *[part[2] for part in partials], *earlier, *after)


def grad_attention_kernel(c_ref, w_ref, out_ref, across_ref):
    for start in range(0, HD, 256):
        out = dot_nt(c_ref[...], w_ref[start : start + 256, :]).astype(BF16)
        out_ref[:, start : start + 256] = out
        across_ref[start : start + 256, :] = out.T


def grad_attention_of(cotangent, weight):
    return pl.pallas_call(
        grad_attention_kernel,
        in_specs=[WHOLE] * 2,
        out_specs=[WHOLE] * 2,
        out_shape=[jax.ShapeDtypeStruct((ROWS, HD), BF16), jax.ShapeDtypeStruct((HD, ROWS), BF16)],
        compiler_params=params(8),
        cost_estimate=SMALL,
    )(cotangent, weight)


def project_kernel(a_ref, w_ref, _, out_ref, mark_ref):
    mark_ref[...] = jnp.zeros_like(mark_ref)
    for start in range(0, D, 512):
        out_ref[:, start : start + 512] = dot_tn(a_ref[...], w_ref[:, start : start + 512]).astype(BF16)


def project(attention, weight, after):
    return pl.pallas_call(
        project_kernel,
        in_specs=[WHOLE] * 2 + [ANY],
        out_specs=[WHOLE] * 2,
        out_shape=[jax.ShapeDtypeStruct((ROWS, D), BF16), MARK],
        compiler_params=params(8),
        cost_estimate=LARGE,
    )(attention, weight, after)


def stack_kernel(count, *refs):
    out, start = refs[-1], 0
    for ref in refs[:count]:
        out[pl.ds(start, ref.shape[0]), :] = ref[...]
        start = start + ref.shape[0]


def stack(arrays, after):
    rows, width = sum(array.shape[0] for array in arrays), arrays[0].shape[1]
    return pl.pallas_call(
        partial(stack_kernel, len(arrays)),
        in_specs=[WHOLE] * len(arrays) + [ANY] * len(after),
        out_specs=WHOLE,
        out_shape=jax.ShapeDtypeStruct((rows, width), BF16),
        compiler_params=params(4),
        cost_estimate=SMALL,
    )(*arrays, *after)


def grad_weight_kernel(place_ref, ot_ref, c_ref, keep_ref, give_ref, mark_ref, lhs):
    mark_ref[...] = jnp.zeros_like(mark_ref)
    _, _, core, y, _ = position(place_ref)
    for slot in range(2):
        half = core if slot == 0 else 1 - core
        for step in range(4):
            target = lax.rem(y + step, 4)
            for j in range(HEADS):
                source = pl.multiple_of(j * 128 + half * 64 + target * 16, 16)
                row = ((slot * 4 + step) * HEADS + j) * 16
                lhs[row : row + 16, :] = ot_ref[pl.ds(source, 16), :]
    for out, row in ((give_ref, HD // 2), (keep_ref, 0)):
        for start in range(0, D, 512):
            at = slice(start, start + 512)
            out[:, at] = dot_nn(lhs[row : row + HD // 2, :], c_ref[:, at]).astype(BF16)


def grad_weight_part(place, ot, cotangent):
    shape = jax.ShapeDtypeStruct((HD // 2, D), BF16)
    return pl.pallas_call(
        grad_weight_kernel,
        in_specs=[pl.BlockSpec(memory_space=pltpu.SMEM)] + [WHOLE] * 2,
        out_specs=[WHOLE] * 3,
        out_shape=[shape, shape, MARK],
        scratch_shapes=[pltpu.VMEM((HD, ROWS), BF16)],
        compiler_params=params(8),
        cost_estimate=SMALL,
    )(place, ot, cotangent)


def split_sum_kernel(count, axis, bounds, *refs):
    ins, outs = refs[:count], refs[len(refs) - len(bounds) :]
    for (start, size), out in zip(bounds, outs):
        at = (slice(None),) * axis + (pl.ds(start, size),)
        total = ins[0][at].astype(F32)
        for ref in ins[1:]:
            total = total + ref[at].astype(F32)
        out[...] = total.astype(out.dtype)


def split_sum(arrays, axis, sizes, after=()):
    shape = arrays[0].shape
    starts = np.cumsum([0] + list(sizes))
    bounds = [(int(start), int(size)) for start, size in zip(starts, sizes)]
    whole = pl.BlockSpec(memory_space=pltpu.VMEM)
    outs = [jax.ShapeDtypeStruct(shape[:axis] + (size,) + shape[axis + 1 :], BF16) for size in sizes]
    count = math.prod(shape)
    return pl.pallas_call(
        partial(split_sum_kernel, len(arrays), axis, bounds),
        in_specs=[whole] * len(arrays) + [ANY] * len(after),
        out_specs=[whole] * len(sizes),
        out_shape=outs,
        compiler_params=params(16),
        cost_estimate=SMALL,
    )(*arrays, *after)


def relay_kernel(one_ref, three_ref, lower_ref, upper_ref, *refs):
    up, down = refs[len(refs) - 2 :]
    up[:64, :] = (one_ref[:64, :].astype(F32) + lower_ref[...].astype(F32)).astype(BF16)
    up[64:, :] = one_ref[64:, :]
    down[:64, :] = three_ref[:64, :]
    down[64:, :] = (three_ref[64:, :].astype(F32) + upper_ref[...].astype(F32)).astype(BF16)


def relay(arrays, after):
    return pl.pallas_call(
        relay_kernel,
        in_specs=[WHOLE] * 4 + [ANY] * len(after),
        out_specs=[WHOLE] * 2,
        out_shape=[jax.ShapeDtypeStruct((128, D), BF16)] * 2,
        compiler_params=params(8),
        cost_estimate=SMALL,
    )(*arrays, *after)


def back_sum_kernel(*refs):
    outs = refs[len(refs) - 3 :]
    column = 0
    for keep, received in ((refs[0], refs[1]), (refs[2], refs[3])):
        width = keep.shape[2]
        for place, out in enumerate(outs):
            at = (slice(None), slice(place * 128, place * 128 + 128), slice(None))
            total = keep[at].astype(F32) + received[at].astype(F32)
            out[:, :, column : column + width] = total.astype(BF16)
        column = column + width


def back_sum(arrays, after):
    return pl.pallas_call(
        back_sum_kernel,
        in_specs=[WHOLE] * 4 + [ANY] * len(after),
        out_specs=[WHOLE] * 3,
        out_shape=[jax.ShapeDtypeStruct((2, 128, HD), BF16)] * 3,
        compiler_params=params(8),
        cost_estimate=SMALL,
    )(*arrays, *after)


def finish_kernel(*refs):
    dk_ref, dv_ref, one, two, three, four = refs[:6]
    outs, mark_ref = refs[-3:-1], refs[-1]
    mark_ref[...] = jnp.zeros_like(mark_ref)
    token, row = iota((256, 128), 0), iota((256, 128), 1)
    spread = jnp.zeros((256, 128), F32)
    start = 0
    for factor, count in ((4, 64), (8, 32), (16, 16), (16, 16)):
        local = row - start
        inside = (local >= 0) & (local < count) & (token >= local * factor) & (token < local * factor + factor)
        spread = jnp.where(inside, 1.0 / factor, spread)
        start = start + count
    spread = spread.astype(BF16)
    for place, (own, out) in enumerate(zip((dk_ref, dv_ref), outs)):
        rows = jnp.concatenate([ref[place] for ref in (one, two, three, four)], 0)
        out[...] = (own[...].astype(F32) + dot_nn(spread, rows)).astype(BF16)


def finish(dk, dv, returned):
    half = pl.BlockSpec((256, HD), lambda i: (i, 0))
    shape = jax.ShapeDtypeStruct((ROWS, HD), BF16)
    return pl.pallas_call(
        finish_kernel,
        grid=(2,),
        in_specs=[half] * 2 + [pl.BlockSpec((2, r.shape[1] // 2, HD), lambda i: (0, i, 0)) for r in returned],
        out_specs=[half, half, pl.BlockSpec((8, 128), lambda i: (0, 0))],
        out_shape=[shape, shape, MARK],
        compiler_params=params(16),
        cost_estimate=LARGE,
    )(dk, dv, *returned)


def total_kernel(ref, _, out_ref):
    sums = ref[0].astype(F32)
    for place in range(1, 16):
        sums = sums + ref[place].astype(F32)
    out_ref[...] = sums


def total(parts, after):
    return pl.pallas_call(
        total_kernel,
        in_specs=[WHOLE, ANY],
        out_specs=WHOLE,
        out_shape=jax.ShapeDtypeStruct((8, D), F32),
        compiler_params=params(4),
        cost_estimate=SMALL,
    )(parts, after)


def xz_groups():
    return [
        [(((x * 2 + z_lo) * 2 + core) * 4 + y) * 2 + z_hi for x in range(4) for z_lo in range(2) for z_hi in range(2)]
        for core in range(2)
        for y in range(4)
    ]


def body(query, key, value, segment_ids, out_weight, cotangent):
    query, key, value = query[0], key[0], value[0]
    cotangent = cotangent[0]
    place = lax.axis_index(("ctx", "dp")).astype(jnp.int32).reshape(1)

    one, two, three, fq, fk, mark = pool(place, segment_ids, key, value)
    from_z = swap(one, "ctx", 2)
    two, three, mark = lax.optimization_barrier((two, three, pause([mark])))
    grad_attention, grad_across = grad_attention_of(cotangent, out_weight)
    from_x = stack([swap(two, "ctx", 4), swap(three, "ctx", 12), swap(three, "ctx", 8)], [grad_attention, mark])
    from_xz = swap(from_x, "ctx", 2)
    sooner = [from_z, from_x, swap(from_z, "ctx", 1), swap(from_x, "ctx", 1)]
    early, mixed, stats = early_forward(query, key, value, fq, fk, sooner, [])
    from_xz, stats = lax.optimization_barrier((from_xz, stats))
    later = [from_xz, swap(from_xz, "ctx", 1)]
    pieces = sooner + later

    late, attention, rows = late_forward(query, grad_across, fq, mixed, stats, later)
    kept, given, mark = grad_weight_part(place, attention, cotangent)
    one = coarse_backward(query, grad_attention, grad_across, rows, early, late, pieces, range(FIRST), [mark])
    parts = split_sum([kept, swap(given, "ctx", 1)], 0, (128, 128, 64, 64, 128), [one[3]])
    lower, upper = shift(parts[2], "dp", 2), shift(parts[3], "dp", -2)
    rest = coarse_backward(query, grad_attention, grad_across, rows, early, late, pieces, range(FIRST, HEADS), [parts[0]])
    own_one, own_two, own_xz = back_sum([one[0], swap(one[1], "ctx", 1), rest[0], swap(rest[1], "ctx", 1)], [])
    back_xz = swap(own_xz, "ctx", 2)
    back_z = swap(own_one, "ctx", 2)
    partials = [(0, FIRST, one[2]), (FIRST, HEADS, rest[2])]
    *earlier, mark = local_backward(
        query, key, value, grad_across, rows, early, partials, range(4), (), [own_one]
    )
    up, down = relay([parts[1], parts[4], lower, upper], [mark])
    output, mark = project(attention, out_weight, up)
    grad_query, dk, dv, mark = local_backward(
        query, key, value, grad_across, rows, early, partials, range(4, HEADS), earlier, [mark]
    )
    two, three, four = split_sum([own_two, back_xz], 1, (64, 32, 32), [mark])
    returned = [back_z, swap(two, "ctx", 4), swap(three, "ctx", 12), swap(four, "ctx", 8)]
    (summed,) = split_sum([parts[0], shift(up, "dp", 2), shift(down, "dp", -2)], 0, (128,), [two])
    spread = lax.all_to_all(summed.reshape(16, 8, D), ("ctx", "dp"), 0, 0, axis_index_groups=xz_groups())
    grad_key, grad_value, mark = finish(dk, dv, returned)
    grad_weight = total(spread, mark)
    return output[None], grad_query[None], grad_key[None], grad_value[None], grad_weight


def solution(mesh):
    in_specs = (
        P("dp", "ctx", None),
        P("dp", "ctx", None),
        P("dp", "ctx", None),
        P("dp", "ctx"),
        P(),
        P("dp", "ctx", None),
    )
    out_specs = (
        P("dp", "ctx", None),
        P("dp", "ctx", None),
        P("dp", "ctx", None),
        P("dp", "ctx", None),
        P(("ctx", "dp"), None),
    )
    return jax.shard_map(body, mesh=mesh, in_specs=in_specs, out_specs=out_specs, check_vma=False)
```

```python
from functools import partial
import math

import jax
import jax.numpy as jnp
import numpy as np
from jax import lax
from jax.experimental import pallas as pl
from jax.experimental.pallas import tpu as pltpu
from jax.sharding import PartitionSpec as P

HEADS = 8
HEAD_DIM = 128
HD = 1024
D = 2048
ROWS = 512
GROUPS = 1
PER = HEADS // GROUPS
COLS = PER * HEAD_DIM
FACTORS = (4, 8, 16)
COARSE = tuple(ROWS // factor for factor in FACTORS)
SCALE = 1.0 / math.sqrt(HEAD_DIM)
BIG = float(2**30)
F32 = jnp.float32
BF16 = jnp.bfloat16
LARGE = pl.CostEstimate(flops=2 * 10**10, bytes_accessed=1024, transcendentals=0)
SMALL = pl.CostEstimate(flops=1024, bytes_accessed=1024, transcendentals=0)


def params(mebibytes):
    return pltpu.CompilerParams(vmem_limit_bytes=int(mebibytes * 2**20))


def swap(array, axis, bits):
    return lax.ppermute(array, axis, [(i, i ^ bits) for i in range(lax.axis_size(axis))])


def shift(array, axis, step):
    size = lax.axis_size(axis)
    return lax.ppermute(array, axis, [(i, (i + step) % size) for i in range(size)])


def position(place_ref):
    place = place_ref[0]
    return place >> 5, (place >> 4) & 1, (place >> 3) & 1, (place >> 1) & 3, place & 1


def dot_nt(a, b):
    return lax.dot_general(a, b, (((1,), (1,)), ((), ())), preferred_element_type=F32)


def dot_nn(a, b):
    return lax.dot_general(a, b, (((1,), (0,)), ((), ())), preferred_element_type=F32)


def dot_tn(a, b):
    return lax.dot_general(a, b, (((0,), (0,)), ((), ())), preferred_element_type=F32)


def iota(shape, dim):
    return lax.broadcasted_iota(jnp.int32, shape, dim)


def offset_parts(factor):
    rest = math.log(factor) / SCALE
    parts = []
    for _ in range(3):
        part = float(np.asarray(rest, dtype=jnp.bfloat16))
        parts.append(part)
        rest = rest - part
    return parts


def pool_matrix(factor, weight):
    count = ROWS // factor
    row, col = iota((count, ROWS), 0), iota((count, ROWS), 1)
    inside = (col >= row * factor) & (col < row * factor + weight)
    return jnp.where(inside, 1.0 / weight, 0.0).astype(BF16)


def pool_kernel(place_ref, seg_hbm, key_hbm, value_hbm, one, two, three, fq_ref, fk_ref, mark_ref, seg_ref, key_ref, value_ref, sems):
    copies = [
        pltpu.make_async_copy(source, target, sems.at[place])
        for place, (source, target) in enumerate(((seg_hbm, seg_ref), (key_hbm, key_ref), (value_hbm, value_ref)))
    ]
    for copy in copies:
        copy.start()
    mark_ref[...] = jnp.zeros_like(mark_ref)
    outs = (one, two, three)
    starts = np.cumsum((0,) + COARSE)
    pool = jnp.concatenate([pool_matrix(factor, factor) for factor in FACTORS], 0)
    pick = jnp.concatenate([pool_matrix(factor, 1) for factor in FACTORS], 0)
    copies[0].wait()
    seg = seg_ref[...]
    kind = iota((8, ROWS), 0)
    rows = jnp.where(kind < 2, jnp.where(seg == kind, 1.0, 0.0), jnp.where(kind == 2, 1.0, 0.0)).astype(BF16)
    i, j = iota((8, HEAD_DIM), 0), iota((8, HEAD_DIM), 1)
    to_key = jnp.where((i < 2) & (i == j), 1.0, 0.0).astype(BF16)
    wrong = ((i == 0) & (j == 1)) | ((i == 1) & (j == 0))
    ones = (i == 2) & (j >= 2) & (j < 5)
    to_query = jnp.where(wrong, -BIG, jnp.where(ones, 1.0, 0.0)).astype(BF16)
    own = dot_tn(rows, to_key).astype(BF16)
    fk_ref[...] = own
    fq_ref[...] = dot_tn(rows, to_query).astype(BF16)
    picked = dot_nn(pick, own)
    lane = iota((1, HEAD_DIM), 1)
    for place, (factor, out) in enumerate(zip(FACTORS, outs)):
        parts = offset_parts(factor)
        offset = jnp.where(lane == 2, parts[0], jnp.where(lane == 3, parts[1], jnp.where(lane == 4, parts[2], 0.0)))
        out[:, 2 * HD :] = (picked[starts[place] : starts[place + 1]] + offset).astype(BF16)
    for copy, ref, column in zip(copies[1:], (key_ref, value_ref), (0, HD)):
        copy.wait()
        for start in range(0, HD, 256):
            mean = dot_nn(pool, ref[:, start : start + 256])
            for place, out in enumerate(outs):
                out[:, column + start : column + start + 256] = mean[starts[place] : starts[place + 1]].astype(BF16)


WIDTH = 2 * HD + HEAD_DIM
POOL_LIMIT = 52
WHOLE = pl.BlockSpec(memory_space=pltpu.VMEM)
ANY = pl.BlockSpec(memory_space=pl.ANY)
HBM = pl.BlockSpec(memory_space=pltpu.HBM)
MARK = jax.ShapeDtypeStruct((8, 128), F32)


def pool(place, seg, key, value):
    feature = jax.ShapeDtypeStruct((ROWS, HEAD_DIM), BF16)
    token = pltpu.VMEM((ROWS, HD), BF16)
    return pl.pallas_call(
        pool_kernel,
        in_specs=[pl.BlockSpec(memory_space=pltpu.SMEM)] + [HBM] * 3,
        out_specs=[WHOLE] * 6,
        out_shape=[jax.ShapeDtypeStruct((count, WIDTH), BF16) for count in COARSE] + [feature, feature, MARK],
        scratch_shapes=[pltpu.VMEM((1, ROWS), jnp.int32), token, token, pltpu.SemaphoreType.DMA((3,))],
        compiler_params=params(POOL_LIMIT),
        cost_estimate=SMALL,
    )(place, seg, key, value)


def pause_kernel(*refs):
    refs[-1][...] = jnp.zeros_like(refs[-1])


def pause(after):
    return pl.pallas_call(
        pause_kernel,
        in_specs=[ANY] * len(after),
        out_specs=WHOLE,
        out_shape=MARK,
        compiler_params=params(1),
        cost_estimate=SMALL,
    )(*after)


COARSE_ROWS = 768
RATE = SCALE * math.log2(math.e)


def columns(h):
    if isinstance(h, int):
        return slice(h * HEAD_DIM, h * HEAD_DIM + HEAD_DIM)
    return pl.ds(pl.multiple_of(h * HEAD_DIM, HEAD_DIM), HEAD_DIM)


def pair(refs, place, at):
    return jnp.concatenate([refs[2 * place][:, at], refs[2 * place + 1][:, at]], 0)


def joined(total, add):
    return add if total is None else total + add


def each_head(step, heads, unroll):
    if unroll == len(heads):
        for h in heads:
            step(h)
    else:
        lax.fori_loop(heads[0], heads[-1] + 1, lambda h, carry: (step(h), carry)[1], 0, unroll=unroll)


EARLY = 1024
LATE = 256


def early_forward_kernel(*refs):
    q_ref, k_ref, v_ref, fq_ref, fk_ref = refs[:5]
    pieces = refs[5:9]
    p_ref, mixed_ref, stat_ref, scores = refs[-4:]

    def step(h):
        at, beside = columns(h), columns(HEADS + h)
        query = jnp.concatenate([q_ref[:, at], fq_ref[...]], 1)
        top = None
        for place in range(4):
            rows = pl.ds(place * 256, 256)
            if place < 2:
                key = jnp.concatenate([k_ref[rows, at], fk_ref[rows, :]], 1)
            else:
                key = jnp.concatenate([pair(pieces, place - 2, at), pair(pieces, place - 2, slice(2 * HD, WIDTH))], 1)
            here = dot_nt(key, query) * RATE
            scores[rows, :] = here
            peak = jnp.max(here, 0, keepdims=True)
            top = peak if top is None else jnp.maximum(top, peak)
        total, mixed = None, None
        for place in range(4):
            rows = pl.ds(place * 256, 256)
            here = jnp.exp2(scores[rows, :] - top)
            total = joined(total, jnp.sum(here, 0, keepdims=True))
            here = here.astype(BF16)
            p_ref[h, rows, :] = here
            value = v_ref[rows, at] if place < 2 else pair(pieces, place - 2, beside)
            mixed = joined(mixed, dot_tn(value, here))
        mixed_ref[at, :] = mixed
        stat_ref[h, 0:1, :] = top
        stat_ref[h, 1:2, :] = total

    each_head(step, range(HEADS), 2)


def early_forward(query, key, value, fq, fk, pieces, after):
    return pl.pallas_call(
        early_forward_kernel,
        in_specs=[WHOLE] * 9 + [ANY] * len(after),
        out_specs=[WHOLE] * 3,
        out_shape=[
            jax.ShapeDtypeStruct((HEADS, EARLY, ROWS), BF16),
            jax.ShapeDtypeStruct((HD, ROWS), F32),
            jax.ShapeDtypeStruct((HEADS, 8, ROWS), F32),
        ],
        scratch_shapes=[pltpu.VMEM((EARLY, ROWS), F32)],
        compiler_params=params(12),
        cost_estimate=SMALL,
    )(query, key, value, fq, fk, *pieces, *after)


def late_forward_kernel(*refs):
    q_ref, across_ref, fq_ref, mixed_ref, stat_ref = refs[:5]
    pieces = refs[5:7]
    p_ref, ot_ref, row_ref = refs[7:]

    feature = pair(pieces, 0, slice(2 * HD, WIDTH))
    scores = []
    for h in range(HEADS):
        query = jnp.concatenate([q_ref[:, columns(h)], fq_ref[...]], 1)
        scores.append(dot_nt(jnp.concatenate([pair(pieces, 0, columns(h)), feature], 1), query) * RATE)
    for h in range(HEADS):
        before, total = stat_ref[h, 0:1, :], stat_ref[h, 1:2, :]
        top = jnp.maximum(before, jnp.max(scores[h], 0, keepdims=True))
        factor = jnp.exp2(before - top)
        here = jnp.exp2(scores[h] - top)
        inverse = 1.0 / (total * factor + jnp.sum(here, 0, keepdims=True))
        row_ref[h, 1:2, :] = factor * inverse
        p_ref[h] = (here * inverse).astype(BF16)
    for h in range(HEADS):
        at = columns(h)
        mixed = dot_tn(pair(pieces, 0, columns(HEADS + h)), p_ref[h]) + mixed_ref[at, :] * row_ref[h, 1:2, :]
        ot_ref[at, :] = mixed.astype(BF16)
        row_ref[h, 0:1, :] = jnp.sum(across_ref[at, :].astype(F32) * mixed, 0, keepdims=True)


def late_forward(query, across, fq, mixed, stats, pieces):
    return pl.pallas_call(
        late_forward_kernel,
        in_specs=[WHOLE] * 7,
        out_specs=[WHOLE] * 3,
        out_shape=[
            jax.ShapeDtypeStruct((HEADS, LATE, ROWS), BF16),
            jax.ShapeDtypeStruct((HD, ROWS), BF16),
            jax.ShapeDtypeStruct((HEADS, 8, ROWS), F32),
        ],
        compiler_params=params(12),
        cost_estimate=SMALL,
    )(query, across, fq, mixed, stats, *pieces)


def scaled(across, factor):
    across = (across.astype(F32) * factor).astype(BF16)
    return across, across.T


def coarse_backward_kernel(heads, *refs):
    q_ref, g_ref, across_ref, row_ref, early_ref, late_ref = refs[:6]
    pieces = refs[6:12]
    keep_ref, give_ref, dq_ref, mark_ref = refs[-4:]
    mark_ref[...] = jnp.zeros_like(mark_ref)

    def step(h):
        at, to = columns(h), columns(h - heads[0])
        q, g = q_ref[:, at], g_ref[:, at]
        delta, factor = row_ref[h, 0:1, :], row_ref[h, 1:2, :]
        across, scaled_g = scaled(across_ref[at, :], factor)
        scaled_delta = delta * factor
        grad_q = None
        for place in range(3):
            key, value = pair(pieces, place, at), pair(pieces, place, columns(HEADS + h))
            if place < 2:
                weight = early_ref[h, pl.ds(512 + place * 256, 256), :]
                slope = dot_nn(value, across) - scaled_delta
                grad_v = dot_nn(weight, scaled_g)
            else:
                weight = late_ref[h]
                slope = dot_nn(value, across_ref[at, :]) - delta
                grad_v = dot_nn(weight, g)
            slope = (weight.astype(F32) * slope).astype(BF16)
            grads = ((dot_nn(slope, q) * SCALE).astype(BF16), grad_v.astype(BF16))
            for side, grad in enumerate(grads):
                for half in range(2):
                    out, row = ((keep_ref, give_ref)[half], place * 128) if place == 2 else ((keep_ref, give_ref)[place], half * 128)
                    out[side, pl.ds(row, 128), to] = grad[half * 128 : half * 128 + 128]
            grad_q = joined(grad_q, dot_tn(key, slope))
        dq_ref[to, :] = grad_q

    each_head(step, heads, len(heads))


def coarse_backward(query, grad, across, rows, early, late, pieces, heads, after):
    width = len(heads) * HEAD_DIM
    return pl.pallas_call(
        partial(coarse_backward_kernel, heads),
        in_specs=[WHOLE] * 12 + [ANY] * len(after),
        out_specs=[WHOLE] * 4,
        out_shape=[
            jax.ShapeDtypeStruct((2, 384, width), BF16),
            jax.ShapeDtypeStruct((2, 384, width), BF16),
            jax.ShapeDtypeStruct((width, ROWS), F32),
            MARK,
        ],
        compiler_params=params(12),
        cost_estimate=SMALL,
    )(query, grad, across, rows, early, late, *pieces, *after)


def local_backward_kernel(heads, parts, before, *refs):
    q_ref, k_ref, v_ref, across_ref, row_ref, p_ref = refs[:6]
    part_refs = refs[6 : 6 + len(parts)]
    dq_ref, dk_ref, dv_ref, mark_ref = refs[-4:]
    mark_ref[...] = jnp.zeros_like(mark_ref)
    for ref, out in zip(refs[6 + len(parts) : 6 + len(parts) + before], (dq_ref, dk_ref, dv_ref)):
        out[:, : heads[0] * HEAD_DIM] = ref[...]

    def step(part, first, h):
        at = columns(h)
        q = q_ref[:, at]
        delta, factor = row_ref[h, 0:1, :], row_ref[h, 1:2, :]
        across, g = scaled(across_ref[at, :], factor)
        delta = delta * factor
        grad_q = part[columns(h - first), :]
        for start in (0, 256):
            rows = pl.ds(start, 256)
            weight = p_ref[h, rows, :]
            slope = (weight.astype(F32) * (dot_nn(v_ref[rows, at], across) - delta)).astype(BF16)
            dk_ref[rows, at] = (dot_nn(slope, q) * SCALE).astype(BF16)
            dv_ref[rows, at] = dot_nn(weight, g).astype(BF16)
            grad_q = grad_q + dot_tn(k_ref[rows, at], slope)
        dq_ref[:, at] = (grad_q * SCALE).astype(BF16).T

    for part, (first, last) in zip(part_refs, parts):
        inside = [h for h in heads if first <= h < last]
        each_head(partial(step, part, first), inside, len(inside))


def local_backward(query, key, value, across, rows, weights, partials, heads, earlier, after):
    partials = [part for part in partials if part[0] <= heads[-1] and heads[0] < part[1]]
    token = jax.ShapeDtypeStruct((ROWS, (heads[-1] + 1) * HEAD_DIM), BF16)
    return pl.pallas_call(
        partial(local_backward_kernel, heads, [part[:2] for part in partials], len(earlier)),
        in_specs=[WHOLE] * (6 + len(partials) + len(earlier)) + [ANY] * len(after),
        out_specs=[WHOLE] * 4,
        out_shape=[token, token, token, MARK],
        compiler_params=params(12),
        cost_estimate=SMALL,
    )(query, key, value, across, rows, weights, *[part[2] for part in partials], *earlier, *after)


def grad_attention_kernel(c_ref, w_ref, out_ref, across_ref):
    for start in range(0, HD, 256):
        out = dot_nt(c_ref[...], w_ref[start : start + 256, :]).astype(BF16)
        out_ref[:, start : start + 256] = out
        across_ref[start : start + 256, :] = out.T


def grad_attention_of(cotangent, weight):
    return pl.pallas_call(
        grad_attention_kernel,
        in_specs=[WHOLE] * 2,
        out_specs=[WHOLE] * 2,
        out_shape=[jax.ShapeDtypeStruct((ROWS, HD), BF16), jax.ShapeDtypeStruct((HD, ROWS), BF16)],
        compiler_params=params(8),
        cost_estimate=SMALL,
    )(cotangent, weight)


def project_kernel(a_ref, w_ref, _, out_ref, mark_ref):
    mark_ref[...] = jnp.zeros_like(mark_ref)
    for start in range(0, D, 512):
        out_ref[:, start : start + 512] = dot_tn(a_ref[...], w_ref[:, start : start + 512]).astype(BF16)


def project(attention, weight, after):
    return pl.pallas_call(
        project_kernel,
        in_specs=[WHOLE] * 2 + [ANY],
        out_specs=[WHOLE] * 2,
        out_shape=[jax.ShapeDtypeStruct((ROWS, D), BF16), MARK],
        compiler_params=params(8),
        cost_estimate=LARGE,
    )(attention, weight, after)


def stack_kernel(count, *refs):
    out, start = refs[-1], 0
    for ref in refs[:count]:
        out[pl.ds(start, ref.shape[0]), :] = ref[...]
        start = start + ref.shape[0]


def stack(arrays, after):
    rows, width = sum(array.shape[0] for array in arrays), arrays[0].shape[1]
    return pl.pallas_call(
        partial(stack_kernel, len(arrays)),
        in_specs=[WHOLE] * len(arrays) + [ANY] * len(after),
        out_specs=WHOLE,
        out_shape=jax.ShapeDtypeStruct((rows, width), BF16),
        compiler_params=params(4),
        cost_estimate=SMALL,
    )(*arrays, *after)


def grad_weight_kernel(place_ref, ot_ref, c_ref, keep_ref, give_ref, mark_ref, lhs):
    mark_ref[...] = jnp.zeros_like(mark_ref)
    _, _, core, y, _ = position(place_ref)
    for slot in range(2):
        half = core if slot == 0 else 1 - core
        for step in range(4):
            target = lax.rem(y + step, 4)
            for j in range(HEADS):
                source = pl.multiple_of(j * 128 + half * 64 + target * 16, 16)
                row = ((slot * 4 + step) * HEADS + j) * 16
                lhs[row : row + 16, :] = ot_ref[pl.ds(source, 16), :]
    for out, row in ((give_ref, HD // 2), (keep_ref, 0)):
        for start in range(0, D, 512):
            at = slice(start, start + 512)
            out[:, at] = dot_nn(lhs[row : row + HD // 2, :], c_ref[:, at]).astype(BF16)


def grad_weight_part(place, ot, cotangent):
    shape = jax.ShapeDtypeStruct((HD // 2, D), BF16)
    return pl.pallas_call(
        grad_weight_kernel,
        in_specs=[pl.BlockSpec(memory_space=pltpu.SMEM)] + [WHOLE] * 2,
        out_specs=[WHOLE] * 3,
        out_shape=[shape, shape, MARK],
        scratch_shapes=[pltpu.VMEM((HD, ROWS), BF16)],
        compiler_params=params(8),
        cost_estimate=SMALL,
    )(place, ot, cotangent)


def split_sum_kernel(count, axis, bounds, *refs):
    ins, outs = refs[:count], refs[len(refs) - len(bounds) :]
    for (start, size), out in zip(bounds, outs):
        at = (slice(None),) * axis + (pl.ds(start, size),)
        total = ins[0][at].astype(F32)
        for ref in ins[1:]:
            total = total + ref[at].astype(F32)
        out[...] = total.astype(out.dtype)


def split_sum(arrays, axis, sizes, after=()):
    shape = arrays[0].shape
    starts = np.cumsum([0] + list(sizes))
    bounds = [(int(start), int(size)) for start, size in zip(starts, sizes)]
    whole = pl.BlockSpec(memory_space=pltpu.VMEM)
    outs = [jax.ShapeDtypeStruct(shape[:axis] + (size,) + shape[axis + 1 :], BF16) for size in sizes]
    count = math.prod(shape)
    return pl.pallas_call(
        partial(split_sum_kernel, len(arrays), axis, bounds),
        in_specs=[whole] * len(arrays) + [ANY] * len(after),
        out_specs=[whole] * len(sizes),
        out_shape=outs,
        compiler_params=params(16),
        cost_estimate=SMALL,
    )(*arrays, *after)


def relay_kernel(one_ref, three_ref, lower_ref, upper_ref, *refs):
    up, down = refs[len(refs) - 2 :]
    up[:64, :] = (one_ref[:64, :].astype(F32) + lower_ref[...].astype(F32)).astype(BF16)
    up[64:, :] = one_ref[64:, :]
    down[:64, :] = three_ref[:64, :]
    down[64:, :] = (three_ref[64:, :].astype(F32) + upper_ref[...].astype(F32)).astype(BF16)


def relay(arrays, after):
    return pl.pallas_call(
        relay_kernel,
        in_specs=[WHOLE] * 4 + [ANY] * len(after),
        out_specs=[WHOLE] * 2,
        out_shape=[jax.ShapeDtypeStruct((128, D), BF16)] * 2,
        compiler_params=params(8),
        cost_estimate=SMALL,
    )(*arrays, *after)


def finish_kernel(*refs):
    dk_ref, dv_ref, one, two, three, four = refs[:6]
    outs, mark_ref = refs[-3:-1], refs[-1]
    mark_ref[...] = jnp.zeros_like(mark_ref)
    token, row = iota((256, 128), 0), iota((256, 128), 1)
    spread = jnp.zeros((256, 128), F32)
    start = 0
    for factor, count in ((4, 64), (8, 32), (16, 16), (16, 16)):
        local = row - start
        inside = (local >= 0) & (local < count) & (token >= local * factor) & (token < local * factor + factor)
        spread = jnp.where(inside, 1.0 / factor, spread)
        start = start + count
    spread = spread.astype(BF16)
    for place, (own, out) in enumerate(zip((dk_ref, dv_ref), outs)):
        rows = jnp.concatenate([ref[place] for ref in (one, two, three, four)], 0)
        out[...] = (own[...].astype(F32) + dot_nn(spread, rows)).astype(BF16)


def finish(dk, dv, returned):
    half = pl.BlockSpec((256, HD), lambda i: (i, 0))
    shape = jax.ShapeDtypeStruct((ROWS, HD), BF16)
    return pl.pallas_call(
        finish_kernel,
        grid=(2,),
        in_specs=[half] * 2 + [pl.BlockSpec((2, r.shape[1] // 2, HD), lambda i: (0, i, 0)) for r in returned],
        out_specs=[half, half, pl.BlockSpec((8, 128), lambda i: (0, 0))],
        out_shape=[shape, shape, MARK],
        compiler_params=params(16),
        cost_estimate=LARGE,
    )(dk, dv, *returned)


def total_kernel(ref, _, out_ref):
    sums = ref[0].astype(F32)
    for place in range(1, 16):
        sums = sums + ref[place].astype(F32)
    out_ref[...] = sums


def total(parts, after):
    return pl.pallas_call(
        total_kernel,
        in_specs=[WHOLE, ANY],
        out_specs=WHOLE,
        out_shape=jax.ShapeDtypeStruct((8, D), F32),
        compiler_params=params(4),
        cost_estimate=SMALL,
    )(parts, after)


def xz_groups():
    return [
        [(((x * 2 + z_lo) * 2 + core) * 4 + y) * 2 + z_hi for x in range(4) for z_lo in range(2) for z_hi in range(2)]
        for core in range(2)
        for y in range(4)
    ]


def body(query, key, value, segment_ids, out_weight, cotangent):
    query, key, value = query[0], key[0], value[0]
    cotangent = cotangent[0]
    place = lax.axis_index(("ctx", "dp")).astype(jnp.int32).reshape(1)

    one, two, three, fq, fk, mark = pool(place, segment_ids, key, value)
    from_z = swap(one, "ctx", 2)
    two, three, mark = lax.optimization_barrier((two, three, pause([mark])))
    grad_attention, grad_across = grad_attention_of(cotangent, out_weight)
    from_x = stack([swap(two, "ctx", 4), swap(three, "ctx", 12), swap(three, "ctx", 8)], [grad_attention, mark])
    from_xz = swap(from_x, "ctx", 2)
    sooner = [from_z, from_x, swap(from_z, "ctx", 1), swap(from_x, "ctx", 1)]
    early, mixed, stats = early_forward(query, key, value, fq, fk, sooner, [])
    from_xz, stats = lax.optimization_barrier((from_xz, stats))
    later = [from_xz, swap(from_xz, "ctx", 1)]
    pieces = sooner + later

    late, attention, rows = late_forward(query, grad_across, fq, mixed, stats, later)
    kept, given, mark = grad_weight_part(place, attention, cotangent)
    keep, give, partial_q, mark = coarse_backward(
        query, grad_attention, grad_across, rows, early, late, pieces, range(HEADS), [mark]
    )
    parts = split_sum([kept, swap(given, "ctx", 1)], 0, (128, 128, 64, 64, 128), [mark])
    lower, upper = shift(parts[2], "dp", 2), shift(parts[3], "dp", -2)
    own_one, own_two, own_xz = split_sum([keep, swap(give, "ctx", 1)], 1, (128, 128, 128), [parts[0]])
    back_xz = swap(own_xz, "ctx", 2)
    partials = [(0, HEADS, partial_q)]
    *earlier, mark = local_backward(
        query, key, value, grad_across, rows, early, partials, range(7), (), [own_one]
    )
    up, down = relay([parts[1], parts[4], lower, upper], [mark])
    output, mark = project(attention, out_weight, up)
    own_one, mark = lax.optimization_barrier((own_one, mark))
    back_z = swap(own_one, "ctx", 2)
    grad_query, dk, dv, mark = local_backward(
        query, key, value, grad_across, rows, early, partials, range(7, HEADS), earlier, [mark]
    )
    two, three, four = split_sum([own_two, back_xz], 1, (64, 32, 32), [mark])
    returned = [back_z, swap(two, "ctx", 4), swap(three, "ctx", 12), swap(four, "ctx", 8)]
    (summed,) = split_sum([parts[0], shift(up, "dp", 2), shift(down, "dp", -2)], 0, (128,), [two])
    spread = lax.all_to_all(summed.reshape(16, 8, D), ("ctx", "dp"), 0, 0, axis_index_groups=xz_groups())
    grad_key, grad_value, mark = finish(dk, dv, returned)
    grad_weight = total(spread, mark)
    return output[None], grad_query[None], grad_key[None], grad_value[None], grad_weight


def solution(mesh):
    in_specs = (
        P("dp", "ctx", None),
        P("dp", "ctx", None),
        P("dp", "ctx", None),
        P("dp", "ctx"),
        P(),
        P("dp", "ctx", None),
    )
    out_specs = (
        P("dp", "ctx", None),
        P("dp", "ctx", None),
        P("dp", "ctx", None),
        P("dp", "ctx", None),
        P(("ctx", "dp"), None),
    )
    return jax.shard_map(body, mesh=mesh, in_specs=in_specs, out_specs=out_specs, check_vma=False)
```

```python
from functools import partial
import math

import jax
import jax.numpy as jnp
import numpy as np
from jax import lax
from jax.experimental import pallas as pl
from jax.experimental.pallas import tpu as pltpu
from jax.sharding import PartitionSpec as P

HEADS = 8
HEAD_DIM = 128
HD = 1024
D = 2048
ROWS = 512
GROUPS = 1
PER = HEADS // GROUPS
COLS = PER * HEAD_DIM
FACTORS = (4, 8, 16)
COARSE = tuple(ROWS // factor for factor in FACTORS)
SCALE = 1.0 / math.sqrt(HEAD_DIM)
BIG = float(2**30)
F32 = jnp.float32
BF16 = jnp.bfloat16
LARGE = pl.CostEstimate(flops=2 * 10**10, bytes_accessed=1024, transcendentals=0)
SMALL = pl.CostEstimate(flops=1024, bytes_accessed=1024, transcendentals=0)


def params(mebibytes):
    return pltpu.CompilerParams(vmem_limit_bytes=int(mebibytes * 2**20))


def swap(array, axis, bits):
    return lax.ppermute(array, axis, [(i, i ^ bits) for i in range(lax.axis_size(axis))])


def shift(array, axis, step):
    size = lax.axis_size(axis)
    return lax.ppermute(array, axis, [(i, (i + step) % size) for i in range(size)])


def position(place_ref):
    place = place_ref[0]
    return place >> 5, (place >> 4) & 1, (place >> 3) & 1, (place >> 1) & 3, place & 1


def dot_nt(a, b):
    return lax.dot_general(a, b, (((1,), (1,)), ((), ())), preferred_element_type=F32)


def dot_nn(a, b):
    return lax.dot_general(a, b, (((1,), (0,)), ((), ())), preferred_element_type=F32)


def dot_tn(a, b):
    return lax.dot_general(a, b, (((0,), (0,)), ((), ())), preferred_element_type=F32)


def iota(shape, dim):
    return lax.broadcasted_iota(jnp.int32, shape, dim)


def offset_parts(factor):
    rest = math.log(factor) / SCALE
    parts = []
    for _ in range(3):
        part = float(np.asarray(rest, dtype=jnp.bfloat16))
        parts.append(part)
        rest = rest - part
    return parts


def pool_matrix(factor, weight):
    count = ROWS // factor
    row, col = iota((count, ROWS), 0), iota((count, ROWS), 1)
    inside = (col >= row * factor) & (col < row * factor + weight)
    return jnp.where(inside, 1.0 / weight, 0.0).astype(BF16)


def pool_kernel(place_ref, seg_hbm, key_hbm, value_hbm, one, two, three, fq_ref, fk_ref, mark_ref, seg_ref, key_ref, value_ref, sems):
    copies = [pltpu.make_async_copy(seg_hbm, seg_ref, sems.at[0])]
    for source, target in ((key_hbm, key_ref), (value_hbm, value_ref)):
        for start in range(0, HD, 256):
            at = pl.ds(start, 256)
            copies.append(pltpu.make_async_copy(source.at[:, at], target.at[:, at], sems.at[len(copies)]))
    for copy in copies:
        copy.start()
    mark_ref[...] = jnp.zeros_like(mark_ref)
    outs = (one, two, three)
    starts = np.cumsum((0,) + COARSE)
    pool = jnp.concatenate([pool_matrix(factor, factor) for factor in FACTORS], 0)
    pick = jnp.concatenate([pool_matrix(factor, 1) for factor in FACTORS], 0)
    copies[0].wait()
    seg = seg_ref[...]
    kind = iota((8, ROWS), 0)
    rows = jnp.where(kind < 2, jnp.where(seg == kind, 1.0, 0.0), jnp.where(kind == 2, 1.0, 0.0)).astype(BF16)
    i, j = iota((8, HEAD_DIM), 0), iota((8, HEAD_DIM), 1)
    to_key = jnp.where((i < 2) & (i == j), 1.0, 0.0).astype(BF16)
    wrong = ((i == 0) & (j == 1)) | ((i == 1) & (j == 0))
    ones = (i == 2) & (j >= 2) & (j < 5)
    to_query = jnp.where(wrong, -BIG, jnp.where(ones, 1.0, 0.0)).astype(BF16)
    own = dot_tn(rows, to_key).astype(BF16)
    fk_ref[...] = own
    fq_ref[...] = dot_tn(rows, to_query).astype(BF16)
    picked = dot_nn(pick, own)
    lane = iota((1, HEAD_DIM), 1)
    for place, (factor, out) in enumerate(zip(FACTORS, outs)):
        parts = offset_parts(factor)
        offset = jnp.where(lane == 2, parts[0], jnp.where(lane == 3, parts[1], jnp.where(lane == 4, parts[2], 0.0)))
        out[:, 2 * HD :] = (picked[starts[place] : starts[place + 1]] + offset).astype(BF16)
    for place, copy in enumerate(copies[1:]):
        ref, start, column = (key_ref, value_ref)[place // 4], place % 4 * 256, place * 256
        copy.wait()
        mean = dot_nn(pool, ref[:, start : start + 256])
        for level, out in enumerate(outs):
            out[:, column : column + 256] = mean[starts[level] : starts[level + 1]].astype(BF16)


WIDTH = 2 * HD + HEAD_DIM
POOL_LIMIT = 52
WHOLE = pl.BlockSpec(memory_space=pltpu.VMEM)
ANY = pl.BlockSpec(memory_space=pl.ANY)
HBM = pl.BlockSpec(memory_space=pltpu.HBM)
MARK = jax.ShapeDtypeStruct((8, 128), F32)


def pool(place, seg, key, value):
    feature = jax.ShapeDtypeStruct((ROWS, HEAD_DIM), BF16)
    token = pltpu.VMEM((ROWS, HD), BF16)
    return pl.pallas_call(
        pool_kernel,
        in_specs=[pl.BlockSpec(memory_space=pltpu.SMEM)] + [HBM] * 3,
        out_specs=[WHOLE] * 6,
        out_shape=[jax.ShapeDtypeStruct((count, WIDTH), BF16) for count in COARSE] + [feature, feature, MARK],
        scratch_shapes=[pltpu.VMEM((1, ROWS), jnp.int32), token, token, pltpu.SemaphoreType.DMA((9,))],
        compiler_params=params(POOL_LIMIT),
        cost_estimate=SMALL,
    )(place, seg, key, value)


def pause_kernel(*refs):
    refs[-1][...] = jnp.zeros_like(refs[-1])


def pause(after):
    return pl.pallas_call(
        pause_kernel,
        in_specs=[ANY] * len(after),
        out_specs=WHOLE,
        out_shape=MARK,
        compiler_params=params(1),
        cost_estimate=SMALL,
    )(*after)


COARSE_ROWS = 768
RATE = SCALE * math.log2(math.e)


def columns(h):
    if isinstance(h, int):
        return slice(h * HEAD_DIM, h * HEAD_DIM + HEAD_DIM)
    return pl.ds(pl.multiple_of(h * HEAD_DIM, HEAD_DIM), HEAD_DIM)


def pair(refs, place, at):
    return jnp.concatenate([refs[2 * place][:, at], refs[2 * place + 1][:, at]], 0)


def joined(total, add):
    return add if total is None else total + add


def each_head(step, heads, unroll):
    if unroll == len(heads):
        for h in heads:
            step(h)
    else:
        lax.fori_loop(heads[0], heads[-1] + 1, lambda h, carry: (step(h), carry)[1], 0, unroll=unroll)


EARLY = 1024
LATE = 256


def early_forward_kernel(*refs):
    q_ref, k_ref, v_ref, fq_ref, fk_ref = refs[:5]
    pieces = refs[5:9]
    p_ref, mixed_ref, stat_ref, scores = refs[-4:]

    def step(h):
        at, beside = columns(h), columns(HEADS + h)
        query = jnp.concatenate([q_ref[:, at], fq_ref[...]], 1)
        top = None
        for place in range(4):
            rows = pl.ds(place * 256, 256)
            if place < 2:
                key = jnp.concatenate([k_ref[rows, at], fk_ref[rows, :]], 1)
            else:
                key = jnp.concatenate([pair(pieces, place - 2, at), pair(pieces, place - 2, slice(2 * HD, WIDTH))], 1)
            here = dot_nt(key, query) * RATE
            scores[rows, :] = here
            peak = jnp.max(here, 0, keepdims=True)
            top = peak if top is None else jnp.maximum(top, peak)
        total, mixed = None, None
        for place in range(4):
            rows = pl.ds(place * 256, 256)
            here = jnp.exp2(scores[rows, :] - top)
            total = joined(total, jnp.sum(here, 0, keepdims=True))
            here = here.astype(BF16)
            p_ref[h, rows, :] = here
            value = v_ref[rows, at] if place < 2 else pair(pieces, place - 2, beside)
            mixed = joined(mixed, dot_tn(value, here))
        mixed_ref[at, :] = mixed
        stat_ref[h, 0:1, :] = top
        stat_ref[h, 1:2, :] = total

    each_head(step, range(HEADS), 2)


def early_forward(query, key, value, fq, fk, pieces, after):
    return pl.pallas_call(
        early_forward_kernel,
        in_specs=[WHOLE] * 9 + [ANY] * len(after),
        out_specs=[WHOLE] * 3,
        out_shape=[
            jax.ShapeDtypeStruct((HEADS, EARLY, ROWS), BF16),
            jax.ShapeDtypeStruct((HD, ROWS), F32),
            jax.ShapeDtypeStruct((HEADS, 8, ROWS), F32),
        ],
        scratch_shapes=[pltpu.VMEM((EARLY, ROWS), F32)],
        compiler_params=params(12),
        cost_estimate=SMALL,
    )(query, key, value, fq, fk, *pieces, *after)


def late_forward_kernel(*refs):
    q_ref, across_ref, fq_ref, mixed_ref, stat_ref = refs[:5]
    pieces = refs[5:7]
    p_ref, ot_ref, row_ref = refs[7:]

    feature = pair(pieces, 0, slice(2 * HD, WIDTH))
    scores = []
    for h in range(HEADS):
        query = jnp.concatenate([q_ref[:, columns(h)], fq_ref[...]], 1)
        scores.append(dot_nt(jnp.concatenate([pair(pieces, 0, columns(h)), feature], 1), query) * RATE)
    for h in range(HEADS):
        before, total = stat_ref[h, 0:1, :], stat_ref[h, 1:2, :]
        top = jnp.maximum(before, jnp.max(scores[h], 0, keepdims=True))
        factor = jnp.exp2(before - top)
        here = jnp.exp2(scores[h] - top)
        inverse = 1.0 / (total * factor + jnp.sum(here, 0, keepdims=True))
        row_ref[h, 1:2, :] = factor * inverse
        p_ref[h] = (here * inverse).astype(BF16)
    for h in range(HEADS):
        at = columns(h)
        mixed = dot_tn(pair(pieces, 0, columns(HEADS + h)), p_ref[h]) + mixed_ref[at, :] * row_ref[h, 1:2, :]
        ot_ref[at, :] = mixed.astype(BF16)
        row_ref[h, 0:1, :] = jnp.sum(across_ref[at, :].astype(F32) * mixed, 0, keepdims=True)


def late_forward(query, across, fq, mixed, stats, pieces):
    return pl.pallas_call(
        late_forward_kernel,
        in_specs=[WHOLE] * 7,
        out_specs=[WHOLE] * 3,
        out_shape=[
            jax.ShapeDtypeStruct((HEADS, LATE, ROWS), BF16),
            jax.ShapeDtypeStruct((HD, ROWS), BF16),
            jax.ShapeDtypeStruct((HEADS, 8, ROWS), F32),
        ],
        compiler_params=params(12),
        cost_estimate=SMALL,
    )(query, across, fq, mixed, stats, *pieces)


def scaled(across, factor):
    across = (across.astype(F32) * factor).astype(BF16)
    return across, across.T


def coarse_backward_kernel(heads, *refs):
    q_ref, g_ref, across_ref, row_ref, early_ref, late_ref = refs[:6]
    pieces = refs[6:12]
    keep_ref, give_ref, dq_ref, mark_ref = refs[-4:]
    mark_ref[...] = jnp.zeros_like(mark_ref)

    def step(h):
        at, to = columns(h), columns(h - heads[0])
        q, g = q_ref[:, at], g_ref[:, at]
        delta, factor = row_ref[h, 0:1, :], row_ref[h, 1:2, :]
        across, scaled_g = scaled(across_ref[at, :], factor)
        scaled_delta = delta * factor
        grad_q = None
        for place in range(3):
            key, value = pair(pieces, place, at), pair(pieces, place, columns(HEADS + h))
            if place < 2:
                weight = early_ref[h, pl.ds(512 + place * 256, 256), :]
                slope = dot_nn(value, across) - scaled_delta
                grad_v = dot_nn(weight, scaled_g)
            else:
                weight = late_ref[h]
                slope = dot_nn(value, across_ref[at, :]) - delta
                grad_v = dot_nn(weight, g)
            slope = (weight.astype(F32) * slope).astype(BF16)
            grads = ((dot_nn(slope, q) * SCALE).astype(BF16), grad_v.astype(BF16))
            for side, grad in enumerate(grads):
                for half in range(2):
                    out, row = ((keep_ref, give_ref)[half], place * 128) if place == 2 else ((keep_ref, give_ref)[place], half * 128)
                    out[side, pl.ds(row, 128), to] = grad[half * 128 : half * 128 + 128]
            grad_q = joined(grad_q, dot_tn(key, slope))
        dq_ref[to, :] = grad_q

    each_head(step, heads, len(heads))


def coarse_backward(query, grad, across, rows, early, late, pieces, heads, after):
    width = len(heads) * HEAD_DIM
    return pl.pallas_call(
        partial(coarse_backward_kernel, heads),
        in_specs=[WHOLE] * 12 + [ANY] * len(after),
        out_specs=[WHOLE] * 4,
        out_shape=[
            jax.ShapeDtypeStruct((2, 384, width), BF16),
            jax.ShapeDtypeStruct((2, 384, width), BF16),
            jax.ShapeDtypeStruct((width, ROWS), F32),
            MARK,
        ],
        compiler_params=params(12),
        cost_estimate=SMALL,
    )(query, grad, across, rows, early, late, *pieces, *after)


def local_backward_kernel(heads, parts, before, *refs):
    q_ref, k_ref, v_ref, across_ref, row_ref, p_ref = refs[:6]
    part_refs = refs[6 : 6 + len(parts)]
    dq_ref, dk_ref, dv_ref, mark_ref = refs[-4:]
    mark_ref[...] = jnp.zeros_like(mark_ref)
    for ref, out in zip(refs[6 + len(parts) : 6 + len(parts) + before], (dq_ref, dk_ref, dv_ref)):
        out[:, : heads[0] * HEAD_DIM] = ref[...]

    def step(part, first, h):
        at = columns(h)
        q = q_ref[:, at]
        delta, factor = row_ref[h, 0:1, :], row_ref[h, 1:2, :]
        across, g = scaled(across_ref[at, :], factor)
        delta = delta * factor
        grad_q = part[columns(h - first), :]
        for start in (0, 256):
            rows = pl.ds(start, 256)
            weight = p_ref[h, rows, :]
            slope = (weight.astype(F32) * (dot_nn(v_ref[rows, at], across) - delta)).astype(BF16)
            dk_ref[rows, at] = (dot_nn(slope, q) * SCALE).astype(BF16)
            dv_ref[rows, at] = dot_nn(weight, g).astype(BF16)
            grad_q = grad_q + dot_tn(k_ref[rows, at], slope)
        dq_ref[:, at] = (grad_q * SCALE).astype(BF16).T

    for part, (first, last) in zip(part_refs, parts):
        inside = [h for h in heads if first <= h < last]
        each_head(partial(step, part, first), inside, len(inside))


def local_backward(query, key, value, across, rows, weights, partials, heads, earlier, after):
    partials = [part for part in partials if part[0] <= heads[-1] and heads[0] < part[1]]
    token = jax.ShapeDtypeStruct((ROWS, (heads[-1] + 1) * HEAD_DIM), BF16)
    return pl.pallas_call(
        partial(local_backward_kernel, heads, [part[:2] for part in partials], len(earlier)),
        in_specs=[WHOLE] * (6 + len(partials) + len(earlier)) + [ANY] * len(after),
        out_specs=[WHOLE] * 4,
        out_shape=[token, token, token, MARK],
        compiler_params=params(12),
        cost_estimate=SMALL,
    )(query, key, value, across, rows, weights, *[part[2] for part in partials], *earlier, *after)


def grad_attention_kernel(c_ref, w_ref, out_ref, across_ref):
    for start in range(0, HD, 256):
        out = dot_nt(c_ref[...], w_ref[start : start + 256, :]).astype(BF16)
        out_ref[:, start : start + 256] = out
        across_ref[start : start + 256, :] = out.T


def grad_attention_of(cotangent, weight):
    return pl.pallas_call(
        grad_attention_kernel,
        in_specs=[WHOLE] * 2,
        out_specs=[WHOLE] * 2,
        out_shape=[jax.ShapeDtypeStruct((ROWS, HD), BF16), jax.ShapeDtypeStruct((HD, ROWS), BF16)],
        compiler_params=params(8),
        cost_estimate=SMALL,
    )(cotangent, weight)


def project_kernel(a_ref, w_ref, _, out_ref, mark_ref):
    mark_ref[...] = jnp.zeros_like(mark_ref)
    for start in range(0, D, 512):
        out_ref[:, start : start + 512] = dot_tn(a_ref[...], w_ref[:, start : start + 512]).astype(BF16)


def project(attention, weight, after):
    return pl.pallas_call(
        project_kernel,
        in_specs=[WHOLE] * 2 + [ANY],
        out_specs=[WHOLE] * 2,
        out_shape=[jax.ShapeDtypeStruct((ROWS, D), BF16), MARK],
        compiler_params=params(8),
        cost_estimate=LARGE,
    )(attention, weight, after)


def stack_kernel(count, *refs):
    out, start = refs[-1], 0
    for ref in refs[:count]:
        out[pl.ds(start, ref.shape[0]), :] = ref[...]
        start = start + ref.shape[0]


def stack(arrays, after):
    rows, width = sum(array.shape[0] for array in arrays), arrays[0].shape[1]
    return pl.pallas_call(
        partial(stack_kernel, len(arrays)),
        in_specs=[WHOLE] * len(arrays) + [ANY] * len(after),
        out_specs=WHOLE,
        out_shape=jax.ShapeDtypeStruct((rows, width), BF16),
        compiler_params=params(4),
        cost_estimate=SMALL,
    )(*arrays, *after)


def grad_weight_kernel(place_ref, ot_ref, c_ref, keep_ref, give_ref, mark_ref, lhs):
    mark_ref[...] = jnp.zeros_like(mark_ref)
    _, _, core, y, _ = position(place_ref)
    for slot in range(2):
        half = core if slot == 0 else 1 - core
        for step in range(4):
            target = lax.rem(y + step, 4)
            for j in range(HEADS):
                source = pl.multiple_of(j * 128 + half * 64 + target * 16, 16)
                row = ((slot * 4 + step) * HEADS + j) * 16
                lhs[row : row + 16, :] = ot_ref[pl.ds(source, 16), :]
    for out, row in ((give_ref, HD // 2), (keep_ref, 0)):
        for start in range(0, D, 512):
            at = slice(start, start + 512)
            out[:, at] = dot_nn(lhs[row : row + HD // 2, :], c_ref[:, at]).astype(BF16)


def grad_weight_part(place, ot, cotangent):
    shape = jax.ShapeDtypeStruct((HD // 2, D), BF16)
    return pl.pallas_call(
        grad_weight_kernel,
        in_specs=[pl.BlockSpec(memory_space=pltpu.SMEM)] + [WHOLE] * 2,
        out_specs=[WHOLE] * 3,
        out_shape=[shape, shape, MARK],
        scratch_shapes=[pltpu.VMEM((HD, ROWS), BF16)],
        compiler_params=params(8),
        cost_estimate=SMALL,
    )(place, ot, cotangent)


def split_sum_kernel(count, axis, bounds, *refs):
    ins, outs = refs[:count], refs[len(refs) - len(bounds) :]
    for (start, size), out in zip(bounds, outs):
        at = (slice(None),) * axis + (pl.ds(start, size),)
        total = ins[0][at].astype(F32)
        for ref in ins[1:]:
            total = total + ref[at].astype(F32)
        out[...] = total.astype(out.dtype)


def split_sum(arrays, axis, sizes, after=()):
    shape = arrays[0].shape
    starts = np.cumsum([0] + list(sizes))
    bounds = [(int(start), int(size)) for start, size in zip(starts, sizes)]
    whole = pl.BlockSpec(memory_space=pltpu.VMEM)
    outs = [jax.ShapeDtypeStruct(shape[:axis] + (size,) + shape[axis + 1 :], BF16) for size in sizes]
    count = math.prod(shape)
    return pl.pallas_call(
        partial(split_sum_kernel, len(arrays), axis, bounds),
        in_specs=[whole] * len(arrays) + [ANY] * len(after),
        out_specs=[whole] * len(sizes),
        out_shape=outs,
        compiler_params=params(16),
        cost_estimate=SMALL,
    )(*arrays, *after)


def relay_kernel(one_ref, three_ref, lower_ref, upper_ref, *refs):
    up, down = refs[len(refs) - 2 :]
    up[:64, :] = (one_ref[:64, :].astype(F32) + lower_ref[...].astype(F32)).astype(BF16)
    up[64:, :] = one_ref[64:, :]
    down[:64, :] = three_ref[:64, :]
    down[64:, :] = (three_ref[64:, :].astype(F32) + upper_ref[...].astype(F32)).astype(BF16)


def relay(arrays, after):
    return pl.pallas_call(
        relay_kernel,
        in_specs=[WHOLE] * 4 + [ANY] * len(after),
        out_specs=[WHOLE] * 2,
        out_shape=[jax.ShapeDtypeStruct((128, D), BF16)] * 2,
        compiler_params=params(8),
        cost_estimate=SMALL,
    )(*arrays, *after)


def finish_kernel(*refs):
    dk_ref, dv_ref, one, two, three, four = refs[:6]
    outs, mark_ref = refs[-3:-1], refs[-1]
    mark_ref[...] = jnp.zeros_like(mark_ref)
    token, row = iota((256, 128), 0), iota((256, 128), 1)
    spread = jnp.zeros((256, 128), F32)
    start = 0
    for factor, count in ((4, 64), (8, 32), (16, 16), (16, 16)):
        local = row - start
        inside = (local >= 0) & (local < count) & (token >= local * factor) & (token < local * factor + factor)
        spread = jnp.where(inside, 1.0 / factor, spread)
        start = start + count
    spread = spread.astype(BF16)
    for place, (own, out) in enumerate(zip((dk_ref, dv_ref), outs)):
        rows = jnp.concatenate([ref[place] for ref in (one, two, three, four)], 0)
        out[...] = (own[...].astype(F32) + dot_nn(spread, rows)).astype(BF16)


def finish(dk, dv, returned):
    half = pl.BlockSpec((256, HD), lambda i: (i, 0))
    shape = jax.ShapeDtypeStruct((ROWS, HD), BF16)
    return pl.pallas_call(
        finish_kernel,
        grid=(2,),
        in_specs=[half] * 2 + [pl.BlockSpec((2, r.shape[1] // 2, HD), lambda i: (0, i, 0)) for r in returned],
        out_specs=[half, half, pl.BlockSpec((8, 128), lambda i: (0, 0))],
        out_shape=[shape, shape, MARK],
        compiler_params=params(16),
        cost_estimate=LARGE,
    )(dk, dv, *returned)


def total_kernel(ref, _, out_ref):
    sums = ref[0].astype(F32)
    for place in range(1, 16):
        sums = sums + ref[place].astype(F32)
    out_ref[...] = sums


def total(parts, after):
    return pl.pallas_call(
        total_kernel,
        in_specs=[WHOLE, ANY],
        out_specs=WHOLE,
        out_shape=jax.ShapeDtypeStruct((8, D), F32),
        compiler_params=params(4),
        cost_estimate=SMALL,
    )(parts, after)


def xz_groups():
    return [
        [(((x * 2 + z_lo) * 2 + core) * 4 + y) * 2 + z_hi for x in range(4) for z_lo in range(2) for z_hi in range(2)]
        for core in range(2)
        for y in range(4)
    ]


def body(query, key, value, segment_ids, out_weight, cotangent):
    query, key, value = query[0], key[0], value[0]
    cotangent = cotangent[0]
    place = lax.axis_index(("ctx", "dp")).astype(jnp.int32).reshape(1)

    one, two, three, fq, fk, mark = pool(place, segment_ids, key, value)
    from_z = swap(one, "ctx", 2)
    two, three, mark = lax.optimization_barrier((two, three, pause([mark])))
    grad_attention, grad_across = grad_attention_of(cotangent, out_weight)
    from_x = stack([swap(two, "ctx", 4), swap(three, "ctx", 12), swap(three, "ctx", 8)], [grad_attention, mark])
    from_xz = swap(from_x, "ctx", 2)
    sooner = [from_z, from_x, swap(from_z, "ctx", 1), swap(from_x, "ctx", 1)]
    early, mixed, stats = early_forward(query, key, value, fq, fk, sooner, [])
    from_xz, stats = lax.optimization_barrier((from_xz, stats))
    later = [from_xz, swap(from_xz, "ctx", 1)]
    pieces = sooner + later

    late, attention, rows = late_forward(query, grad_across, fq, mixed, stats, later)
    kept, given, mark = grad_weight_part(place, attention, cotangent)
    keep, give, partial_q, mark = coarse_backward(
        query, grad_attention, grad_across, rows, early, late, pieces, range(HEADS), [mark]
    )
    parts = split_sum([kept, swap(given, "ctx", 1)], 0, (128, 128, 64, 64, 128), [mark])
    lower, upper = shift(parts[2], "dp", 2), shift(parts[3], "dp", -2)
    own_one, own_two, own_xz = split_sum([keep, swap(give, "ctx", 1)], 1, (128, 128, 128), [parts[0]])
    back_xz = swap(own_xz, "ctx", 2)
    partials = [(0, HEADS, partial_q)]
    *earlier, mark = local_backward(
        query, key, value, grad_across, rows, early, partials, range(7), (), [own_one]
    )
    up, down = relay([parts[1], parts[4], lower, upper], [mark])
    output, mark = project(attention, out_weight, up)
    own_one, mark = lax.optimization_barrier((own_one, mark))
    back_z = swap(own_one, "ctx", 2)
    grad_query, dk, dv, mark = local_backward(
        query, key, value, grad_across, rows, early, partials, range(7, HEADS), earlier, [mark]
    )
    two, three, four = split_sum([own_two, back_xz], 1, (64, 32, 32), [mark])
    returned = [back_z, swap(two, "ctx", 4), swap(three, "ctx", 12), swap(four, "ctx", 8)]
    (summed,) = split_sum([parts[0], shift(up, "dp", 2), shift(down, "dp", -2)], 0, (128,), [two])
    spread = lax.all_to_all(summed.reshape(16, 8, D), ("ctx", "dp"), 0, 0, axis_index_groups=xz_groups())
    grad_key, grad_value, mark = finish(dk, dv, returned)
    grad_weight = total(spread, mark)
    return output[None], grad_query[None], grad_key[None], grad_value[None], grad_weight


def solution(mesh):
    in_specs = (
        P("dp", "ctx", None),
        P("dp", "ctx", None),
        P("dp", "ctx", None),
        P("dp", "ctx"),
        P(),
        P("dp", "ctx", None),
    )
    out_specs = (
        P("dp", "ctx", None),
        P("dp", "ctx", None),
        P("dp", "ctx", None),
        P("dp", "ctx", None),
        P(("ctx", "dp"), None),
    )
    return jax.shard_map(body, mesh=mesh, in_specs=in_specs, out_specs=out_specs, check_vma=False)
```
